32 devices in a mesh: groups: 2 (over y), seq: 4 (over z), mp: 4 (over x, core).
Axes of the slice: x: 2, y: 2, z: 4, core: 2. Of those that a mesh axis runs over, the one named last changes fastest.
Arguments:
- tiles: bfloat16 [1536, 1536], P(('groups', 'seq')), parts along dimension 0, may hold values from -6 to 6
- counts: int32 [8], P(('groups', 'seq')), parts along dimension 0, may hold values from 1 to 192, 576 in all
- dest: int32 [1536, 1], P(('groups', 'seq')), parts along dimension 0, may hold values from 0 to 3; in each aligned block of 192 rows (0 to 191, 192 to 383, ...) at most 64 rows name the same one
- gain_enc: float32 [1536], replicated, may hold values from 0.1 to 1.9
- w_gate: bfloat16 [1536, 4096], P('seq', 'mp'), may hold values from -0.15625 to 0.15625
- w_up: bfloat16 [1536, 4096], P('seq', 'mp'), may hold values from -0.15625 to 0.15625
- w_down: bfloat16 [4096, 1536], P('mp', 'seq'), may hold values from -0.09375 to 0.09375
- gain_slide: float32 [1536], replicated, may hold values from 0.1 to 1.9
- w_qkv: bfloat16 [1536, 2304], P(None, 'mp'), may hold values from -0.15625 to 0.15625
- offsets: int32 [12], P('mp'), may hold values from 0 to 7
Outputs:
- attended: bfloat16 [2048, 768], P(('groups', 'seq'), 'mp'), parts along dimension 0
The draws below stay inside these ranges and needn't reach their ends.
There are 2 independent parts, one for each index of `groups`. The reference program is written for one: setup_inputs(seed, part) draws one part's arguments, and reference() takes and returns one part's arrays. A program takes and returns all parts, laid end to end along the dimension named above; an argument that names none is the same for every part. Nothing has to cross between parts.
Inputs may be any that keep to these rules, and one draw needn't show every extreme that they name: `dest`: among the tiles of one owner, no value is named by more than 64 tiles, a bound that some block reaches of them. `counts`: some owner has all 192 slots live.
All inputs are finite; a program needn't handle non-finite values. No bound on the sum of `counts` on one device may be relied on, other than what follows from the above.
Results may differ from the reference program's by a relative error of at most 0.013.
The reference program's roundings to bfloat16 on the way (of `slots`, `normed`, `hidden`, `embedded` and `projected`) count: a program that leaves them out, or rounds other values in their place, can miss the bound.
Values may be sent and summed in bfloat16 or wider, within the bound.
No kernel may reach another device: no remote copies, remote signals or barrier semaphores. Data moves between devices by JAX's collectives and lax.ppermute only.
A program may use at most 64 MiB of HBM per device.

```python
import math
import jax
import jax.numpy as jnp
import numpy as np
from jax import lax

D_ENC = 1536
HID = 4096
SLIDE_HEADS = 12
HEAD_WIDTH = 64
D_SLIDE = 768
DILATION_STEP = 8
TILE_DEV = 192
ENCODER_SLOTS = 256
CAP = 64
TILES = 768
SEQUENCE_SLOTS = 1024
N_SEQ = 4


def place_ends(drawn, rng, low, top_value):
    dims = drawn.shape
    spot = [jax.random.randint(jax.random.fold_in(rng, axis), (), 0, dims[axis]) for axis in range(len(dims))]
    drawn = drawn.at[tuple(spot)].set(low)
    longest = dims.index(max(dims))
    spot[longest] = (spot[longest] + 1) % dims[longest]
    return drawn.at[tuple(spot)].set(top_value)


def block_scale(stream_key, dims, cuts, low, high):
    gain = 1.0
    for dim, blocks in cuts:
        draws = jax.random.uniform(jax.random.fold_in(jax.random.fold_in(stream_key, 6), dim), (blocks,), jnp.float32, low / len(cuts), high / len(cuts))
        gain = gain * jnp.repeat(jnp.exp(draws), dims[dim] // blocks).reshape((-1,) + (1,) * (len(dims) - 1 - dim))
    return gain


def length_profile(amount, total, reach, skew):
    portions = [(1 << 20) // math.isqrt(standing ** skew) + 1 for standing in range(2, amount + 1)]
    spare, given = total - reach - (amount - 1), [1] * (amount - 1)
    while spare > 0:
        movable = [i for i in range(amount - 1) if given[i] < reach]
        whole, budget = sum([portions[i] for i in movable]), spare
        for i in movable:
            extra = min(reach - given[i], max(1, budget * portions[i] // whole), spare)
            given[i] = given[i] + extra
            spare = spare - extra
    return np.array([reach] + given)


def ragged(stream_key, amount, total, limit, skew):
    if amount == 2:
        one = jax.random.randint(stream_key, (), max(1, total - limit), min(limit, total - 1) + 1)
        return jnp.stack([one, total - one])
    sizes = jnp.asarray(length_profile(amount, total, limit, skew), jnp.int32)
    couples = (amount - 1) // 2
    giver, taker = sizes[1:1 + 2 * couples:2], sizes[2:2 + 2 * couples:2]
    slack = jnp.minimum(giver - 1, limit - taker)
    shifted = jax.random.randint(jax.random.fold_in(stream_key, 1), (couples,), 0, 1 << 20) % (slack + 1)
    sizes = sizes.at[1:1 + 2 * couples:2].set(giver - shifted).at[2:2 + 2 * couples:2].set(taker + shifted)
    return sizes[jax.random.permutation(jax.random.fold_in(stream_key, 2), amount)]


def shared_out(own_key, own, number, rows, number_of, top, reach, slope):
    ranking = jax.random.permutation(own_key, number_of)
    heavy_load, usual = portions_of(number_of, rows * top, reach, slope, True), portions_of(number_of, rows * top, reach, slope, False)
    places = jnp.arange(number_of)

    def named(tallies, offset_by):
        used = int((tallies > 0).sum())
        fixed = max(1, used // 4)
        shifted = fixed + (places - fixed + offset_by * (used - fixed)) % max(1, number_of - fixed)
        return jnp.zeros((number_of,), jnp.int32).at[ranking[jnp.where(places < fixed, places, shifted)]].set(jnp.asarray(tallies, jnp.int32))

    tallies = jnp.where(number % 4 == 0, named(heavy_load, number // 4), named(usual, number - number // 4 - 1))
    mixed = jax.random.permutation(jax.random.fold_in(own, 3), number_of)
    source_of, sink = mixed[0:number_of // 2 * 2:2], mixed[1:number_of // 2 * 2:2]
    slack = jnp.minimum(tallies[source_of] - 1, reach - tallies[sink]) // 2
    slack = jnp.where((source_of == ranking[0]) | (sink == ranking[0]) | (tallies[sink] == 0), 0, jnp.maximum(slack, 0))
    shifted = jax.random.randint(jax.random.fold_in(own, 4), (number_of // 2,), 0, 1 << 20) % (slack + 1)
    tallies = tallies.at[source_of].add(-shifted).at[sink].add(shifted)
    labels = jnp.searchsorted(jnp.cumsum(tallies), jnp.arange(rows * top), side="right").astype(jnp.int32)
    table = labels.reshape(top, rows).T
    table = table[jax.random.permutation(jax.random.fold_in(own, 1), rows)]
    offset_by = jax.random.randint(jax.random.fold_in(own, 2), (rows, 1), 0, top)
    return jnp.take_along_axis(table, (jnp.arange(top)[None, :] + offset_by) % top, axis=1)


def portions_of(number_of, total, most, slope, full):
    weights = [(1 << 20) // math.isqrt(standing ** slope) + 1 for standing in range(1, number_of + 1)]
    largest = most if full else min(most, max(-(-total // number_of), total * weights[0] // sum(weights)))
    least = 1 if total - largest >= number_of - 1 else 0
    given, rest = [largest] + [least] * (number_of - 1), total - largest - least * (number_of - 1)
    while rest > 0:
        free = [i for i in range(1, number_of) if given[i] < largest] or [i for i in range(1, number_of) if given[i] < most]
        whole, left = sum([weights[i] for i in free]), rest
        for i in free:
            more = min(most - given[i], max(1, left * weights[i] // whole), rest)
            given[i] = given[i] + more
            rest = rest - more
    return np.array(given)


def gaussian(key, dims, scale, reach, shards=(), held_as=jnp.bfloat16):
    drawn = jax.random.normal(key, dims, jnp.float32) * scale
    if len(shards) > 0:
        drawn = block_scale(key, dims, shards, -0.22, 0.18) * drawn
    return jnp.clip(drawn, min=-reach, max=reach).astype(held_as)


def setup_inputs(seed: int = 0, part: int = 0) -> dict:
    splits = jax.random.split(jax.random.key(seed), 11)
    own_keys = jax.random.split(jax.random.fold_in(splits[10], part), 11)
    tiles = gaussian(own_keys[0], (TILES, D_ENC), 1.0, 6.0, ((0, 4),))
    counts = ragged(own_keys[1], N_SEQ, TILE_DEV * N_SEQ * 3 // 4, TILE_DEV, 2).astype(jnp.int32)
    dest_keys = jax.random.split(jax.random.fold_in(own_keys[2], 1), TILES // TILE_DEV)
    dest_turns = jax.random.permutation(jax.random.fold_in(own_keys[2], 3), TILES // TILE_DEV)
    dest = jax.vmap(lambda own, number: shared_out(jax.random.fold_in(own_keys[2], 2), own, number, TILE_DEV, N_SEQ, 1, CAP, 2))(dest_keys, dest_turns).reshape((TILES, 1))
    gain_enc = jnp.clip(1.0 + 0.18 * jax.random.normal(splits[3], (D_ENC,), jnp.float32), 0.1, 1.9)
    w_gate = gaussian(splits[4], (D_ENC, HID), D_ENC ** -0.5, 0.15625, ((0, 4), (1, 4)))
    w_up = gaussian(splits[5], (D_ENC, HID), D_ENC ** -0.5, 0.15625, ((0, 4), (1, 4)))
    w_down = gaussian(splits[6], (HID, D_ENC), HID ** -0.5, 0.09375, ((0, 4), (1, 4)))
    gain_slide = jnp.clip(1.0 + 0.18 * jax.random.normal(splits[7], (D_ENC,), jnp.float32), 0.1, 1.9)
    w_qkv = gaussian(splits[8], (D_ENC, 3 * D_SLIDE), D_ENC ** -0.5, 0.15625, ((1, 4),))
    offsets = place_ends(jax.random.randint(splits[9], (SLIDE_HEADS,), 0, DILATION_STEP), jax.random.fold_in(splits[9], 1), 0, DILATION_STEP - 1).astype(jnp.int32)
    return {"tiles": tiles, "counts": counts, "dest": dest, "gain_enc": gain_enc, "w_gate": w_gate, "w_up": w_up, "w_down": w_down, "gain_slide": gain_slide, "w_qkv": w_qkv, "offsets": offsets}


epsilon = 1e-05

def place_tiles(tiles, counts, dest):
    indices = jnp.arange(TILES, dtype=jnp.int32)
    source = indices // TILE_DEV
    live_rows = indices % TILE_DEV < counts[source]
    target = dest[:, 0]
    chosen = ((target[:, None] == jnp.arange(N_SEQ, dtype=jnp.int32)[None, :]) & live_rows[:, None]).astype(jnp.int32)
    blocked = chosen.reshape(N_SEQ, TILE_DEV, N_SEQ)
    earlier = (jnp.cumsum(blocked, axis=1) - blocked).reshape(TILES, N_SEQ)
    arrival = lax.optimization_barrier(jnp.sum(earlier * chosen, axis=1))
    position = jnp.where(live_rows, target * ENCODER_SLOTS + source * CAP + arrival, SEQUENCE_SLOTS).astype(jnp.int32)
    return jnp.zeros((SEQUENCE_SLOTS, D_ENC), jnp.bfloat16).at[position].set(tiles, mode='drop')

def encode_block(arrived, gain_enc, w_gate, w_up, w_down, gain_slide, w_qkv):
    arrived_f = arrived.astype(jnp.float32)
    inverse = lax.rsqrt(lax.optimization_barrier(jnp.mean(arrived_f * arrived_f, axis=-1, keepdims=True)) + epsilon)
    normed = (arrived_f * inverse * gain_enc).astype(jnp.bfloat16)
    gate_act = jnp.dot(normed, w_gate, preferred_element_type=jnp.float32)
    up_act = jnp.dot(normed, w_up, preferred_element_type=jnp.float32)
    hidden = (jax.nn.silu(gate_act) * up_act).astype(jnp.bfloat16)
    embedded = (arrived_f + jnp.dot(hidden, w_down, preferred_element_type=jnp.float32)).astype(jnp.bfloat16)
    embedded_f = embedded.astype(jnp.float32)
    slide_inverse = lax.rsqrt(lax.optimization_barrier(jnp.mean(embedded_f * embedded_f, axis=-1, keepdims=True)) + epsilon)
    scaled = (embedded_f * gain_slide).astype(jnp.bfloat16)
    return (jnp.dot(scaled, w_qkv, preferred_element_type=jnp.float32) * slide_inverse).astype(jnp.bfloat16)

def rounded_weights(weights):
    lowered = lax.optimization_barrier(weights.astype(jnp.bfloat16))
    return lowered.astype(jnp.float32)

def reference(tiles, counts, dest, gain_enc, w_gate, w_up, w_down, gain_slide, w_qkv, offsets):
    slots = place_tiles(tiles, counts, dest)
    blocks = slots.reshape(N_SEQ, ENCODER_SLOTS, D_ENC)
    projected = lax.map(lambda block_rows: encode_block(block_rows, gain_enc, w_gate, w_up, w_down, gain_slide, w_qkv), blocks)
    fields = projected.reshape(N_SEQ, ENCODER_SLOTS, SLIDE_HEADS, 3, HEAD_WIDTH)
    query_rows = fields[:, :, :, 0, :]
    gathered_keys = fields[:, :, :, 1, :]
    gathered_values = fields[:, :, :, 2, :]
    scale_factor = HEAD_WIDTH ** (-0.5)

    def local_branch(triple):
        query_block, key_block, value_block = triple
        scores = jnp.einsum('qhe,khe->hqk', query_block.astype(jnp.float32), key_block.astype(jnp.float32)) * scale_factor
        weights = jnp.exp(scores)
        numer = jnp.einsum('hqk,khe->qhe', rounded_weights(weights), value_block.astype(jnp.float32))
        return (numer, lax.optimization_barrier(jnp.sum(weights, axis=-1)).T)
    local_num, local_den = lax.map(local_branch, (query_rows, gathered_keys, gathered_values))
    local_num = local_num.reshape(SEQUENCE_SLOTS, SLIDE_HEADS, HEAD_WIDTH)
    local_den = local_den.reshape(SEQUENCE_SLOTS, SLIDE_HEADS)
    flattened_query = query_rows.reshape(SEQUENCE_SLOTS // DILATION_STEP, DILATION_STEP, SLIDE_HEADS, HEAD_WIDTH)
    flattened_key = gathered_keys.reshape(SEQUENCE_SLOTS // DILATION_STEP, DILATION_STEP, SLIDE_HEADS, HEAD_WIDTH)
    flattened_value = gathered_values.reshape(SEQUENCE_SLOTS // DILATION_STEP, DILATION_STEP, SLIDE_HEADS, HEAD_WIDTH)

    def pick_rows(slide_field, head_index, residue):
        per_head = lax.dynamic_index_in_dim(slide_field, head_index, 2, False)
        return lax.dynamic_index_in_dim(per_head, residue, 1, False).astype(jnp.float32)

    def global_branch(head_index):
        residue = offsets[head_index]
        query_sel = pick_rows(flattened_query, head_index, residue)
        key_sel = pick_rows(flattened_key, head_index, residue)
        value_sel = pick_rows(flattened_value, head_index, residue)
        scores = jnp.einsum('qe,ke->qk', query_sel, key_sel) * scale_factor
        weights = jnp.exp(scores)
        numer = jnp.einsum('qk,ke->qe', rounded_weights(weights), value_sel)
        return (numer, lax.optimization_barrier(jnp.sum(weights, axis=-1)))
    remote_num, remote_den = lax.map(global_branch, jnp.arange(SLIDE_HEADS, dtype=jnp.int32))
    row_selector = (jnp.arange(DILATION_STEP, dtype=jnp.int32)[None, :] == offsets[:, None]).astype(jnp.float32)
    spread_num = jnp.einsum('hre,hd->rdhe', remote_num, row_selector).reshape(SEQUENCE_SLOTS, SLIDE_HEADS, HEAD_WIDTH)
    spread_den = jnp.einsum('hr,hd->rdh', remote_den, row_selector).reshape(SEQUENCE_SLOTS, SLIDE_HEADS)
    result = (local_num + spread_num) / (local_den + spread_den)[..., None]
    return result.reshape(SEQUENCE_SLOTS, SLIDE_HEADS * HEAD_WIDTH).astype(jnp.bfloat16)
```

```python
import jax
import jax.numpy as jnp
from jax import lax
from jax.sharding import PartitionSpec as P

D_ENC = 1536
HEAD_WIDTH = 64
DILATION_STEP = 8
ENCODER_SLOTS = 256


epsilon = 1e-05


def gather_seq(package):
    count = lax.axis_size("seq")
    if count & (count - 1) == 0 and count <= 4:
        return jnp.concatenate([package] + [swap(package, "seq", d) for d in range(1, count)])
    return lax.all_gather(package, "seq", axis=0, tiled=True)


def gathered_plan(tiles, counts, dest, gain_enc, w_gate, w_up, w_down, gain_slide, w_qkv, offsets):
    seq_count = lax.axis_size("seq")
    capacity = ENCODER_SLOTS // seq_count
    tile_rows = tiles.shape[0]
    target = dest[:, 0]
    live_rows = jnp.arange(tile_rows, dtype=jnp.int32) < counts[0]
    chosen = (
        (target[:, None] == jnp.arange(seq_count, dtype=jnp.int32)[None, :]) & live_rows[:, None]
    ).astype(jnp.int32)
    arrival = jnp.sum((jnp.cumsum(chosen, axis=0) - chosen) * chosen, axis=1)
    slot_index = jnp.where(live_rows, target * capacity + arrival, ENCODER_SLOTS)
    outgoing = (
        jnp.zeros((ENCODER_SLOTS, D_ENC), jnp.bfloat16).at[slot_index].set(tiles, mode="drop")
    )
    arrived = lax.all_to_all(outgoing, "seq", split_axis=0, concat_axis=0, tiled=True)
    arrived_f = arrived.astype(jnp.float32)
    inverse = lax.rsqrt(jnp.mean(arrived_f * arrived_f, axis=-1, keepdims=True) + epsilon)
    normed = (arrived_f * inverse * gain_enc).astype(jnp.bfloat16)

    def add_rows(portion):
        return jnp.dot(normed, portion, preferred_element_type=jnp.float32)

    gate_act = add_rows(lax.all_gather(w_gate, "seq", axis=0, tiled=True))
    up_act = add_rows(lax.all_gather(w_up, "seq", axis=0, tiled=True))
    hidden = (jax.nn.silu(gate_act) * up_act).astype(jnp.bfloat16)
    partial_out = jnp.dot(
        hidden,
        lax.all_gather(w_down, "seq", axis=1, tiled=True),
        preferred_element_type=jnp.float32,
    )
    share = lax.psum_scatter(partial_out, "mp", scatter_dimension=1, tiled=True)
    share_width = share.shape[1]
    own_cols = lax.dynamic_slice_in_dim(
        arrived_f, lax.axis_index("mp") * share_width, share_width, 1
    )
    embedded_cols = (own_cols + share).astype(jnp.bfloat16)
    embedded = lax.all_gather(embedded_cols, "mp", axis=1, tiled=True)
    return slide_layer(embedded, gain_slide, w_qkv, offsets)


def slide_layer(embedded, gain_slide, w_qkv, offsets):
    portion_f = embedded.astype(jnp.float32)
    accumulated = jnp.dot(
        (portion_f * gain_slide).astype(jnp.bfloat16), w_qkv, preferred_element_type=jnp.float32
    )
    accumulated, squares = (accumulated, jnp.sum(portion_f * portion_f, axis=1))
    projected = accumulated * lax.rsqrt(squares / D_ENC + epsilon)[:, None]
    qkv_act = projected.astype(jnp.bfloat16)
    local_head_output = offsets.shape[0]
    fields = qkv_act.reshape(ENCODER_SLOTS, local_head_output, 3, HEAD_WIDTH)
    query_rows = fields[:, :, 0, :]
    keys_local = fields[:, :, 1, :]
    values_local = fields[:, :, 2, :]
    scale_factor = HEAD_WIDTH ** (-0.5)
    row_selector = (jnp.arange(DILATION_STEP, dtype=jnp.int32)[None, :] == offsets[:, None]).astype(
        jnp.float32
    )
    selected_rows = ENCODER_SLOTS // DILATION_STEP

    def select_rows(slide_field):
        reshaped_rows = slide_field.astype(jnp.float32).reshape(
            selected_rows, DILATION_STEP, local_head_output, HEAD_WIDTH
        )
        return jnp.einsum("rdhe,hd->rhe", reshaped_rows, row_selector).astype(jnp.bfloat16)

    query_sel = select_rows(query_rows)
    package = jnp.concatenate([select_rows(keys_local), select_rows(values_local)], axis=2).reshape(
        selected_rows, local_head_output * 2 * HEAD_WIDTH
    )
    portion = gather_seq(package)
    parts_kv = portion.reshape(portion.shape[0], local_head_output, 2, HEAD_WIDTH)
    scores = (
        jnp.einsum(
            "qhe,khe->hqk", query_sel, parts_kv[:, :, 0, :], preferred_element_type=jnp.float32
        )
        * scale_factor
    )
    weights = jnp.exp(scores)
    numer = jnp.einsum(
        "hqk,khe->hqe",
        weights.astype(jnp.bfloat16),
        parts_kv[:, :, 1, :],
        preferred_element_type=jnp.float32,
    )
    remote_den = jnp.sum(weights, axis=-1)
    scores = (
        jnp.einsum("qhe,khe->hqk", query_rows, keys_local, preferred_element_type=jnp.float32)
        * scale_factor
    )
    weights = jnp.exp(scores)
    local_num = jnp.einsum(
        "hqk,khe->hqe",
        weights.astype(jnp.bfloat16),
        values_local,
        preferred_element_type=jnp.float32,
    )
    local_den = jnp.sum(weights, axis=-1)
    spread_num = jnp.einsum("hre,hd->hrde", numer, row_selector).reshape(
        local_head_output, ENCODER_SLOTS, HEAD_WIDTH
    )
    spread_den = jnp.einsum("hr,hd->hrd", remote_den, row_selector).reshape(
        local_head_output, ENCODER_SLOTS
    )
    result = (local_num + spread_num) / (local_den + spread_den)[..., None]
    return (
        jnp.transpose(result, (1, 0, 2))
        .reshape(ENCODER_SLOTS, local_head_output * HEAD_WIDTH)
        .astype(jnp.bfloat16)
    )


def swap(array, axis, distance):
    size = lax.axis_size(axis)
    return lax.ppermute(array, axis, [(i, i ^ distance) for i in range(size)])


def block_at(array, index, size, axis):
    return lax.dynamic_slice_in_dim(array, index * size, size, axis)


def place_blocks(blocks, owner, axis):
    size = blocks[0].shape[axis]
    shape = list(blocks[0].shape)
    shape[axis] = size * len(blocks)
    whole = jnp.zeros(shape, blocks[0].dtype)
    for d, block in enumerate(blocks):
        whole = lax.dynamic_update_slice_in_dim(whole, block, (owner ^ d) * size, axis)
    return whole


def exchange_weights(block_for, after=None):
    seq, group = lax.axis_index("seq"), lax.axis_index("groups")
    count = lax.axis_size("seq")
    halved = lax.axis_size("groups") == 2
    outgoing = [block_for(seq ^ d) for d in range(count)]
    if halved:
        for d in range(2, count):
            outgoing[d] = block_at(outgoing[d], group, outgoing[d].shape[0] // 2, 0)
    if after is not None:
        outgoing, _ = lax.optimization_barrier((outgoing, after))
    incoming = [outgoing[0]] + [swap(outgoing[d], "seq", d) for d in range(1, count)]
    if halved:
        for d in range(2, count):
            mine = incoming[d]
            other = swap(mine, "groups", 1)
            incoming[d] = jnp.where(
                group == 0,
                jnp.concatenate([mine, other], axis=0),
                jnp.concatenate([other, mine], axis=0),
            )
    return incoming


def spread_mp(own, axis):
    blocks = [own]
    distance = lax.axis_size("mp") // 2
    found = {0: own}
    while distance >= 1:
        keys = sorted(found)
        sent = jnp.stack([found[k] for k in keys])
        got = swap(sent, "mp", distance)
        for i, k in enumerate(keys):
            found[k ^ distance] = got[i]
        distance //= 2
    blocks = [found[d] for d in range(lax.axis_size("mp"))]
    return place_blocks(blocks, lax.axis_index("mp"), axis)


def split_hidden_plan(
    tiles, counts, dest, gain_enc, w_gate, w_up, w_down, gain_slide, w_qkv, offsets
):
    count, mp_size = lax.axis_size("seq"), lax.axis_size("mp")
    seq, mp = lax.axis_index("seq"), lax.axis_index("mp")
    capacity = ENCODER_SLOTS // count
    tile_rows = tiles.shape[0]
    features = D_ENC // mp_size
    units = w_gate.shape[1] // count

    target = dest[:, 0]
    rows = jnp.arange(tile_rows, dtype=jnp.int32)
    live_rows = rows < counts[0]
    same = (target[:, None] == target[None, :]) & (rows[None, :] < rows[:, None])
    arrival = jnp.sum((same & live_rows[None, :]).astype(jnp.int32), axis=1)
    code = jnp.where(live_rows, target * capacity + arrival, ENCODER_SLOTS)

    own_tiles = block_at(tiles, mp, features, 1)
    code_row = jnp.pad(code.astype(jnp.bfloat16)[None, :], ((0, 15), (0, features - tile_rows)))
    package = jnp.concatenate([own_tiles, code_row], axis=0)
    arrived = [package] + [swap(package, "seq", d) for d in range(1, count)]
    own_quarter = jnp.concatenate([a[:tile_rows] for a in arrived], axis=0)

    def both_columns(dest_seq):
        return jnp.concatenate(
            [block_at(w_gate, dest_seq, units, 1), block_at(w_up, dest_seq, units, 1)], axis=1
        )

    gate_up_blocks = exchange_weights(both_columns, None)
    tokens = spread_mp(own_quarter, 1)
    gate_up = place_blocks(gate_up_blocks, seq, 0)

    down_parts = exchange_weights(
        lambda dest_seq: block_at(w_down, dest_seq, units, 0), gate_up_blocks[-1]
    )
    down_stack = jnp.stack(down_parts)
    down_rows = []
    for j in range(mp_size):
        part = lax.dynamic_index_in_dim(down_stack, seq ^ mp ^ j, 0, False)
        down_rows.append(swap(part, "mp", j) if j else part)
    down = place_blocks(down_rows, mp, 0)

    tokens_f = tokens.astype(jnp.float32)
    inverse = lax.rsqrt(jnp.mean(tokens_f * tokens_f, axis=-1, keepdims=True) + epsilon)
    normed = (tokens_f * inverse * gain_enc).astype(jnp.bfloat16)
    acts = jnp.dot(normed, gate_up, preferred_element_type=jnp.float32)
    hidden_own = (jax.nn.silu(acts[:, :units]) * acts[:, units:]).astype(jnp.bfloat16)
    hidden = spread_mp(hidden_own, 1)
    partial_out = jnp.dot(hidden, down, preferred_element_type=jnp.float32).astype(jnp.bfloat16)

    codes = jnp.stack([a[tile_rows, :tile_rows] for a in arrived]).astype(jnp.int32)
    owners = seq ^ jnp.arange(count, dtype=jnp.int32)[:, None]
    position = ((codes // capacity) ^ seq) * ENCODER_SLOTS + owners * capacity + codes % capacity
    position = jnp.where(codes < ENCODER_SLOTS, position, -1).reshape(-1)

    def routed(d, array):
        chosen = (
            jnp.arange(ENCODER_SLOTS, dtype=jnp.int32)[:, None] + d * ENCODER_SLOTS
            == position[None, :]
        ).astype(jnp.bfloat16)
        return jnp.dot(chosen, array, preferred_element_type=jnp.float32)

    share = routed(0, own_quarter)
    sums = [routed(0, partial_out)]
    for d in range(1, count):
        sums.append(swap(routed(d, partial_out).astype(jnp.bfloat16), "seq", d).astype(jnp.float32))
    embedded_cols = (share + sum(sums)).astype(jnp.bfloat16)
    embedded = spread_mp(embedded_cols, 1)
    return slide_layer(embedded, gain_slide, w_qkv, offsets)


def on_device(*arrays):
    count, mp_size = lax.axis_size("seq"), lax.axis_size("mp")
    if count == mp_size and count & (count - 1) == 0 and count <= 4:
        return split_hidden_plan(*arrays)
    return gathered_plan(*arrays)


def solution(mesh):
    return jax.shard_map(
        on_device,
        mesh=mesh,
        in_specs=(
            P(("groups", "seq"), None),
            P(("groups", "seq")),
            P(("groups", "seq"), None),
            P(),
            P("seq", "mp"),
            P("seq", "mp"),
            P("mp", "seq"),
            P(),
            P(None, "mp"),
            P("mp"),
        ),
        out_specs=P(("groups", "seq"), "mp"),
        check_vma=False,
    )
```

```python
import functools

import jax
import jax.numpy as jnp
from jax import lax
from jax.experimental import pallas as pl
from jax.experimental.pallas import tpu as pltpu
from jax.sharding import PartitionSpec as P

D_ENC = 1536
HEAD_WIDTH = 64
DILATION_STEP = 8
ENCODER_SLOTS = 256


epsilon = 1e-05


def gather_seq(package):
    count = lax.axis_size("seq")
    if count & (count - 1) == 0 and count <= 4:
        return jnp.concatenate([package] + [swap(package, "seq", d) for d in range(1, count)])
    return lax.all_gather(package, "seq", axis=0, tiled=True)


def gathered_plan(tiles, counts, dest, gain_enc, w_gate, w_up, w_down, gain_slide, w_qkv, offsets):
    seq_count = lax.axis_size("seq")
    capacity = ENCODER_SLOTS // seq_count
    tile_rows = tiles.shape[0]
    target = dest[:, 0]
    live_rows = jnp.arange(tile_rows, dtype=jnp.int32) < counts[0]
    chosen = (
        (target[:, None] == jnp.arange(seq_count, dtype=jnp.int32)[None, :]) & live_rows[:, None]
    ).astype(jnp.int32)
    arrival = jnp.sum((jnp.cumsum(chosen, axis=0) - chosen) * chosen, axis=1)
    slot_index = jnp.where(live_rows, target * capacity + arrival, ENCODER_SLOTS)
    outgoing = (
        jnp.zeros((ENCODER_SLOTS, D_ENC), jnp.bfloat16).at[slot_index].set(tiles, mode="drop")
    )
    arrived = lax.all_to_all(outgoing, "seq", split_axis=0, concat_axis=0, tiled=True)
    arrived_f = arrived.astype(jnp.float32)
    inverse = lax.rsqrt(jnp.mean(arrived_f * arrived_f, axis=-1, keepdims=True) + epsilon)
    normed = (arrived_f * inverse * gain_enc).astype(jnp.bfloat16)

    def add_rows(portion):
        return jnp.dot(normed, portion, preferred_element_type=jnp.float32)

    gate_act = add_rows(lax.all_gather(w_gate, "seq", axis=0, tiled=True))
    up_act = add_rows(lax.all_gather(w_up, "seq", axis=0, tiled=True))
    hidden = (jax.nn.silu(gate_act) * up_act).astype(jnp.bfloat16)
    partial_out = jnp.dot(
        hidden,
        lax.all_gather(w_down, "seq", axis=1, tiled=True),
        preferred_element_type=jnp.float32,
    )
    share = lax.psum_scatter(partial_out, "mp", scatter_dimension=1, tiled=True)
    share_width = share.shape[1]
    own_cols = lax.dynamic_slice_in_dim(
        arrived_f, lax.axis_index("mp") * share_width, share_width, 1
    )
    embedded_cols = (own_cols + share).astype(jnp.bfloat16)
    embedded = lax.all_gather(embedded_cols, "mp", axis=1, tiled=True)
    return slide_layer(embedded, gain_slide, w_qkv, offsets)


def slide_layer(embedded, gain_slide, w_qkv, offsets):
    portion_f = embedded.astype(jnp.float32)
    accumulated = jnp.dot(
        (portion_f * gain_slide).astype(jnp.bfloat16), w_qkv, preferred_element_type=jnp.float32
    )
    accumulated, squares = (accumulated, jnp.sum(portion_f * portion_f, axis=1))
    projected = accumulated * lax.rsqrt(squares / D_ENC + epsilon)[:, None]
    qkv_act = projected.astype(jnp.bfloat16)
    local_head_output = offsets.shape[0]
    fields = qkv_act.reshape(ENCODER_SLOTS, local_head_output, 3, HEAD_WIDTH)
    query_rows = fields[:, :, 0, :]
    keys_local = fields[:, :, 1, :]
    values_local = fields[:, :, 2, :]
    scale_factor = HEAD_WIDTH ** (-0.5)
    row_selector = (jnp.arange(DILATION_STEP, dtype=jnp.int32)[None, :] == offsets[:, None]).astype(
        jnp.float32
    )
    selected_rows = ENCODER_SLOTS // DILATION_STEP

    def select_rows(slide_field):
        reshaped_rows = slide_field.astype(jnp.float32).reshape(
            selected_rows, DILATION_STEP, local_head_output, HEAD_WIDTH
        )
        return jnp.einsum("rdhe,hd->rhe", reshaped_rows, row_selector).astype(jnp.bfloat16)

    query_sel = select_rows(query_rows)
    package = jnp.concatenate([select_rows(keys_local), select_rows(values_local)], axis=2).reshape(
        selected_rows, local_head_output * 2 * HEAD_WIDTH
    )
    portion = gather_seq(package)
    parts_kv = portion.reshape(portion.shape[0], local_head_output, 2, HEAD_WIDTH)
    scores = (
        jnp.einsum(
            "qhe,khe->hqk", query_sel, parts_kv[:, :, 0, :], preferred_element_type=jnp.float32
        )
        * scale_factor
    )
    weights = jnp.exp(scores)
    numer = jnp.einsum(
        "hqk,khe->hqe",
        weights.astype(jnp.bfloat16),
        parts_kv[:, :, 1, :],
        preferred_element_type=jnp.float32,
    )
    remote_den = jnp.sum(weights, axis=-1)
    scores = (
        jnp.einsum("qhe,khe->hqk", query_rows, keys_local, preferred_element_type=jnp.float32)
        * scale_factor
    )
    weights = jnp.exp(scores)
    local_num = jnp.einsum(
        "hqk,khe->hqe",
        weights.astype(jnp.bfloat16),
        values_local,
        preferred_element_type=jnp.float32,
    )
    local_den = jnp.sum(weights, axis=-1)
    spread_num = jnp.einsum("hre,hd->hrde", numer, row_selector).reshape(
        local_head_output, ENCODER_SLOTS, HEAD_WIDTH
    )
    spread_den = jnp.einsum("hr,hd->hrd", remote_den, row_selector).reshape(
        local_head_output, ENCODER_SLOTS
    )
    result = (local_num + spread_num) / (local_den + spread_den)[..., None]
    return (
        jnp.transpose(result, (1, 0, 2))
        .reshape(ENCODER_SLOTS, local_head_output * HEAD_WIDTH)
        .astype(jnp.bfloat16)
    )


def swap(array, axis, distance):
    size = lax.axis_size(axis)
    return lax.ppermute(array, axis, [(i, i ^ distance) for i in range(size)])


def block_at(array, index, size, axis):
    return lax.dynamic_slice_in_dim(array, index * size, size, axis)


def copy_all(pairs, sems):
    copies = [pltpu.make_async_copy(a, b, sems.at[i]) for i, (a, b) in enumerate(pairs)]
    for copy in copies:
        copy.start()
    for copy in copies:
        copy.wait()


def call(body, outs, inputs, ids, copies=0, scratch=(), spaces=None, cost=None):
    vmem, anywhere = pltpu.VMEM, pl.ANY
    spaces = spaces or [vmem] * len(inputs)
    in_specs = [pl.BlockSpec(memory_space=pltpu.SMEM)]
    in_specs += [pl.BlockSpec(memory_space=space) for space in spaces]
    out_space = anywhere if cost == "copies" else vmem
    scratch = list(scratch)
    if copies:
        scratch.append(pltpu.SemaphoreType.DMA((copies,)))
    return pl.pallas_call(
        body,
        out_shape=[jax.ShapeDtypeStruct(shape, kind) for shape, kind in outs],
        in_specs=in_specs,
        out_specs=[pl.BlockSpec(memory_space=out_space)] * len(outs),
        scratch_shapes=scratch,
        compiler_params=pltpu.CompilerParams(vmem_limit_bytes=40 * 1024 * 1024),
    )(ids, *inputs)


def at(index, size):
    return pl.ds(pl.multiple_of(index * size, size), size)


def cut_body(count, ids, tiles, w_gate, w_up, w_down, quarter, *outs_and_sems):
    outs, sems = outs_and_sems[:-1], outs_and_sems[-1]
    seq, mp, group = ids[0], ids[1], ids[2]
    depth = w_gate.shape[0]
    units = w_gate.shape[1] // count
    pairs = [(tiles.at[:, at(mp, quarter.shape[1])], quarter)]
    for d in range(1, count):
        target = outs[d - 1]
        rows = pl.ds(0, depth)
        if target.shape[0] != depth:
            rows = at(group, depth // 2)
        for i, weight in enumerate((w_gate, w_up)):
            pairs.append(
                (weight.at[rows, at(seq ^ d, units)], target.at[:, pl.ds(i * units, units)])
            )
    for e in range(count):
        target = outs[count - 1 + e]
        half = target.shape[0]
        pairs.append((w_down.at[at((e ^ mp) * 2 + group, half), :], target))
    copy_all(pairs, sems)


def hidden_body(count, ids, gain, tiles, w_gate, w_up, *refs):
    (own, far, near, near_far) = refs[: count - 1], *refs[count - 1 : count + 2]
    blocks = refs[count + 2 : count + 7]
    first, second, weights, sems = refs[count + 7 :]
    seq, mp, group = ids[0], ids[1], ids[2]
    depth = w_gate.shape[0]
    units = w_gate.shape[1] // count
    half = depth // 2
    pairs = []
    for i, weight in enumerate((w_gate, w_up)):
        pairs.append(
            (weight.at[:, at(seq, units)], weights.at[at(seq, depth), pl.ds(i * units, units)])
        )
    pairs.append((blocks[0], weights.at[at(seq ^ 1, depth), :]))
    for d in (2, 3):
        mine, other = blocks[2 * d - 3], blocks[2 * d - 2]
        pairs.append((mine, weights.at[at((seq ^ d) * 2 + group, half), :]))
        pairs.append((other, weights.at[at((seq ^ d) * 2 + 1 - group, half), :]))
    copy_all(pairs, sems)

    def gated(pieces):
        values = [piece.astype(jnp.float32) for piece, _ in pieces]
        squares = sum(jnp.sum(v * v, axis=1, keepdims=True) for v in values)
        inverse = lax.rsqrt(squares * (1.0 / D_ENC) + epsilon)
        acts = 0.0
        for v, (_, index) in zip(values, pieces):
            normed = (v * inverse * gain[:, at(index, depth)]).astype(jnp.bfloat16)
            acts += jnp.dot(normed, weights[at(index, depth), :], preferred_element_type=jnp.float32)
        gate_act = acts[:, :units]
        return (gate_act * jax.nn.sigmoid(gate_act) * acts[:, units:]).astype(jnp.bfloat16)

    rows = tiles.shape[0]
    for d in (2, 3, 1, 0):
        if d == 0:
            pieces = [(tiles[:, pl.ds(q * depth, depth)], q) for q in range(count)]
        else:
            pieces = [(own[d - 1][...], mp), (far[d - 1], mp ^ 2)]
            pieces += [(near[d - 1], mp ^ 1), (near_far[d - 1], mp ^ 3)]
        out = first if d >= 2 else second
        out[pl.ds((d % 2) * rows, rows), :] = gated(pieces)


def down_body(count, keep, ids, own, far, near, near_far, *refs):
    parts = refs[: 2 * count]
    low, high, weights, sems = refs[2 * count :]
    seq, mp, group = ids[0], ids[1], ids[2]
    units = own.shape[1]
    half = units // 2
    pairs = []
    for e in range(count):
        pairs.append((parts[2 * e], weights.at[at((e ^ seq) * 2 + group, half), :]))
        pairs.append((parts[2 * e + 1], weights.at[at((e ^ seq) * 2 + 1 - group, half), :]))
    copy_all(pairs, sems)
    rows = low.shape[0]
    for i, out in enumerate((low, high)):
        span = pl.ds(i * rows, rows)
        total = 0.0
        for piece, index in ((own, mp), (far, mp ^ 2), (near, mp ^ 1), (near_far, mp ^ 3)):
            total += jnp.dot(
                piece[span, :], weights[at(index, units), :], preferred_element_type=jnp.float32
            )
        out[...] = total.astype(out.dtype)


def project_body(count, ids, gain, code, w_qkv, own, far, near, near_far, *outs):
    seq, mp = ids[0], ids[1]
    features = own.shape[1]
    capacity = outs[0].shape[0]
    heads = w_qkv.shape[1] // (3 * HEAD_WIDTH)
    squares, total = 0.0, 0.0
    for piece, index in ((own, mp), (far, mp ^ 2), (near, mp ^ 1), (near_far, mp ^ 3)):
        v = piece[...].astype(jnp.float32)
        squares += jnp.sum(v * v, axis=1, keepdims=True)
        scaled = (v * gain[:, at(index, features)]).astype(jnp.bfloat16)
        total += jnp.dot(
            scaled, w_qkv[at(index, features), :], preferred_element_type=jnp.float32
        )
    projected = (total * lax.rsqrt(squares / D_ENC + epsilon)).astype(jnp.bfloat16)
    codes = code[...]
    rows = codes.shape[1]
    slot = lax.broadcasted_iota(jnp.int32, (capacity, rows), 0)

    def pick(wanted, array):
        chosen = jnp.where(codes == wanted, 1.0, 0.0).astype(jnp.bfloat16)
        return jnp.dot(chosen, array, preferred_element_type=jnp.float32).astype(jnp.bfloat16)

    spread = []
    per_block = capacity // DILATION_STEP
    index = lax.broadcasted_iota(jnp.int32, (count * per_block, rows), 0)
    for h in range(heads):
        wanted = (index // per_block) * capacity + (index % per_block) * DILATION_STEP + ids[4 + h]
        start = (3 * h + 1) * HEAD_WIDTH
        both = pick(wanted, projected[:, start : start + 2 * HEAD_WIDTH])
        spread.append(
            jnp.concatenate([both[:, :HEAD_WIDTH], both[:, HEAD_WIDTH:]], axis=0)
        )
    width = projected.shape[1]
    beside = jnp.concatenate(spread, axis=1)
    for d, out in enumerate(outs):
        out[:, :width] = pick((seq ^ d) * capacity + slot, projected)
        out[:, width:] = beside


def attend_body(count, ids, *refs):
    packages, out, rows = refs[:count], refs[count], refs[count + 1]
    seq = ids[0]
    capacity = packages[0].shape[0]
    heads = out.shape[1] // HEAD_WIDTH
    width = heads * 3 * HEAD_WIDTH
    for d, package in enumerate(packages):
        rows[at(seq ^ d, capacity), :] = package[:, :width]
    far = [package[:, width:] for package in packages]
    half = capacity // 2
    far_keys = jnp.concatenate([f[:half] for f in far], axis=0)
    far_values = jnp.concatenate([f[half:] for f in far], axis=0)
    residue = lax.broadcasted_iota(jnp.int32, (out.shape[0], 1), 0) % DILATION_STEP
    scale_factor = HEAD_WIDTH ** (-0.5)

    def branch(query, key, value, mask):
        scores = lax.dot_general(
            query, key, (((1,), (1,)), ((), ())), preferred_element_type=jnp.float32
        )
        weights = jnp.exp(scores * scale_factor)
        if mask is not None:
            weights = jnp.where(mask, weights, 0.0)
        numer = jnp.dot(
            weights.astype(jnp.bfloat16), value, preferred_element_type=jnp.float32
        )
        return numer, jnp.sum(weights, axis=1, keepdims=True)

    results = []
    for h in range(heads):
        query, key, value = (
            rows[:, pl.ds((3 * h + i) * HEAD_WIDTH, HEAD_WIDTH)] for i in range(3)
        )
        span = slice(h * HEAD_WIDTH, (h + 1) * HEAD_WIDTH)
        near_num, near_den = branch(query, key, value, None)
        far_num, far_den = branch(query, far_keys[:, span], far_values[:, span], residue == ids[4 + h])
        results.append((near_num + far_num) / (near_den + far_den))
    out[...] = jnp.concatenate(results, axis=1).astype(jnp.bfloat16)


def spread_mp(own):
    far = swap(own, "mp", 2)
    return far, swap(own, "mp", 1), swap(far, "mp", 1)


def split_hidden_plan(
    tiles, counts, dest, gain_enc, w_gate, w_up, w_down, gain_slide, w_qkv, offsets
):
    count, mp_size = lax.axis_size("seq"), lax.axis_size("mp")
    seq, mp, group = (lax.axis_index(name) for name in ("seq", "mp", "groups"))
    capacity = ENCODER_SLOTS // count
    tile_rows = tiles.shape[0]
    features = D_ENC // mp_size
    depth = w_gate.shape[0]
    units = w_gate.shape[1] // count
    bf16 = jnp.bfloat16
    ids = jnp.concatenate(
        [jnp.stack([seq, mp, group, counts[0]]).astype(jnp.int32), offsets]
    )
    anywhere = pl.ANY

    cut = call(
        functools.partial(cut_body, count),
        [((tile_rows, features), bf16), ((depth, 2 * units), bf16)]
        + [((depth // 2, 2 * units), bf16)] * (count - 2)
        + [((units // 2, features), bf16)] * count,
        (tiles, w_gate, w_up, w_down),
        ids,
        copies=1 + 2 * (count - 1) + count,
        spaces=[anywhere] * 4,
        cost="copies",
    )
    quarter, gate_up_out, down_out = cut[0], cut[1:count], cut[count:]

    own = [swap(quarter, "seq", d) for d in range(1, count)]
    blocks = [swap(gate_up_out[0], "seq", 1)]
    for d in range(2, count):
        mine = swap(gate_up_out[d - 1], "seq", d)
        blocks += [mine, swap(mine, "groups", 1)]
    spread = spread_mp(jnp.stack(own))
    first, second = call(
        functools.partial(hidden_body, count),
        [((2 * tile_rows, units), bf16)] * 2,
        (gain_enc[None, :], tiles, w_gate, w_up, *own, *spread, *blocks),
        ids,
        copies=7,
        scratch=[pltpu.VMEM((D_ENC, 2 * units), bf16)],
        spaces=[pltpu.VMEM] * 2 + [anywhere] * 2 + [pltpu.VMEM] * (count + 2) + [anywhere] * 5,
    )

    parts = []
    for e in range(count):
        send, _ = lax.optimization_barrier((down_out[e], blocks[-2]))
        perm = []
        for s in range(count):
            for m in range(mp_size):
                perm.append((s * mp_size + m, (e ^ m) * mp_size + s))
        mine = lax.ppermute(send, ("seq", "mp"), perm)
        parts.append(mine)
    others = swap(jnp.stack(parts), "groups", 1)
    parts = [piece for e in range(count) for piece in (parts[e], others[e])]

    def down(rows_hidden, kinds):
        return call(
            functools.partial(down_body, count, None),
            [((tile_rows, features), kind) for kind in kinds],
            (rows_hidden, *spread_mp(rows_hidden), *parts),
            ids,
            copies=2 * count,
            scratch=[pltpu.VMEM((count * units, features), bf16)],
            spaces=[pltpu.VMEM] * 4 + [anywhere] * (2 * count),
        )

    sum_2, sum_3 = down(first, (bf16, bf16))
    sum_0, sum_1 = down(second, (jnp.float32, bf16))
    arrived = [swap(part, "seq", d) for d, part in ((2, sum_2), (3, sum_3), (1, sum_1))]
    embedded_cols = (
        block_at(tiles, mp, features, 1).astype(jnp.float32)
        + (sum_0 + sum(part.astype(jnp.float32) for part in arrived))
    ).astype(bf16)

    target = dest[:, 0]
    rows = jnp.arange(tile_rows, dtype=jnp.int32)
    live_rows = rows < counts[0]
    same = (target[None, :] == dest) & (rows[:, None] < rows[None, :])
    arrival = jnp.sum((same & live_rows[:, None]).astype(jnp.int32), axis=0)
    code = jnp.where(live_rows, target * capacity + arrival, -1)[None, :]

    heads = offsets.shape[0]
    packages = call(
        functools.partial(project_body, count),
        [((capacity, 4 * heads * HEAD_WIDTH), bf16)] * count,
        (gain_slide[None, :], code, w_qkv, embedded_cols, *spread_mp(embedded_cols)),
        ids,
    )
    packages = [packages[0]] + [swap(packages[d], "seq", d) for d in range(1, count)]
    return call(
        functools.partial(attend_body, count),
        [((ENCODER_SLOTS, heads * HEAD_WIDTH), bf16)],
        tuple(packages),
        ids,
        scratch=[pltpu.VMEM((ENCODER_SLOTS, 3 * heads * HEAD_WIDTH), bf16)],
    )[0]


def on_device(*arrays):
    sizes = lax.axis_size("groups"), lax.axis_size("seq"), lax.axis_size("mp")
    if sizes == (2, 4, 4):
        return split_hidden_plan(*arrays)
    return gathered_plan(*arrays)


def solution(mesh):
    return jax.shard_map(
        on_device,
        mesh=mesh,
        in_specs=(
            P(("groups", "seq"), None),
            P(("groups", "seq")),
            P(("groups", "seq"), None),
            P(),
            P("seq", "mp"),
            P("seq", "mp"),
            P("mp", "seq"),
            P(),
            P(None, "mp"),
            P("mp"),
        ),
        out_specs=P(("groups", "seq"), "mp"),
        check_vma=False,
    )
```

```python
import functools

import jax
import jax.numpy as jnp
from jax import lax
from jax.experimental import pallas as pl
from jax.experimental.pallas import tpu as pltpu
from jax.sharding import PartitionSpec as P

D_ENC = 1536
HEAD_WIDTH = 64
DILATION_STEP = 8
ENCODER_SLOTS = 256


epsilon = 1e-05


def gather_seq(package):
    count = lax.axis_size("seq")
    if count & (count - 1) == 0 and count <= 4:
        return jnp.concatenate([package] + [swap(package, "seq", d) for d in range(1, count)])
    return lax.all_gather(package, "seq", axis=0, tiled=True)


def gathered_plan(tiles, counts, dest, gain_enc, w_gate, w_up, w_down, gain_slide, w_qkv, offsets):
    seq_count = lax.axis_size("seq")
    capacity = ENCODER_SLOTS // seq_count
    tile_rows = tiles.shape[0]
    target = dest[:, 0]
    live_rows = jnp.arange(tile_rows, dtype=jnp.int32) < counts[0]
    chosen = (
        (target[:, None] == jnp.arange(seq_count, dtype=jnp.int32)[None, :]) & live_rows[:, None]
    ).astype(jnp.int32)
    arrival = jnp.sum((jnp.cumsum(chosen, axis=0) - chosen) * chosen, axis=1)
    slot_index = jnp.where(live_rows, target * capacity + arrival, ENCODER_SLOTS)
    outgoing = (
        jnp.zeros((ENCODER_SLOTS, D_ENC), jnp.bfloat16).at[slot_index].set(tiles, mode="drop")
    )
    arrived = lax.all_to_all(outgoing, "seq", split_axis=0, concat_axis=0, tiled=True)
    arrived_f = arrived.astype(jnp.float32)
    inverse = lax.rsqrt(jnp.mean(arrived_f * arrived_f, axis=-1, keepdims=True) + epsilon)
    normed = (arrived_f * inverse * gain_enc).astype(jnp.bfloat16)

    def add_rows(portion):
        return jnp.dot(normed, portion, preferred_element_type=jnp.float32)

    gate_act = add_rows(lax.all_gather(w_gate, "seq", axis=0, tiled=True))
    up_act = add_rows(lax.all_gather(w_up, "seq", axis=0, tiled=True))
    hidden = (jax.nn.silu(gate_act) * up_act).astype(jnp.bfloat16)
    partial_out = jnp.dot(
        hidden,
        lax.all_gather(w_down, "seq", axis=1, tiled=True),
        preferred_element_type=jnp.float32,
    )
    share = lax.psum_scatter(partial_out, "mp", scatter_dimension=1, tiled=True)
    share_width = share.shape[1]
    own_cols = lax.dynamic_slice_in_dim(
        arrived_f, lax.axis_index("mp") * share_width, share_width, 1
    )
    embedded_cols = (own_cols + share).astype(jnp.bfloat16)
    embedded = lax.all_gather(embedded_cols, "mp", axis=1, tiled=True)
    return slide_layer(embedded, gain_slide, w_qkv, offsets)


def slide_layer(embedded, gain_slide, w_qkv, offsets):
    portion_f = embedded.astype(jnp.float32)
    accumulated = jnp.dot(
        (portion_f * gain_slide).astype(jnp.bfloat16), w_qkv, preferred_element_type=jnp.float32
    )
    accumulated, squares = (accumulated, jnp.sum(portion_f * portion_f, axis=1))
    projected = accumulated * lax.rsqrt(squares / D_ENC + epsilon)[:, None]
    qkv_act = projected.astype(jnp.bfloat16)
    local_head_output = offsets.shape[0]
    fields = qkv_act.reshape(ENCODER_SLOTS, local_head_output, 3, HEAD_WIDTH)
    query_rows = fields[:, :, 0, :]
    keys_local = fields[:, :, 1, :]
    values_local = fields[:, :, 2, :]
    scale_factor = HEAD_WIDTH ** (-0.5)
    row_selector = (jnp.arange(DILATION_STEP, dtype=jnp.int32)[None, :] == offsets[:, None]).astype(
        jnp.float32
    )
    selected_rows = ENCODER_SLOTS // DILATION_STEP

    def select_rows(slide_field):
        reshaped_rows = slide_field.astype(jnp.float32).reshape(
            selected_rows, DILATION_STEP, local_head_output, HEAD_WIDTH
        )
        return jnp.einsum("rdhe,hd->rhe", reshaped_rows, row_selector).astype(jnp.bfloat16)

    query_sel = select_rows(query_rows)
    package = jnp.concatenate([select_rows(keys_local), select_rows(values_local)], axis=2).reshape(
        selected_rows, local_head_output * 2 * HEAD_WIDTH
    )
    portion = gather_seq(package)
    parts_kv = portion.reshape(portion.shape[0], local_head_output, 2, HEAD_WIDTH)
    scores = (
        jnp.einsum(
            "qhe,khe->hqk", query_sel, parts_kv[:, :, 0, :], preferred_element_type=jnp.float32
        )
        * scale_factor
    )
    weights = jnp.exp(scores)
    numer = jnp.einsum(
        "hqk,khe->hqe",
        weights.astype(jnp.bfloat16),
        parts_kv[:, :, 1, :],
        preferred_element_type=jnp.float32,
    )
    remote_den = jnp.sum(weights, axis=-1)
    scores = (
        jnp.einsum("qhe,khe->hqk", query_rows, keys_local, preferred_element_type=jnp.float32)
        * scale_factor
    )
    weights = jnp.exp(scores)
    local_num = jnp.einsum(
        "hqk,khe->hqe",
        weights.astype(jnp.bfloat16),
        values_local,
        preferred_element_type=jnp.float32,
    )
    local_den = jnp.sum(weights, axis=-1)
    spread_num = jnp.einsum("hre,hd->hrde", numer, row_selector).reshape(
        local_head_output, ENCODER_SLOTS, HEAD_WIDTH
    )
    spread_den = jnp.einsum("hr,hd->hrd", remote_den, row_selector).reshape(
        local_head_output, ENCODER_SLOTS
    )
    result = (local_num + spread_num) / (local_den + spread_den)[..., None]
    return (
        jnp.transpose(result, (1, 0, 2))
        .reshape(ENCODER_SLOTS, local_head_output * HEAD_WIDTH)
        .astype(jnp.bfloat16)
    )


def swap(array, axis, distance):
    size = lax.axis_size(axis)
    return lax.ppermute(array, axis, [(i, i ^ distance) for i in range(size)])


def block_at(array, index, size, axis):
    return lax.dynamic_slice_in_dim(array, index * size, size, axis)


def call(body, outs, inputs, spaces=None, scratch=(), copies=0, megabytes=40):
    spaces = spaces or [pltpu.VMEM] * len(inputs)
    out_space = pl.ANY if copies else pltpu.VMEM
    scratch = list(scratch)
    if copies:
        scratch.append(pltpu.SemaphoreType.DMA((copies,)))
    return pl.pallas_call(
        body,
        out_shape=[jax.ShapeDtypeStruct(shape, kind) for shape, kind in outs],
        in_specs=[pl.BlockSpec(memory_space=space) for space in spaces],
        out_specs=[pl.BlockSpec(memory_space=out_space)] * len(outs),
        scratch_shapes=scratch,
        compiler_params=pltpu.CompilerParams(vmem_limit_bytes=megabytes * 1024 * 1024),
    )(*inputs)


def at(index, size):
    return pl.ds(pl.multiple_of(index * size, size), size)


def place():
    return tuple(lax.axis_index(name) for name in ("seq", "mp", "groups"))


def column_block(seq, mp):
    step = jnp.where(mp == 2, seq + 1, seq + 3) & 3
    return jnp.where(mp < 2, seq ^ (2 * mp), step)


def column_user(seq, mp):
    step = jnp.where(mp == 2, seq + 3, seq + 1) & 3
    return jnp.where(mp < 2, seq ^ (2 * mp), step)


def cut_body(
    count, tiles, w_gate, w_up, w_down, quarter, mixed, third, next_block, kept, *downs_and_sems
):
    downs, sems = downs_and_sems[:-1], downs_and_sems[-1]
    seq, mp, group = place()
    depth, units = w_gate.shape[0], w_gate.shape[1] // count
    half, features = depth // 2, quarter.shape[1]
    copies = []

    def copy(source, target, other=None):
        started = pltpu.make_async_copy(source, target, sems.at[len(copies)])
        if other is None:
            started.start()
        else:
            second = pltpu.make_async_copy(other, target, sems.at[len(copies)])
            pl.when(group == 0)(started.start)
            pl.when(group != 0)(second.start)
        copies.append(started)

    own_columns = tiles.at[:, at(mp, features)]
    copy(own_columns, quarter)
    copy(own_columns, mixed.at[:, pl.ds(0, features)])
    for owner, target, start in ((seq ^ 2, mixed, features), (seq ^ 3, third, 0)):
        for i in range(2):
            span = pl.ds(i * half, half), at(owner, units)
            copy(w_gate.at[span], target.at[:, pl.ds(start + i * units, units)], w_up.at[span])
    for owner, target in ((seq ^ 1, next_block), (seq, kept)):
        for i, weight in enumerate((w_gate, w_up)):
            copy(weight.at[:, at(owner, units)], target.at[:, pl.ds(i * units, units)])
    for j, down in enumerate(downs):
        copy(w_down.at[at(column_user(seq, mp ^ j), units), :], down)
    for started in copies:
        started.wait()


def restack_body(first, mixed, third, stacked, columns):
    features = first.shape[1]
    stacked[0] = first[...]
    stacked[1] = mixed[:, :features]
    stacked[2] = third[...]
    columns[...] = mixed[:, features:]


def code_body(capacity, counts, dest, dest_row, code):
    rows = dest_row.shape[1]
    later = lax.broadcasted_iota(jnp.int32, (rows, rows), 1)
    earlier = lax.broadcasted_iota(jnp.int32, (rows, rows), 0)
    same = (dest[...] == dest_row[...]) & (earlier < later)
    rank = jnp.sum(jnp.where(same, 1, 0), axis=0, keepdims=True)
    live = lax.broadcasted_iota(jnp.int32, (1, rows), 1) < counts[0]
    code[...] = jnp.where(live, dest_row[...] * capacity + rank, -1)


def hidden_body(
    count, gain, tiles, own, far, near, near_far, kept, next_block, *refs
):
    halves, (first, second, normed, weights) = refs[:4], refs[4:]
    seq, mp, group = place()
    depth, units = weights.shape[1:]
    half = depth // 2
    rows = tiles.shape[0]
    for i, piece in enumerate(halves):
        weights[i, :half, :] = piece[:, :units]
        weights[i, half:, :] = piece[:, units:]

    def gated(d):
        if d == 0:
            pieces = [(tiles[:, pl.ds(q * depth, depth)], q) for q in range(count)]
        else:
            pieces = [(own[d - 1], mp), (far[d - 1], mp ^ 2)]
            pieces += [(near[d - 1], mp ^ 1), (near_far[d - 1], mp ^ 3)]
        values = [piece.astype(jnp.float32) for piece, _ in pieces]
        squares = sum(jnp.sum(v * v, axis=1, keepdims=True) for v in values)
        inverse = lax.rsqrt(squares * (1.0 / D_ENC) + epsilon)
        for v, (_, index) in zip(values, pieces):
            normed[index] = (v * inverse * gain[:, at(index, depth)]).astype(jnp.bfloat16)
        dot = functools.partial(jnp.dot, preferred_element_type=jnp.float32)
        both = dot(normed[seq], kept[...]) + dot(normed[seq ^ 1], next_block[...])
        mine = dot(normed[seq ^ 2], weights[0]) + dot(normed[seq ^ 3], weights[2])
        other = dot(normed[seq ^ 2], weights[1]) + dot(normed[seq ^ 3], weights[3])
        gate_act = both[:, :units] + jnp.where(group == 0, mine, other)
        up_act = both[:, units:] + jnp.where(group == 0, other, mine)
        return (gate_act * jax.nn.sigmoid(gate_act) * up_act).astype(jnp.bfloat16)

    for d in range(count - 1, -1, -1):
        out = first if d >= 2 else second
        out[pl.ds((d % 2) * rows, rows), :] = gated(d)


def down_body(own, far, near, near_far, weights, low, high):
    rows = low.shape[0]
    for i, out in enumerate((low, high)):
        total = 0.0
        for j, piece in enumerate((own, near, far, near_far)):
            total += jnp.dot(
                piece[pl.ds(i * rows, rows), :], weights[j], preferred_element_type=jnp.float32
            )
        out[...] = total.astype(out.dtype)


def project_body(count, offsets, gain, code, w_qkv_t, own, far, near, near_far, *outs):
    seq, mp, _ = place()
    features = own.shape[1]
    capacity = outs[0].shape[0]
    heads = offsets.shape[0]
    squares, total = 0.0, 0.0
    for j, piece in enumerate((own, near, far, near_far)):
        index = column_block(seq, mp ^ j)
        v = piece[...].astype(jnp.float32)
        squares += jnp.sum(v * v, axis=1, keepdims=True)
        scaled = (v * gain[:, at(index, features)]).astype(jnp.bfloat16)
        total += lax.dot_general(
            scaled,
            w_qkv_t[:, at(index, features)],
            (((1,), (1,)), ((), ())),
            preferred_element_type=jnp.float32,
        )
    projected = (total * lax.rsqrt(squares * (1.0 / D_ENC) + epsilon)).astype(jnp.bfloat16)
    codes = code[...]
    rows = codes.shape[1]

    def pick(wanted, array):
        chosen = jnp.where(codes == wanted, 1.0, 0.0).astype(jnp.bfloat16)
        return jnp.dot(chosen, array, preferred_element_type=jnp.float32).astype(jnp.bfloat16)

    spread = []
    per_block = capacity // DILATION_STEP
    index = lax.broadcasted_iota(jnp.int32, (count * per_block, rows), 0)
    for h in range(heads):
        wanted = (index // per_block) * capacity + (index % per_block) * DILATION_STEP + offsets[h]
        start = (3 * h + 1) * HEAD_WIDTH
        both = pick(wanted, projected[:, start : start + 2 * HEAD_WIDTH])
        spread.append(jnp.concatenate([both[:, :HEAD_WIDTH], both[:, HEAD_WIDTH:]], axis=0))
    width = projected.shape[1]
    beside = jnp.concatenate(spread, axis=1)
    slot = lax.broadcasted_iota(jnp.int32, (capacity, rows), 0)
    for d, out in enumerate(outs):
        out[:, :width] = pick((seq ^ d) * capacity + slot, projected)
        out[:, width:] = beside


def attend_body(count, offsets, *refs):
    packages, out, rows = refs[:count], refs[count], refs[count + 1]
    seq, _, _ = place()
    capacity = packages[0].shape[0]
    heads = offsets.shape[0]
    width = heads * 3 * HEAD_WIDTH
    for d, package in enumerate(packages):
        rows[at(seq ^ d, capacity), :] = package[:, :width]
    far = [package[:, width:] for package in packages]
    half = capacity // 2
    far_keys = jnp.concatenate([f[:half] for f in far], axis=0)
    far_values = jnp.concatenate([f[half:] for f in far], axis=0)
    residue = lax.broadcasted_iota(jnp.int32, (1, out.shape[1]), 1) % DILATION_STEP
    scale_factor = HEAD_WIDTH ** (-0.5)

    def branch(query, key, value, mask):
        scores = lax.dot_general(
            key, query, (((1,), (1,)), ((), ())), preferred_element_type=jnp.float32
        )
        weights = jnp.exp(scores * scale_factor)
        if mask is not None:
            weights = jnp.where(mask, weights, 0.0)
        numer = lax.dot_general(
            value,
            weights.astype(jnp.bfloat16),
            (((0,), (0,)), ((), ())),
            preferred_element_type=jnp.float32,
        )
        return numer, jnp.sum(weights, axis=0, keepdims=True)

    for h in range(heads):
        query, key, value = (
            rows[:, pl.ds((3 * h + i) * HEAD_WIDTH, HEAD_WIDTH)] for i in range(3)
        )
        span = slice(h * HEAD_WIDTH, (h + 1) * HEAD_WIDTH)
        near_num, near_den = branch(query, key, value, None)
        mask = residue == offsets[h]
        far_num, far_den = branch(query, far_keys[:, span], far_values[:, span], mask)
        out[span, :] = ((near_num + far_num) / (near_den + far_den)).astype(jnp.bfloat16)


def spread_mp(own, after=None):
    far = swap(own, "mp", 2)
    near = swap(own, "mp", 1)
    relayed = far
    if after is not None:
        relayed, _ = lax.optimization_barrier((far, after))
    return far, near, swap(relayed, "mp", 1)


def split_hidden_plan(
    tiles, counts, dest, gain_enc, w_gate, w_up, w_down, gain_slide, w_qkv, offsets
):
    count, mp_size = lax.axis_size("seq"), lax.axis_size("mp")
    seq, mp = lax.axis_index("seq"), lax.axis_index("mp")
    capacity = ENCODER_SLOTS // count
    tile_rows = tiles.shape[0]
    features = D_ENC // mp_size
    depth = w_gate.shape[0]
    units = w_gate.shape[1] // count
    heads = offsets.shape[0]
    bf16 = jnp.bfloat16
    vmem, smem = pltpu.VMEM, pltpu.SMEM

    quarter, mixed, third, next_block, kept, *downs = call(
        functools.partial(cut_body, count),
        [
            ((tile_rows, features), bf16),
            ((depth // 2, features + 2 * units), bf16),
            ((depth // 2, 2 * units), bf16),
            ((depth, 2 * units), bf16),
            ((depth, 2 * units), bf16),
        ]
        + [((units, features), bf16)] * mp_size,
        (tiles, w_gate, w_up, w_down),
        spaces=[pltpu.HBM] * 4,
        copies=10 + mp_size,
        megabytes=60,
    )
    code = call(
        functools.partial(code_body, capacity),
        [((1, tile_rows), jnp.int32)],
        (counts, dest, dest.reshape(1, tile_rows)),
        spaces=[smem, vmem, vmem],
    )[0]

    own_1, mixed_in, own_3 = swap(quarter, "seq", 1), swap(mixed, "seq", 2), swap(quarter, "seq", 3)
    downs = [downs[0]] + [swap(downs[j], "mp", j) for j in range(1, mp_size)]
    own_1, mixed_in, own_3, downs, code = lax.optimization_barrier(
        (own_1, mixed_in, own_3, downs, code)
    )
    own, columns = call(
        restack_body,
        [((count - 1, tile_rows, features), bf16), (third.shape, bf16)],
        (own_1, mixed_in, own_3),
    )
    third, next_block, _ = lax.optimization_barrier((third, next_block, own))
    third_in, next_in = swap(third, "seq", 3), swap(next_block, "seq", 1)
    halves = [columns, swap(columns, "groups", 1), third_in, swap(third_in, "groups", 1)]
    spread = spread_mp(own)
    first, second = call(
        functools.partial(hidden_body, count),
        [((2 * tile_rows, units), bf16)] * 2,
        (gain_enc[None, :], tiles, own, *spread, kept, next_in, *halves),
        scratch=[
            pltpu.VMEM((count, tile_rows, depth), bf16),
            pltpu.VMEM((len(halves), depth, units), bf16),
        ],
    )

    down_send, _ = lax.optimization_barrier((jnp.stack(downs), (third_in, next_in)))
    perm = []
    for s in range(count):
        for m in range(mp_size):
            user = (s ^ 2 * m) if m < 2 else (s + 2 * m - 5) % count
            perm.append((s * mp_size + m, user * mp_size + m))
    down_in = lax.ppermute(down_send, ("seq", "mp"), perm)

    def down(rows_hidden, kinds, after):
        return call(
            down_body,
            [((tile_rows, features), kind) for kind in kinds],
            (rows_hidden, *spread_mp(rows_hidden, after), down_in),
        )

    sum_2, sum_3 = down(first, (bf16, bf16), None)
    sum_0, sum_1 = down(second, (jnp.float32, bf16), sum_2)
    holder = [0, 2, 1, 3]

    def to_owner(part, d):
        perm = []
        for s in range(count):
            for m in range(mp_size):
                owner = s ^ d
                perm.append((s * mp_size + m, owner * mp_size + holder[(s + holder[m] - owner) % count]))
        return lax.ppermute(part, ("seq", "mp"), perm)

    arrived = [to_owner(part, d) for d, part in ((2, sum_2), (3, sum_3), (1, sum_1))]
    embedded_cols = (
        block_at(tiles, column_block(seq, mp), features, 1).astype(jnp.float32)
        + (sum_0 + sum(part.astype(jnp.float32) for part in arrived))
    ).astype(bf16)

    packages = call(
        functools.partial(project_body, count),
        [((capacity, 4 * heads * HEAD_WIDTH), bf16)] * count,
        (offsets, gain_slide[None, :], code, w_qkv.T, embedded_cols, *spread_mp(embedded_cols)),
        spaces=[smem] + [vmem] * 7,
    )
    packages = [packages[0]] + [swap(packages[d], "seq", d) for d in range(1, count)]
    return call(
        functools.partial(attend_body, count),
        [((heads * HEAD_WIDTH, ENCODER_SLOTS), bf16)],
        (offsets, *packages),
        spaces=[smem] + [vmem] * count,
        scratch=[pltpu.VMEM((ENCODER_SLOTS, 3 * heads * HEAD_WIDTH), bf16)],
    )[0].T


def on_device(*arrays):
    sizes = lax.axis_size("groups"), lax.axis_size("seq"), lax.axis_size("mp")
    if sizes == (2, 4, 4):
        return split_hidden_plan(*arrays)
    return gathered_plan(*arrays)


def solution(mesh):
    return jax.shard_map(
        on_device,
        mesh=mesh,
        in_specs=(
            P(("groups", "seq"), None),
            P(("groups", "seq")),
            P(("groups", "seq"), None),
            P(),
            P("seq", "mp"),
            P("seq", "mp"),
            P("mp", "seq"),
            P(),
            P(None, "mp"),
            P("mp"),
        ),
        out_specs=P(("groups", "seq"), "mp"),
        check_vma=False,
    )
```

```python
import functools

import jax
import jax.numpy as jnp
from jax import lax
from jax.experimental import pallas as pl
from jax.experimental.pallas import tpu as pltpu
from jax.sharding import PartitionSpec as P

D_ENC = 1536
HEAD_WIDTH = 64
DILATION_STEP = 8
ENCODER_SLOTS = 256


epsilon = 1e-05


def gather_seq(package):
    count = lax.axis_size("seq")
    if count & (count - 1) == 0 and count <= 4:
        return jnp.concatenate([package] + [swap(package, "seq", d) for d in range(1, count)])
    return lax.all_gather(package, "seq", axis=0, tiled=True)


def gathered_plan(tiles, counts, dest, gain_enc, w_gate, w_up, w_down, gain_slide, w_qkv, offsets):
    seq_count = lax.axis_size("seq")
    capacity = ENCODER_SLOTS // seq_count
    tile_rows = tiles.shape[0]
    target = dest[:, 0]
    live_rows = jnp.arange(tile_rows, dtype=jnp.int32) < counts[0]
    chosen = (
        (target[:, None] == jnp.arange(seq_count, dtype=jnp.int32)[None, :]) & live_rows[:, None]
    ).astype(jnp.int32)
    arrival = jnp.sum((jnp.cumsum(chosen, axis=0) - chosen) * chosen, axis=1)
    slot_index = jnp.where(live_rows, target * capacity + arrival, ENCODER_SLOTS)
    outgoing = (
        jnp.zeros((ENCODER_SLOTS, D_ENC), jnp.bfloat16).at[slot_index].set(tiles, mode="drop")
    )
    arrived = lax.all_to_all(outgoing, "seq", split_axis=0, concat_axis=0, tiled=True)
    arrived_f = arrived.astype(jnp.float32)
    inverse = lax.rsqrt(jnp.mean(arrived_f * arrived_f, axis=-1, keepdims=True) + epsilon)
    normed = (arrived_f * inverse * gain_enc).astype(jnp.bfloat16)

    def add_rows(portion):
        return jnp.dot(normed, portion, preferred_element_type=jnp.float32)

    gate_act = add_rows(lax.all_gather(w_gate, "seq", axis=0, tiled=True))
    up_act = add_rows(lax.all_gather(w_up, "seq", axis=0, tiled=True))
    hidden = (jax.nn.silu(gate_act) * up_act).astype(jnp.bfloat16)
    partial_out = jnp.dot(
        hidden,
        lax.all_gather(w_down, "seq", axis=1, tiled=True),
        preferred_element_type=jnp.float32,
    )
    share = lax.psum_scatter(partial_out, "mp", scatter_dimension=1, tiled=True)
    share_width = share.shape[1]
    own_cols = lax.dynamic_slice_in_dim(
        arrived_f, lax.axis_index("mp") * share_width, share_width, 1
    )
    embedded_cols = (own_cols + share).astype(jnp.bfloat16)
    embedded = lax.all_gather(embedded_cols, "mp", axis=1, tiled=True)
    return slide_layer(embedded, gain_slide, w_qkv, offsets)


def slide_layer(embedded, gain_slide, w_qkv, offsets):
    portion_f = embedded.astype(jnp.float32)
    accumulated = jnp.dot(
        (portion_f * gain_slide).astype(jnp.bfloat16), w_qkv, preferred_element_type=jnp.float32
    )
    accumulated, squares = (accumulated, jnp.sum(portion_f * portion_f, axis=1))
    projected = accumulated * lax.rsqrt(squares / D_ENC + epsilon)[:, None]
    qkv_act = projected.astype(jnp.bfloat16)
    local_head_output = offsets.shape[0]
    fields = qkv_act.reshape(ENCODER_SLOTS, local_head_output, 3, HEAD_WIDTH)
    query_rows = fields[:, :, 0, :]
    keys_local = fields[:, :, 1, :]
    values_local = fields[:, :, 2, :]
    scale_factor = HEAD_WIDTH ** (-0.5)
    row_selector = (jnp.arange(DILATION_STEP, dtype=jnp.int32)[None, :] == offsets[:, None]).astype(
        jnp.float32
    )
    selected_rows = ENCODER_SLOTS // DILATION_STEP

    def select_rows(slide_field):
        reshaped_rows = slide_field.astype(jnp.float32).reshape(
            selected_rows, DILATION_STEP, local_head_output, HEAD_WIDTH
        )
        return jnp.einsum("rdhe,hd->rhe", reshaped_rows, row_selector).astype(jnp.bfloat16)

    query_sel = select_rows(query_rows)
    package = jnp.concatenate([select_rows(keys_local), select_rows(values_local)], axis=2).reshape(
        selected_rows, local_head_output * 2 * HEAD_WIDTH
    )
    portion = gather_seq(package)
    parts_kv = portion.reshape(portion.shape[0], local_head_output, 2, HEAD_WIDTH)
    scores = (
        jnp.einsum(
            "qhe,khe->hqk", query_sel, parts_kv[:, :, 0, :], preferred_element_type=jnp.float32
        )
        * scale_factor
    )
    weights = jnp.exp(scores)
    numer = jnp.einsum(
        "hqk,khe->hqe",
        weights.astype(jnp.bfloat16),
        parts_kv[:, :, 1, :],
        preferred_element_type=jnp.float32,
    )
    remote_den = jnp.sum(weights, axis=-1)
    scores = (
        jnp.einsum("qhe,khe->hqk", query_rows, keys_local, preferred_element_type=jnp.float32)
        * scale_factor
    )
    weights = jnp.exp(scores)
    local_num = jnp.einsum(
        "hqk,khe->hqe",
        weights.astype(jnp.bfloat16),
        values_local,
        preferred_element_type=jnp.float32,
    )
    local_den = jnp.sum(weights, axis=-1)
    spread_num = jnp.einsum("hre,hd->hrde", numer, row_selector).reshape(
        local_head_output, ENCODER_SLOTS, HEAD_WIDTH
    )
    spread_den = jnp.einsum("hr,hd->hrd", remote_den, row_selector).reshape(
        local_head_output, ENCODER_SLOTS
    )
    result = (local_num + spread_num) / (local_den + spread_den)[..., None]
    return (
        jnp.transpose(result, (1, 0, 2))
        .reshape(ENCODER_SLOTS, local_head_output * HEAD_WIDTH)
        .astype(jnp.bfloat16)
    )


def swap(array, axis, distance):
    size = lax.axis_size(axis)
    return lax.ppermute(array, axis, [(i, i ^ distance) for i in range(size)])


def block_at(array, index, size, axis):
    return lax.dynamic_slice_in_dim(array, index * size, size, axis)


def call(body, outs, inputs, spaces=None, scratch=(), copies=0, megabytes=40):
    spaces = spaces or [pltpu.VMEM] * len(inputs)
    scratch = list(scratch)
    if copies:
        scratch.append(pltpu.SemaphoreType.DMA((copies,)))
    return pl.pallas_call(
        body,
        out_shape=[jax.ShapeDtypeStruct(shape, kind) for shape, kind in outs],
        in_specs=[pl.BlockSpec(memory_space=space) for space in spaces],
        out_specs=[pl.BlockSpec(memory_space=pltpu.VMEM)] * len(outs),
        scratch_shapes=scratch,
        compiler_params=pltpu.CompilerParams(vmem_limit_bytes=megabytes * 1024 * 1024),
    )(*inputs)


def at(index, size):
    return pl.ds(pl.multiple_of(index * size, size), size)


def place():
    return tuple(lax.axis_index(name) for name in ("seq", "mp", "groups"))


def column_block(seq, mp):
    step = jnp.where(mp == 2, seq + 1, seq + 3) & 3
    return jnp.where(mp < 2, seq ^ (2 * mp), step)


def column_user(seq, mp):
    step = jnp.where(mp == 2, seq + 3, seq + 1) & 3
    return jnp.where(mp < 2, seq ^ (2 * mp), step)


def cut_body(
    count, tiles, w_gate, w_up, w_down, next_out, second_out, third_out, kept, near, far, sems
):
    seq, mp, group = place()
    depth, units = w_gate.shape[0], w_gate.shape[1] // count
    half, features = depth // 2, near.shape[2]
    copies = []

    def copy(source, target, other=None):
        started = pltpu.make_async_copy(source, target, sems.at[len(copies)])
        if other is None:
            started.start()
        else:
            second = pltpu.make_async_copy(other, target, sems.at[len(copies)])
            pl.when(group == 0)(started.start)
            pl.when(group != 0)(second.start)
        copies.append(started)

    for d, target in ((1, next_out), (2, second_out), (3, third_out)):
        copy(tiles.at[:, at(mp, features)], target.at[:, pl.ds(0, features)])
        for i in range(2):
            span = pl.ds(i * half, half), at(seq ^ d, units)
            if d == 1:
                for k, weight in enumerate((w_gate, w_up)):
                    columns = pl.ds(features + (2 * i + k) * units, units)
                    copy(weight.at[span], target.at[:, columns])
            else:
                columns = pl.ds(features + i * units, units)
                copy(w_gate.at[span], target.at[:, columns], w_up.at[span])
    for i, weight in enumerate((w_gate, w_up)):
        copy(weight.at[:, at(seq, units)], kept.at[:, pl.ds(i * units, units)])
    for j in range(4):
        rows = at(column_user(seq, mp ^ j), units)
        copy(w_down.at[rows, :], (far if j >= 2 else near).at[j % 2])
    for started in copies:
        started.wait()


def restack_body(first, second, third, stacked, columns):
    features = stacked.shape[2]
    for i, package in enumerate((first, second, third)):
        stacked[i] = package[:, :features]
    columns[0] = second[:, features:]
    columns[1] = third[:, features:]


def code_body(capacity, counts, dest, dest_row, code):
    rows = dest_row.shape[1]
    later = lax.broadcasted_iota(jnp.int32, (rows, rows), 1)
    earlier = lax.broadcasted_iota(jnp.int32, (rows, rows), 0)
    same = (dest[...] == dest_row[...]) & (earlier < later)
    rank = jnp.sum(jnp.where(same, 1, 0), axis=0, keepdims=True)
    live = lax.broadcasted_iota(jnp.int32, (1, rows), 1) < counts[0]
    code[...] = jnp.where(live, dest_row[...] * capacity + rank, -1)


def hidden_body(
    count, gain, tiles, own, far, near, near_far, kept, next_in, columns, others, out, *scratch
):
    normed, weights, next_weights = scratch
    seq, mp, group = place()
    depth, units = weights.shape[1:]
    half = depth // 2
    rows, features = tiles.shape[0], own.shape[2]
    for i in range(2):
        span = pl.ds(i * half, half)
        for k in range(2):
            weights[2 * k, span, :] = columns[k, :, i * units : (i + 1) * units]
            weights[2 * k + 1, span, :] = others[k, :, i * units : (i + 1) * units]
        start = features + 2 * i * units
        next_weights[span, :] = next_in[:, start : start + 2 * units]

    def gated(d):
        if d == 0:
            pieces = [(tiles[:, pl.ds(q * depth, depth)], q) for q in range(count)]
        else:
            pieces = [(own[d - 1], mp), (far[d - 1], mp ^ 2)]
            pieces += [(near[d - 1], mp ^ 1), (near_far[d - 1], mp ^ 3)]
        values = [piece.astype(jnp.float32) for piece, _ in pieces]
        squares = sum(jnp.sum(v * v, axis=1, keepdims=True) for v in values)
        inverse = lax.rsqrt(squares * (1.0 / D_ENC) + epsilon)
        for v, (_, index) in zip(values, pieces):
            normed[d, index] = (v * inverse * gain[:, at(index, depth)]).astype(jnp.bfloat16)
        dot = functools.partial(jnp.dot, preferred_element_type=jnp.float32)
        both = dot(normed[d, seq], kept[...]) + dot(normed[d, seq ^ 1], next_weights[...])
        mine = dot(normed[d, seq ^ 2], weights[0]) + dot(normed[d, seq ^ 3], weights[2])
        other = dot(normed[d, seq ^ 2], weights[1]) + dot(normed[d, seq ^ 3], weights[3])
        gate_act = both[:, :units] + jnp.where(group == 0, mine, other)
        up_act = both[:, units:] + jnp.where(group == 0, other, mine)
        return (gate_act * jax.nn.sigmoid(gate_act) * up_act).astype(jnp.bfloat16)

    for d in range(count - 1, -1, -1):
        out[pl.ds(d * rows, rows), :] = gated(d)


def down_body(own, far, near, near_far, even, odd, *outs):
    rows = outs[0].shape[0]
    for i, out in enumerate(outs):
        total = 0.0
        pairs = ((own, even[0]), (near, odd[0]), (far, even[1]), (near_far, odd[1]))
        for piece, weights in pairs:
            total += jnp.dot(
                piece[pl.ds(i * rows, rows), :], weights, preferred_element_type=jnp.float32
            )
        out[...] = total.astype(out.dtype)


def project_body(count, offsets, gain, code, w_qkv_t, own, far, near, near_far, *outs):
    seq, mp, _ = place()
    features = own.shape[1]
    capacity = outs[0].shape[0]
    heads = offsets.shape[0]
    squares, total = 0.0, 0.0
    for j, piece in enumerate((own, near, far, near_far)):
        index = column_block(seq, mp ^ j)
        v = piece[...].astype(jnp.float32)
        squares += jnp.sum(v * v, axis=1, keepdims=True)
        scaled = (v * gain[:, at(index, features)]).astype(jnp.bfloat16)
        total += lax.dot_general(
            scaled,
            w_qkv_t[:, at(index, features)],
            (((1,), (1,)), ((), ())),
            preferred_element_type=jnp.float32,
        )
    projected = (total * lax.rsqrt(squares * (1.0 / D_ENC) + epsilon)).astype(jnp.bfloat16)
    codes = code[...]
    rows = codes.shape[1]

    def pick(wanted, array):
        chosen = jnp.where(codes == wanted, 1.0, 0.0).astype(jnp.bfloat16)
        return jnp.dot(chosen, array, preferred_element_type=jnp.float32).astype(jnp.bfloat16)

    spread = []
    per_block = capacity // DILATION_STEP
    index = lax.broadcasted_iota(jnp.int32, (count * per_block, rows), 0)
    for h in range(heads):
        wanted = (index // per_block) * capacity + (index % per_block) * DILATION_STEP + offsets[h]
        start = (3 * h + 1) * HEAD_WIDTH
        both = pick(wanted, projected[:, start : start + 2 * HEAD_WIDTH])
        spread.append(jnp.concatenate([both[:, :HEAD_WIDTH], both[:, HEAD_WIDTH:]], axis=0))
    width = projected.shape[1]
    beside = jnp.concatenate(spread, axis=1)
    slot = lax.broadcasted_iota(jnp.int32, (capacity, rows), 0)
    for d, out in enumerate(outs):
        out[:, :width] = pick((seq ^ d) * capacity + slot, projected)
        out[:, width:] = beside


def attend_body(count, offsets, *refs):
    packages, out, rows = refs[:count], refs[count], refs[count + 1]
    seq, _, _ = place()
    capacity = packages[0].shape[0]
    heads = offsets.shape[0]
    width = heads * 3 * HEAD_WIDTH
    for d, package in enumerate(packages):
        rows[at(seq ^ d, capacity), :] = package[:, :width]
    far = [package[:, width:] for package in packages]
    half = capacity // 2
    far_keys = jnp.concatenate([f[:half] for f in far], axis=0)
    far_values = jnp.concatenate([f[half:] for f in far], axis=0)
    residue = lax.broadcasted_iota(jnp.int32, (1, out.shape[1]), 1) % DILATION_STEP
    scale_factor = HEAD_WIDTH ** (-0.5)

    def branch(query, key, value, mask):
        scores = lax.dot_general(
            key, query, (((1,), (1,)), ((), ())), preferred_element_type=jnp.float32
        )
        weights = jnp.exp(scores * scale_factor)
        if mask is not None:
            weights = jnp.where(mask, weights, 0.0)
        numer = lax.dot_general(
            value,
            weights.astype(jnp.bfloat16),
            (((0,), (0,)), ((), ())),
            preferred_element_type=jnp.float32,
        )
        return numer, jnp.sum(weights, axis=0, keepdims=True)

    for h in range(heads):
        query, key, value = (
            rows[:, pl.ds((3 * h + i) * HEAD_WIDTH, HEAD_WIDTH)] for i in range(3)
        )
        span = slice(h * HEAD_WIDTH, (h + 1) * HEAD_WIDTH)
        near_num, near_den = branch(query, key, value, None)
        mask = residue == offsets[h]
        far_num, far_den = branch(query, far_keys[:, span], far_values[:, span], mask)
        out[span, :] = ((near_num + far_num) / (near_den + far_den)).astype(jnp.bfloat16)


def spread_mp(own, beside=None):
    far = swap(own, "mp", 2)
    relayed = far if beside is None else lax.optimization_barrier((far, beside))[0]
    return far, swap(own, "mp", 1), swap(relayed, "mp", 1)


def split_hidden_plan(
    tiles, counts, dest, gain_enc, w_gate, w_up, w_down, gain_slide, w_qkv, offsets
):
    count, mp_size = lax.axis_size("seq"), lax.axis_size("mp")
    seq, mp = lax.axis_index("seq"), lax.axis_index("mp")
    capacity = ENCODER_SLOTS // count
    tile_rows = tiles.shape[0]
    features = D_ENC // mp_size
    depth = w_gate.shape[0]
    units = w_gate.shape[1] // count
    heads = offsets.shape[0]
    bf16 = jnp.bfloat16
    vmem, smem = pltpu.VMEM, pltpu.SMEM

    *packages, kept, down_near, down_far = call(
        functools.partial(cut_body, count),
        [
            ((tile_rows, features + 4 * units), bf16),
            ((tile_rows, features + 2 * units), bf16),
            ((tile_rows, features + 2 * units), bf16),
            ((depth, 2 * units), bf16),
            ((2, units, features), bf16),
            ((2, units, features), bf16),
        ],
        (tiles, w_gate, w_up, w_down),
        spaces=[pltpu.HBM] * 4,
        copies=17,
        megabytes=57,
    )
    code = call(
        functools.partial(code_body, capacity),
        [((1, tile_rows), jnp.int32)],
        (counts, dest, dest.reshape(1, tile_rows)),
        spaces=[smem, vmem, vmem],
    )[0]

    packages = [swap(packages[d - 1], "seq", d) for d in range(1, count)]
    from_far = swap(down_far, "mp", 2)
    down_send = [jnp.stack([down_near[j], from_far[j]]) for j in range(2)]
    packages, down_send, code = lax.optimization_barrier((packages, down_send, code))
    own, columns = call(
        restack_body,
        [
            ((count - 1, tile_rows, features), bf16),
            ((count - 2, tile_rows, 2 * units), bf16),
        ],
        packages,
    )
    others = swap(columns, "groups", 1)
    down_send, _ = lax.optimization_barrier((down_send, own))
    down_in = []
    for j in range(2):
        perm = []
        for s in range(count):
            for m in range(mp_size):
                k = m ^ j
                user = (s ^ 2 * k) if k < 2 else (s + 2 * k - 5) % count
                perm.append((s * mp_size + m, user * mp_size + k))
        down_in.append(lax.ppermute(down_send[j], ("seq", "mp"), perm))
    spread = spread_mp(own, (others, down_in[0]))
    hidden = call(
        functools.partial(hidden_body, count),
        [((count * tile_rows, units), bf16)],
        (gain_enc[None, :], tiles, own, *spread, kept, packages[0], columns, others),
        scratch=[
            pltpu.VMEM((count, count, tile_rows, depth), bf16),
            pltpu.VMEM((4, depth, units), bf16),
            pltpu.VMEM((depth, 2 * units), bf16),
        ],
    )[0]
    sums = call(
        down_body,
        [((tile_rows, features), kind) for kind in (jnp.float32, bf16, bf16, bf16)],
        (hidden, *spread_mp(hidden), *down_in),
    )
    holder = [0, 2, 1, 3]

    def to_owner(part, d):
        perm = []
        for s in range(count):
            for m in range(mp_size):
                owner = s ^ d
                perm.append((s * mp_size + m, owner * mp_size + holder[(s + holder[m] - owner) % count]))
        return lax.ppermute(part, ("seq", "mp"), perm)

    arrived = [to_owner(sums[d], d) for d in (2, 3, 1)]
    embedded_cols = (
        block_at(tiles, column_block(seq, mp), features, 1).astype(jnp.float32)
        + (sums[0] + sum(part.astype(jnp.float32) for part in arrived))
    ).astype(bf16)

    packages = call(
        functools.partial(project_body, count),
        [((capacity, 4 * heads * HEAD_WIDTH), bf16)] * count,
        (offsets, gain_slide[None, :], code, w_qkv.T, embedded_cols, *spread_mp(embedded_cols)),
        spaces=[smem] + [vmem] * 7,
    )
    packages = [packages[0]] + [swap(packages[d], "seq", d) for d in range(1, count)]
    return call(
        functools.partial(attend_body, count),
        [((heads * HEAD_WIDTH, ENCODER_SLOTS), bf16)],
        (offsets, *packages),
        spaces=[smem] + [vmem] * count,
        scratch=[pltpu.VMEM((ENCODER_SLOTS, 3 * heads * HEAD_WIDTH), bf16)],
    )[0].T


def on_device(*arrays):
    sizes = lax.axis_size("groups"), lax.axis_size("seq"), lax.axis_size("mp")
    if sizes == (2, 4, 4):
        return split_hidden_plan(*arrays)
    return gathered_plan(*arrays)


def solution(mesh):
    return jax.shard_map(
        on_device,
        mesh=mesh,
        in_specs=(
            P(("groups", "seq"), None),
            P(("groups", "seq")),
            P(("groups", "seq"), None),
            P(),
            P("seq", "mp"),
            P("seq", "mp"),
            P("mp", "seq"),
            P(),
            P(None, "mp"),
            P("mp"),
        ),
        out_specs=P(("groups", "seq"), "mp"),
        check_vma=False,
    )
```

```python
import functools

import jax
import jax.numpy as jnp
from jax import lax
from jax.experimental import pallas as pl
from jax.experimental.pallas import tpu as pltpu
from jax.sharding import PartitionSpec as P

D_ENC = 1536
HEAD_WIDTH = 64
DILATION_STEP = 8
ENCODER_SLOTS = 256


epsilon = 1e-05


def gather_seq(package):
    count = lax.axis_size("seq")
    if count & (count - 1) == 0 and count <= 4:
        return jnp.concatenate([package] + [swap(package, "seq", d) for d in range(1, count)])
    return lax.all_gather(package, "seq", axis=0, tiled=True)


def gathered_plan(tiles, counts, dest, gain_enc, w_gate, w_up, w_down, gain_slide, w_qkv, offsets):
    seq_count = lax.axis_size("seq")
    capacity = ENCODER_SLOTS // seq_count
    tile_rows = tiles.shape[0]
    target = dest[:, 0]
    live_rows = jnp.arange(tile_rows, dtype=jnp.int32) < counts[0]
    chosen = (
        (target[:, None] == jnp.arange(seq_count, dtype=jnp.int32)[None, :]) & live_rows[:, None]
    ).astype(jnp.int32)
    arrival = jnp.sum((jnp.cumsum(chosen, axis=0) - chosen) * chosen, axis=1)
    slot_index = jnp.where(live_rows, target * capacity + arrival, ENCODER_SLOTS)
    outgoing = (
        jnp.zeros((ENCODER_SLOTS, D_ENC), jnp.bfloat16).at[slot_index].set(tiles, mode="drop")
    )
    arrived = lax.all_to_all(outgoing, "seq", split_axis=0, concat_axis=0, tiled=True)
    arrived_f = arrived.astype(jnp.float32)
    inverse = lax.rsqrt(jnp.mean(arrived_f * arrived_f, axis=-1, keepdims=True) + epsilon)
    normed = (arrived_f * inverse * gain_enc).astype(jnp.bfloat16)

    def add_rows(portion):
        return jnp.dot(normed, portion, preferred_element_type=jnp.float32)

    gate_act = add_rows(lax.all_gather(w_gate, "seq", axis=0, tiled=True))
    up_act = add_rows(lax.all_gather(w_up, "seq", axis=0, tiled=True))
    hidden = (jax.nn.silu(gate_act) * up_act).astype(jnp.bfloat16)
    partial_out = jnp.dot(
        hidden,
        lax.all_gather(w_down, "seq", axis=1, tiled=True),
        preferred_element_type=jnp.float32,
    )
    share = lax.psum_scatter(partial_out, "mp", scatter_dimension=1, tiled=True)
    share_width = share.shape[1]
    own_cols = lax.dynamic_slice_in_dim(
        arrived_f, lax.axis_index("mp") * share_width, share_width, 1
    )
    embedded_cols = (own_cols + share).astype(jnp.bfloat16)
    embedded = lax.all_gather(embedded_cols, "mp", axis=1, tiled=True)
    return slide_layer(embedded, gain_slide, w_qkv, offsets)


def slide_layer(embedded, gain_slide, w_qkv, offsets):
    portion_f = embedded.astype(jnp.float32)
    accumulated = jnp.dot(
        (portion_f * gain_slide).astype(jnp.bfloat16), w_qkv, preferred_element_type=jnp.float32
    )
    accumulated, squares = (accumulated, jnp.sum(portion_f * portion_f, axis=1))
    projected = accumulated * lax.rsqrt(squares / D_ENC + epsilon)[:, None]
    qkv_act = projected.astype(jnp.bfloat16)
    local_head_output = offsets.shape[0]
    fields = qkv_act.reshape(ENCODER_SLOTS, local_head_output, 3, HEAD_WIDTH)
    query_rows = fields[:, :, 0, :]
    keys_local = fields[:, :, 1, :]
    values_local = fields[:, :, 2, :]
    scale_factor = HEAD_WIDTH ** (-0.5)
    row_selector = (jnp.arange(DILATION_STEP, dtype=jnp.int32)[None, :] == offsets[:, None]).astype(
        jnp.float32
    )
    selected_rows = ENCODER_SLOTS // DILATION_STEP

    def select_rows(slide_field):
        reshaped_rows = slide_field.astype(jnp.float32).reshape(
            selected_rows, DILATION_STEP, local_head_output, HEAD_WIDTH
        )
        return jnp.einsum("rdhe,hd->rhe", reshaped_rows, row_selector).astype(jnp.bfloat16)

    query_sel = select_rows(query_rows)
    package = jnp.concatenate([select_rows(keys_local), select_rows(values_local)], axis=2).reshape(
        selected_rows, local_head_output * 2 * HEAD_WIDTH
    )
    portion = gather_seq(package)
    parts_kv = portion.reshape(portion.shape[0], local_head_output, 2, HEAD_WIDTH)
    scores = (
        jnp.einsum(
            "qhe,khe->hqk", query_sel, parts_kv[:, :, 0, :], preferred_element_type=jnp.float32
        )
        * scale_factor
    )
    weights = jnp.exp(scores)
    numer = jnp.einsum(
        "hqk,khe->hqe",
        weights.astype(jnp.bfloat16),
        parts_kv[:, :, 1, :],
        preferred_element_type=jnp.float32,
    )
    remote_den = jnp.sum(weights, axis=-1)
    scores = (
        jnp.einsum("qhe,khe->hqk", query_rows, keys_local, preferred_element_type=jnp.float32)
        * scale_factor
    )
    weights = jnp.exp(scores)
    local_num = jnp.einsum(
        "hqk,khe->hqe",
        weights.astype(jnp.bfloat16),
        values_local,
        preferred_element_type=jnp.float32,
    )
    local_den = jnp.sum(weights, axis=-1)
    spread_num = jnp.einsum("hre,hd->hrde", numer, row_selector).reshape(
        local_head_output, ENCODER_SLOTS, HEAD_WIDTH
    )
    spread_den = jnp.einsum("hr,hd->hrd", remote_den, row_selector).reshape(
        local_head_output, ENCODER_SLOTS
    )
    result = (local_num + spread_num) / (local_den + spread_den)[..., None]
    return (
        jnp.transpose(result, (1, 0, 2))
        .reshape(ENCODER_SLOTS, local_head_output * HEAD_WIDTH)
        .astype(jnp.bfloat16)
    )


def swap(array, axis, distance):
    size = lax.axis_size(axis)
    return lax.ppermute(array, axis, [(i, i ^ distance) for i in range(size)])


def block_at(array, index, size, axis):
    return lax.dynamic_slice_in_dim(array, index * size, size, axis)


def call(body, outs, inputs, spaces=None, scratch=(), copies=0, megabytes=40):
    spaces = spaces or [pltpu.VMEM] * len(inputs)
    scratch = list(scratch)
    if copies:
        scratch.append(pltpu.SemaphoreType.DMA((copies,)))
    return pl.pallas_call(
        body,
        out_shape=[jax.ShapeDtypeStruct(shape, kind) for shape, kind in outs],
        in_specs=[pl.BlockSpec(memory_space=space) for space in spaces],
        out_specs=[pl.BlockSpec(memory_space=pltpu.VMEM)] * len(outs),
        scratch_shapes=scratch,
        compiler_params=pltpu.CompilerParams(vmem_limit_bytes=megabytes * 1024 * 1024),
    )(*inputs)


def at(index, size):
    return pl.ds(pl.multiple_of(index * size, size), size)


def place():
    return tuple(lax.axis_index(name) for name in ("seq", "mp", "groups"))


def column_block(seq, mp):
    step = jnp.where(mp == 2, seq + 1, seq + 3) & 3
    return jnp.where(mp < 2, seq ^ (2 * mp), step)


def column_user(seq, mp):
    step = jnp.where(mp == 2, seq + 3, seq + 1) & 3
    return jnp.where(mp < 2, seq ^ (2 * mp), step)


def copier(sems, group):
    copies = []

    def copy(source, target, other=None):
        started = pltpu.make_async_copy(source, target, sems.at[len(copies)])
        if other is None:
            started.start()
        else:
            second = pltpu.make_async_copy(other, target, sems.at[len(copies)])
            pl.when(group == 0)(started.start)
            pl.when(group != 0)(second.start)
        copies.append(started)

    return copies, copy


def cut_first_body(count, tiles, w_gate, w_up, first_out, second_out, quarter, sems):
    seq, mp, group = place()
    copies, copy = copier(sems, group)
    half, units = w_gate.shape[0] // 2, w_gate.shape[1] // count
    features = quarter.shape[1]
    own_columns = tiles.at[:, at(mp, features)]
    for i in range(2):
        span = pl.ds(i * half, half), at(seq ^ 2, units)
        columns = pl.ds(features + i * units, units)
        copy(w_gate.at[span], second_out.at[:, columns], w_up.at[span])
        span = pl.ds(i * half, half), at(seq ^ 1, units)
        for k, weight in enumerate((w_gate, w_up)):
            columns = pl.ds(features + (2 * i + k) * units, units)
            copy(weight.at[span], first_out.at[:, columns])
    for target in (second_out.at[:, pl.ds(0, features)], first_out.at[:, pl.ds(0, features)]):
        copy(own_columns, target)
    copy(own_columns, quarter)
    for started in copies:
        started.wait()


def cut_second_body(count, w_gate, w_up, w_down, third_out, kept, near, far, sems):
    seq, mp, group = place()
    copies, copy = copier(sems, group)
    half, units = w_gate.shape[0] // 2, w_gate.shape[1] // count
    part = units // 2
    for j, target in ((2, far), (0, near)):
        rows = at(column_user(seq, mp ^ j) * 2 + group, part)
        copy(w_down.at[rows, :], target.at[pl.ds(0, part), :])
        rows = at(column_user(seq, mp ^ (j + 1)), units)
        copy(w_down.at[rows, :], target.at[pl.ds(part, units), :])
    for i in range(2):
        span = pl.ds(i * half, half), at(seq ^ 3, units)
        copy(w_gate.at[span], third_out.at[:, pl.ds(i * units, units)], w_up.at[span])
    for i, weight in enumerate((w_gate, w_up)):
        copy(weight.at[:, at(seq, units)], kept.at[:, pl.ds(i * units, units)])
    for started in copies:
        started.wait()


def restack_body(first, second, third, near, far, stacked, columns, even, odd):
    features = stacked.shape[2]
    stacked[0] = first[:, :features]
    stacked[1] = second[:, :features]
    stacked[2] = third[...]
    columns[...] = second[:, features:]
    for i, rows in enumerate((near, far)):
        even[i] = rows[: even.shape[1], :]
        odd[i] = rows[even.shape[1] :, :]


def code_body(capacity, counts, dest, dest_row, code):
    rows = dest_row.shape[1]
    later = lax.broadcasted_iota(jnp.int32, (rows, rows), 1)
    earlier = lax.broadcasted_iota(jnp.int32, (rows, rows), 0)
    same = (dest[...] == dest_row[...]) & (earlier < later)
    rank = jnp.sum(jnp.where(same, 1, 0), axis=0, keepdims=True)
    live = lax.broadcasted_iota(jnp.int32, (1, rows), 1) < counts[0]
    code[...] = jnp.where(live, dest_row[...] * capacity + rank, -1)


def hidden_body(
    count, gain, tiles, own, far, near, near_far, kept, next_in, *refs
):
    halves, (out, normed, weights, next_weights) = refs[:4], refs[4:]
    seq, mp, group = place()
    depth, units = weights.shape[1:]
    half = depth // 2
    rows = tiles.shape[0]
    for i, piece in enumerate(halves):
        weights[i, :half, :] = piece[:, :units]
        weights[i, half:, :] = piece[:, units:]
    for i in range(2):
        start = own.shape[2] + 2 * i * units
        next_weights[i * half : (i + 1) * half, :] = next_in[:, start : start + 2 * units]

    def gated(d):
        if d == 0:
            pieces = [(tiles[:, pl.ds(q * depth, depth)], q) for q in range(count)]
        else:
            pieces = [(own[d - 1], mp), (far[d - 1], mp ^ 2)]
            pieces += [(near[d - 1], mp ^ 1), (near_far[d - 1], mp ^ 3)]
        values = [piece.astype(jnp.float32) for piece, _ in pieces]
        squares = sum(jnp.sum(v * v, axis=1, keepdims=True) for v in values)
        inverse = lax.rsqrt(squares * (1.0 / D_ENC) + epsilon)
        for v, (_, index) in zip(values, pieces):
            normed[d, index] = (v * inverse * gain[:, at(index, depth)]).astype(jnp.bfloat16)
        dot = functools.partial(jnp.dot, preferred_element_type=jnp.float32)
        both = dot(normed[d, seq], kept[...]) + dot(normed[d, seq ^ 1], next_weights[...])
        mine = dot(normed[d, seq ^ 2], weights[0]) + dot(normed[d, seq ^ 3], weights[2])
        other = dot(normed[d, seq ^ 2], weights[1]) + dot(normed[d, seq ^ 3], weights[3])
        gate_act = both[:, :units] + jnp.where(group == 0, mine, other)
        up_act = both[:, units:] + jnp.where(group == 0, other, mine)
        return (gate_act * jax.nn.sigmoid(gate_act) * up_act).astype(jnp.bfloat16)

    for d in range(count - 1, -1, -1):
        out[pl.ds(d * rows, rows), :] = gated(d)


def down_body(own, far, near, near_far, even, even_other, odd, *outs):
    _, _, group = place()
    rows = outs[0].shape[0]
    weights = [None, odd[0], None, odd[1]]
    for j in range(2):
        mine, other = even[j], even_other[j]
        low, high = jnp.where(group == 0, mine, other), jnp.where(group == 0, other, mine)
        weights[2 * j] = jnp.concatenate([low, high], axis=0)
    for i, out in enumerate(outs):
        total = 0.0
        for j, piece in enumerate((own, near, far, near_far)):
            total += jnp.dot(
                piece[pl.ds(i * rows, rows), :], weights[j], preferred_element_type=jnp.float32
            )
        out[...] = total.astype(out.dtype)


def project_body(count, offsets, gain, code, w_qkv_t, own, far, near, near_far, *outs):
    seq, mp, _ = place()
    features = own.shape[1]
    capacity = outs[0].shape[0]
    heads = offsets.shape[0]
    squares, total = 0.0, 0.0
    for j, piece in enumerate((own, near, far, near_far)):
        index = column_block(seq, mp ^ j)
        v = piece[...].astype(jnp.float32)
        squares += jnp.sum(v * v, axis=1, keepdims=True)
        scaled = (v * gain[:, at(index, features)]).astype(jnp.bfloat16)
        total += lax.dot_general(
            scaled,
            w_qkv_t[:, at(index, features)],
            (((1,), (1,)), ((), ())),
            preferred_element_type=jnp.float32,
        )
    projected = (total * lax.rsqrt(squares * (1.0 / D_ENC) + epsilon)).astype(jnp.bfloat16)
    codes = code[...]
    rows = codes.shape[1]

    def pick(wanted, array):
        chosen = jnp.where(codes == wanted, 1.0, 0.0).astype(jnp.bfloat16)
        return jnp.dot(chosen, array, preferred_element_type=jnp.float32).astype(jnp.bfloat16)

    spread = []
    per_block = capacity // DILATION_STEP
    index = lax.broadcasted_iota(jnp.int32, (count * per_block, rows), 0)
    for h in range(heads):
        wanted = (index // per_block) * capacity + (index % per_block) * DILATION_STEP + offsets[h]
        start = (3 * h + 1) * HEAD_WIDTH
        both = pick(wanted, projected[:, start : start + 2 * HEAD_WIDTH])
        spread.append(jnp.concatenate([both[:, :HEAD_WIDTH], both[:, HEAD_WIDTH:]], axis=0))
    width = projected.shape[1]
    beside = jnp.concatenate(spread, axis=1)
    slot = lax.broadcasted_iota(jnp.int32, (capacity, rows), 0)
    for d, out in enumerate(outs):
        out[:, :width] = pick((seq ^ d) * capacity + slot, projected)
        out[:, width:] = beside


def attend_body(count, offsets, *refs):
    packages, out, rows = refs[:count], refs[count], refs[count + 1]
    seq, _, _ = place()
    capacity = packages[0].shape[0]
    heads = offsets.shape[0]
    width = heads * 3 * HEAD_WIDTH
    for d, package in enumerate(packages):
        rows[at(seq ^ d, capacity), :] = package[:, :width]
    far = [package[:, width:] for package in packages]
    half = capacity // 2
    far_keys = jnp.concatenate([f[:half] for f in far], axis=0)
    far_values = jnp.concatenate([f[half:] for f in far], axis=0)
    residue = lax.broadcasted_iota(jnp.int32, (1, out.shape[1]), 1) % DILATION_STEP
    scale_factor = HEAD_WIDTH ** (-0.5)

    def branch(query, key, value, mask):
        scores = lax.dot_general(
            key, query, (((1,), (1,)), ((), ())), preferred_element_type=jnp.float32
        )
        weights = jnp.exp(scores * scale_factor)
        if mask is not None:
            weights = jnp.where(mask, weights, 0.0)
        numer = lax.dot_general(
            value,
            weights.astype(jnp.bfloat16),
            (((0,), (0,)), ((), ())),
            preferred_element_type=jnp.float32,
        )
        return numer, jnp.sum(weights, axis=0, keepdims=True)

    for h in range(heads):
        query, key, value = (
            rows[:, pl.ds((3 * h + i) * HEAD_WIDTH, HEAD_WIDTH)] for i in range(3)
        )
        span = slice(h * HEAD_WIDTH, (h + 1) * HEAD_WIDTH)
        near_num, near_den = branch(query, key, value, None)
        mask = residue == offsets[h]
        far_num, far_den = branch(query, far_keys[:, span], far_values[:, span], mask)
        out[span, :] = ((near_num + far_num) / (near_den + far_den)).astype(jnp.bfloat16)


def spread_mp(own, beside=None):
    far = swap(own, "mp", 2)
    relayed = far if beside is None else lax.optimization_barrier((far, beside))[0]
    return far, swap(own, "mp", 1), swap(relayed, "mp", 1)


def split_hidden_plan(
    tiles, counts, dest, gain_enc, w_gate, w_up, w_down, gain_slide, w_qkv, offsets
):
    count, mp_size = lax.axis_size("seq"), lax.axis_size("mp")
    seq, mp = lax.axis_index("seq"), lax.axis_index("mp")
    capacity = ENCODER_SLOTS // count
    tile_rows = tiles.shape[0]
    features = D_ENC // mp_size
    depth = w_gate.shape[0]
    units = w_gate.shape[1] // count
    heads = offsets.shape[0]
    bf16 = jnp.bfloat16
    vmem, smem = pltpu.VMEM, pltpu.SMEM

    first_out, second_out, quarter = call(
        functools.partial(cut_first_body, count),
        [
            ((tile_rows, features + 4 * units), bf16),
            ((tile_rows, features + 2 * units), bf16),
            ((tile_rows, features), bf16),
        ],
        (tiles, w_gate, w_up),
        spaces=[pltpu.HBM] * 3,
        copies=9,
        megabytes=57,
    )
    third_out, kept, down_near, down_far = call(
        functools.partial(cut_second_body, count),
        [
            ((tile_rows, 2 * units), bf16),
            ((depth, 2 * units), bf16),
            ((3 * units // 2, features), bf16),
            ((3 * units // 2, features), bf16),
        ],
        (w_gate, w_up, w_down),
        spaces=[pltpu.HBM] * 3,
        copies=8,
        megabytes=57,
    )
    code = call(
        functools.partial(code_body, capacity),
        [((1, tile_rows), jnp.int32)],
        (counts, dest, dest.reshape(1, tile_rows)),
        spaces=[smem, vmem, vmem],
    )[0]

    arrived = swap(first_out, "seq", 1), swap(second_out, "seq", 2), swap(quarter, "seq", 3)
    from_far = swap(down_far, "mp", 2)
    arrived, from_far, code = lax.optimization_barrier((arrived, from_far, code))
    own, columns, *down_send = call(
        restack_body,
        [
            ((count - 1, tile_rows, features), bf16),
            ((tile_rows, 2 * units), bf16),
            ((2, units // 2, features), bf16),
            ((2, units, features), bf16),
        ],
        (*arrived, down_near, from_far),
    )
    third_out, _ = lax.optimization_barrier((third_out, own))
    third, others, far, near = lax.optimization_barrier(
        (
            swap(third_out, "seq", 3),
            swap(columns, "groups", 1),
            swap(own, "mp", 2),
            swap(own, "mp", 1),
        )
    )
    halves = columns, others, third, swap(third, "groups", 1)
    spread = far, near, swap(far, "mp", 1)
    down_send, _ = lax.optimization_barrier((down_send, far))
    parts = []
    for j in range(2):
        perm = []
        for s in range(count):
            for m in range(mp_size):
                k = m ^ j
                user = (s ^ 2 * k) if k < 2 else (s + 2 * k - 5) % count
                perm.append((s * mp_size + m, user * mp_size + k))
        parts.append(lax.ppermute(down_send[j], ("seq", "mp"), perm))
    (tiles, *spread), parts[0] = lax.optimization_barrier(((tiles, *spread), parts[0]))
    hidden = call(
        functools.partial(hidden_body, count),
        [((count * tile_rows, units), bf16)],
        (gain_enc[None, :], tiles, own, *spread, kept, arrived[0], *halves),
        scratch=[
            pltpu.VMEM((count, count, tile_rows, depth), bf16),
            pltpu.VMEM((4, depth, units), bf16),
            pltpu.VMEM((depth, 2 * units), bf16),
        ],
    )[0]
    even, odd = parts
    even_other = swap(even, "groups", 1)
    sums = call(
        down_body,
        [((tile_rows, features), kind) for kind in (jnp.float32, bf16, bf16, bf16)],
        (hidden, *spread_mp(hidden, even_other), even, even_other, odd),
    )
    holder = [0, 2, 1, 3]

    def to_owner(part, d):
        perm = []
        for s in range(count):
            for m in range(mp_size):
                owner = s ^ d
                perm.append((s * mp_size + m, owner * mp_size + holder[(s + holder[m] - owner) % count]))
        return lax.ppermute(part, ("seq", "mp"), perm)

    arrived = [to_owner(sums[d], d) for d in (2, 3, 1)]
    embedded_cols = (
        block_at(tiles, column_block(seq, mp), features, 1).astype(jnp.float32)
        + (sums[0] + sum(part.astype(jnp.float32) for part in arrived))
    ).astype(bf16)

    packages = call(
        functools.partial(project_body, count),
        [((capacity, 4 * heads * HEAD_WIDTH), bf16)] * count,
        (offsets, gain_slide[None, :], code, w_qkv.T, embedded_cols, *spread_mp(embedded_cols)),
        spaces=[smem] + [vmem] * 7,
    )
    packages = [packages[0]] + [swap(packages[d], "seq", d) for d in range(1, count)]
    return call(
        functools.partial(attend_body, count),
        [((heads * HEAD_WIDTH, ENCODER_SLOTS), bf16)],
        (offsets, *packages),
        spaces=[smem] + [vmem] * count,
        scratch=[pltpu.VMEM((ENCODER_SLOTS, 3 * heads * HEAD_WIDTH), bf16)],
    )[0].T


def on_device(*arrays):
    sizes = lax.axis_size("groups"), lax.axis_size("seq"), lax.axis_size("mp")
    if sizes == (2, 4, 4):
        return split_hidden_plan(*arrays)
    return gathered_plan(*arrays)


def solution(mesh):
    return jax.shard_map(
        on_device,
        mesh=mesh,
        in_specs=(
            P(("groups", "seq"), None),
            P(("groups", "seq")),
            P(("groups", "seq"), None),
            P(),
            P("seq", "mp"),
            P("seq", "mp"),
            P("mp", "seq"),
            P(),
            P(None, "mp"),
            P("mp"),
        ),
        out_specs=P(("groups", "seq"), "mp"),
        check_vma=False,
    )
```

```python
import functools

import jax
import jax.numpy as jnp
from jax import lax
from jax.experimental import pallas as pl
from jax.experimental.pallas import tpu as pltpu
from jax.sharding import PartitionSpec as P

D_ENC = 1536
HEAD_WIDTH = 64
DILATION_STEP = 8
ENCODER_SLOTS = 256


epsilon = 1e-05


def gather_seq(package):
    count = lax.axis_size("seq")
    if count & (count - 1) == 0 and count <= 4:
        return jnp.concatenate([package] + [swap(package, "seq", d) for d in range(1, count)])
    return lax.all_gather(package, "seq", axis=0, tiled=True)


def gathered_plan(tiles, counts, dest, gain_enc, w_gate, w_up, w_down, gain_slide, w_qkv, offsets):
    seq_count = lax.axis_size("seq")
    capacity = ENCODER_SLOTS // seq_count
    tile_rows = tiles.shape[0]
    target = dest[:, 0]
    live_rows = jnp.arange(tile_rows, dtype=jnp.int32) < counts[0]
    chosen = (
        (target[:, None] == jnp.arange(seq_count, dtype=jnp.int32)[None, :]) & live_rows[:, None]
    ).astype(jnp.int32)
    arrival = jnp.sum((jnp.cumsum(chosen, axis=0) - chosen) * chosen, axis=1)
    slot_index = jnp.where(live_rows, target * capacity + arrival, ENCODER_SLOTS)
    outgoing = (
        jnp.zeros((ENCODER_SLOTS, D_ENC), jnp.bfloat16).at[slot_index].set(tiles, mode="drop")
    )
    arrived = lax.all_to_all(outgoing, "seq", split_axis=0, concat_axis=0, tiled=True)
    arrived_f = arrived.astype(jnp.float32)
    inverse = lax.rsqrt(jnp.mean(arrived_f * arrived_f, axis=-1, keepdims=True) + epsilon)
    normed = (arrived_f * inverse * gain_enc).astype(jnp.bfloat16)

    def add_rows(portion):
        return jnp.dot(normed, portion, preferred_element_type=jnp.float32)

    gate_act = add_rows(lax.all_gather(w_gate, "seq", axis=0, tiled=True))
    up_act = add_rows(lax.all_gather(w_up, "seq", axis=0, tiled=True))
    hidden = (jax.nn.silu(gate_act) * up_act).astype(jnp.bfloat16)
    partial_out = jnp.dot(
        hidden,
        lax.all_gather(w_down, "seq", axis=1, tiled=True),
        preferred_element_type=jnp.float32,
    )
    share = lax.psum_scatter(partial_out, "mp", scatter_dimension=1, tiled=True)
    share_width = share.shape[1]
    own_cols = lax.dynamic_slice_in_dim(
        arrived_f, lax.axis_index("mp") * share_width, share_width, 1
    )
    embedded_cols = (own_cols + share).astype(jnp.bfloat16)
    embedded = lax.all_gather(embedded_cols, "mp", axis=1, tiled=True)
    return slide_layer(embedded, gain_slide, w_qkv, offsets)


def slide_layer(embedded, gain_slide, w_qkv, offsets):
    portion_f = embedded.astype(jnp.float32)
    accumulated = jnp.dot(
        (portion_f * gain_slide).astype(jnp.bfloat16), w_qkv, preferred_element_type=jnp.float32
    )
    accumulated, squares = (accumulated, jnp.sum(portion_f * portion_f, axis=1))
    projected = accumulated * lax.rsqrt(squares / D_ENC + epsilon)[:, None]
    qkv_act = projected.astype(jnp.bfloat16)
    local_head_output = offsets.shape[0]
    fields = qkv_act.reshape(ENCODER_SLOTS, local_head_output, 3, HEAD_WIDTH)
    query_rows = fields[:, :, 0, :]
    keys_local = fields[:, :, 1, :]
    values_local = fields[:, :, 2, :]
    scale_factor = HEAD_WIDTH ** (-0.5)
    row_selector = (jnp.arange(DILATION_STEP, dtype=jnp.int32)[None, :] == offsets[:, None]).astype(
        jnp.float32
    )
    selected_rows = ENCODER_SLOTS // DILATION_STEP

    def select_rows(slide_field):
        reshaped_rows = slide_field.astype(jnp.float32).reshape(
            selected_rows, DILATION_STEP, local_head_output, HEAD_WIDTH
        )
        return jnp.einsum("rdhe,hd->rhe", reshaped_rows, row_selector).astype(jnp.bfloat16)

    query_sel = select_rows(query_rows)
    package = jnp.concatenate([select_rows(keys_local), select_rows(values_local)], axis=2).reshape(
        selected_rows, local_head_output * 2 * HEAD_WIDTH
    )
    portion = gather_seq(package)
    parts_kv = portion.reshape(portion.shape[0], local_head_output, 2, HEAD_WIDTH)
    scores = (
        jnp.einsum(
            "qhe,khe->hqk", query_sel, parts_kv[:, :, 0, :], preferred_element_type=jnp.float32
        )
        * scale_factor
    )
    weights = jnp.exp(scores)
    numer = jnp.einsum(
        "hqk,khe->hqe",
        weights.astype(jnp.bfloat16),
        parts_kv[:, :, 1, :],
        preferred_element_type=jnp.float32,
    )
    remote_den = jnp.sum(weights, axis=-1)
    scores = (
        jnp.einsum("qhe,khe->hqk", query_rows, keys_local, preferred_element_type=jnp.float32)
        * scale_factor
    )
    weights = jnp.exp(scores)
    local_num = jnp.einsum(
        "hqk,khe->hqe",
        weights.astype(jnp.bfloat16),
        values_local,
        preferred_element_type=jnp.float32,
    )
    local_den = jnp.sum(weights, axis=-1)
    spread_num = jnp.einsum("hre,hd->hrde", numer, row_selector).reshape(
        local_head_output, ENCODER_SLOTS, HEAD_WIDTH
    )
    spread_den = jnp.einsum("hr,hd->hrd", remote_den, row_selector).reshape(
        local_head_output, ENCODER_SLOTS
    )
    result = (local_num + spread_num) / (local_den + spread_den)[..., None]
    return (
        jnp.transpose(result, (1, 0, 2))
        .reshape(ENCODER_SLOTS, local_head_output * HEAD_WIDTH)
        .astype(jnp.bfloat16)
    )


def swap(array, axis, distance):
    size = lax.axis_size(axis)
    return lax.ppermute(array, axis, [(i, i ^ distance) for i in range(size)])


def block_at(array, index, size, axis):
    return lax.dynamic_slice_in_dim(array, index * size, size, axis)


def call(body, outs, inputs, spaces=None, scratch=(), copies=0, megabytes=40):
    spaces = spaces or [pltpu.VMEM] * len(inputs)
    scratch = list(scratch)
    if copies:
        scratch.append(pltpu.SemaphoreType.DMA((copies,)))
    return pl.pallas_call(
        body,
        out_shape=[jax.ShapeDtypeStruct(shape, kind) for shape, kind in outs],
        in_specs=[pl.BlockSpec(memory_space=space) for space in spaces],
        out_specs=[pl.BlockSpec(memory_space=pltpu.VMEM)] * len(outs),
        scratch_shapes=scratch,
        compiler_params=pltpu.CompilerParams(vmem_limit_bytes=megabytes * 1024 * 1024),
    )(*inputs)


def at(index, size):
    return pl.ds(pl.multiple_of(index * size, size), size)


def place():
    return tuple(lax.axis_index(name) for name in ("seq", "mp", "groups"))


def column_block(seq, mp):
    step = jnp.where(mp == 2, seq + 1, seq + 3) & 3
    return jnp.where(mp < 2, seq ^ (2 * mp), step)


def column_user(seq, mp):
    step = jnp.where(mp == 2, seq + 3, seq + 1) & 3
    return jnp.where(mp < 2, seq ^ (2 * mp), step)


def copier(sems, group):
    copies, used = [], [0]

    def copy(source, target, other=None):
        started = pltpu.make_async_copy(source, target, sems.at[used[0]])
        if other is None:
            started.start()
        else:
            second = pltpu.make_async_copy(other, target, sems.at[used[0]])
            pl.when(group == 0)(started.start)
            pl.when(group != 0)(second.start)
        copies.append(started)
        used[0] += 1

    return copies, copy


def cut_first_body(
    count, tiles, w_gate, w_up, gain, first_out, second_out, quarter, normed, held, sems
):
    seq, mp, group = place()
    copies, copy = copier(sems, group)
    half, units = w_gate.shape[0] // 2, w_gate.shape[1] // count
    features = quarter.shape[1]
    copy(tiles, held)
    for i in range(2):
        span = pl.ds(i * half, half), at(seq ^ 2, units)
        columns = pl.ds(features + i * units, units)
        copy(w_gate.at[span], second_out.at[:, columns], w_up.at[span])
        span = pl.ds(i * half, half), at(seq ^ 1, units)
        for k, weight in enumerate((w_gate, w_up)):
            columns = pl.ds(features + (2 * i + k) * units, units)
            copy(weight.at[span], first_out.at[:, columns])
    copies.pop(0).wait()
    values = held[...].astype(jnp.float32)
    squares = jnp.sum(values * values, axis=1, keepdims=True)
    inverse = lax.rsqrt(squares * (1.0 / D_ENC) + epsilon)
    normed[...] = (values * inverse * gain[...]).astype(jnp.bfloat16)
    columns = at(mp, features)
    values = held[:, columns].astype(jnp.float32)
    own_columns = (values * inverse * gain[:, columns]).astype(jnp.bfloat16)
    second_out[:, :features] = own_columns
    first_out[:, :features] = own_columns
    quarter[...] = own_columns
    for started in copies:
        started.wait()


def cut_second_body(count, w_gate, w_up, w_down, third_out, kept, near, far, sems):
    seq, mp, group = place()
    copies, copy = copier(sems, group)
    half, units = w_gate.shape[0] // 2, w_gate.shape[1] // count
    part = units // 2
    for j, target in ((2, far), (0, near)):
        rows = at(column_user(seq, mp ^ j) * 2 + group, part)
        copy(w_down.at[rows, :], target.at[pl.ds(0, part), :])
        rows = at(column_user(seq, mp ^ (j + 1)), units)
        copy(w_down.at[rows, :], target.at[pl.ds(part, units), :])
    for i in range(2):
        span = pl.ds(i * half, half), at(seq ^ 3, units)
        copy(w_gate.at[span], third_out.at[:, pl.ds(i * units, units)], w_up.at[span])
    for i, weight in enumerate((w_gate, w_up)):
        copy(weight.at[:, at(seq, units)], kept.at[:, pl.ds(i * units, units)])
    for started in copies:
        started.wait()


def restack_body(first, second, third, stacked, columns):
    features = stacked.shape[2]
    stacked[0] = first[:, :features]
    stacked[1] = second[:, :features]
    stacked[2] = third[...]
    columns[...] = second[:, features:]


def pair_body(near, far, even, odd):
    for i, rows in enumerate((near, far)):
        even[i] = rows[: even.shape[1], :]
        odd[i] = rows[even.shape[1] :, :]


def routes_body(count, counts, offsets, dest, dest_row, routes):
    seq, _, _ = place()
    rows = dest_row.shape[1]
    capacity = ENCODER_SLOTS // count
    later = lax.broadcasted_iota(jnp.int32, (rows, rows), 1)
    earlier = lax.broadcasted_iota(jnp.int32, (rows, rows), 0)
    same = (dest[...] == dest_row[...]) & (earlier < later)
    rank = jnp.sum(jnp.where(same, 1, 0), axis=0, keepdims=True)
    live = lax.broadcasted_iota(jnp.int32, (1, rows), 1) < counts[0]
    codes = jnp.where(live, dest_row[...] * capacity + rank, -1)

    def chosen(wanted):
        return jnp.where(codes == wanted, 1.0, 0.0).astype(jnp.bfloat16)

    slot = lax.broadcasted_iota(jnp.int32, (capacity, rows), 0)
    for d in range(count):
        routes[pl.ds(d * capacity, capacity), :] = chosen((seq ^ d) * capacity + slot)
    per_block = capacity // DILATION_STEP
    spread = count * per_block
    index = lax.broadcasted_iota(jnp.int32, (spread, rows), 0)
    wanted = (index // per_block) * capacity + (index % per_block) * DILATION_STEP
    for h in range(offsets.shape[0]):
        routes[pl.ds(count * capacity + h * spread, spread), :] = chosen(wanted + offsets[h])


def hidden_body(count, normed, own, far, near, near_far, kept, next_in, *refs):
    (second, second_other, third, third_other), (out, weights) = refs[:4], refs[4:]
    seq, mp, group = place()
    depth, units = weights.shape[2:]
    half = depth // 2
    rows = normed.shape[0]
    for k in range(2):
        weights[k, seq] = kept[:, k * units : (k + 1) * units]
        for i in range(2):
            start = own.shape[2] + (2 * i + k) * units
            span = pl.ds(i * half, half)
            weights[k, seq ^ 1, span, :] = next_in[:, start : start + units]
    for d, mine, other in ((2, second, second_other), (3, third, third_other)):
        for i in range(2):
            span, columns = pl.ds(i * half, half), slice(i * units, (i + 1) * units)
            weights[group, seq ^ d, span, :] = mine[:, columns]
            weights[1 - group, seq ^ d, span, :] = other[:, columns]
    for d in range(count):
        if d == 0:
            pieces = [(normed[:, q * depth : (q + 1) * depth], q) for q in range(count)]
        else:
            pieces = [(own[d - 1], mp), (near[d - 1], mp ^ 1)]
            pieces += [(far[d - 1], mp ^ 2), (near_far[d - 1], mp ^ 3)]
        gate_act, up_act = (
            sum(
                jnp.dot(piece, weights[k, index], preferred_element_type=jnp.float32)
                for piece, index in pieces
            )
            for k in range(2)
        )
        gated = gate_act * jax.nn.sigmoid(gate_act) * up_act
        out[pl.ds(d * rows, rows), :] = gated.astype(jnp.bfloat16)


def down_body(own, far, near, near_far, even, even_other, odd, *outs):
    _, _, group = place()
    rows = outs[0].shape[0]
    weights = [None, odd[0], None, odd[1]]
    for j in range(2):
        mine, other = even[j], even_other[j]
        low, high = jnp.where(group == 0, mine, other), jnp.where(group == 0, other, mine)
        weights[2 * j] = jnp.concatenate([low, high], axis=0)
    for i, out in enumerate(outs):
        total = 0.0
        for j, piece in enumerate((own, near, far, near_far)):
            total += jnp.dot(
                piece[pl.ds(i * rows, rows), :], weights[j], preferred_element_type=jnp.float32
            )
        out[...] = total.astype(out.dtype)


def project_body(count, gain, routes, w_qkv_t, own, far, near, near_far, *outs):
    seq, mp, _ = place()
    features = own.shape[1]
    capacity = outs[0].shape[0]
    heads = w_qkv_t.shape[0] // (3 * HEAD_WIDTH)
    squares, total = 0.0, 0.0
    for j, piece in enumerate((own, near, far, near_far)):
        index = column_block(seq, mp ^ j)
        v = piece[...].astype(jnp.float32)
        squares += jnp.sum(v * v, axis=1, keepdims=True)
        scaled = (v * gain[:, at(index, features)]).astype(jnp.bfloat16)
        total += lax.dot_general(
            scaled,
            w_qkv_t[:, at(index, features)],
            (((1,), (1,)), ((), ())),
            preferred_element_type=jnp.float32,
        )
    projected = (total * lax.rsqrt(squares * (1.0 / D_ENC) + epsilon)).astype(jnp.bfloat16)
    routed = jnp.dot(routes[...], projected, preferred_element_type=jnp.float32)
    routed = routed.astype(jnp.bfloat16)
    width = projected.shape[1]
    spread = capacity // 2
    for d, out in enumerate(outs):
        out[:, :width] = routed[d * capacity : (d + 1) * capacity]
    for h in range(heads):
        first = count * capacity + h * spread
        for i in range(2):
            start = (3 * h + 1 + i) * HEAD_WIDTH
            piece = routed[first : first + spread, start : start + HEAD_WIDTH]
            for out in outs:
                span = slice(width + h * HEAD_WIDTH, width + (h + 1) * HEAD_WIDTH)
                out[i * spread : (i + 1) * spread, span] = piece


def attend_body(count, offsets, *refs):
    packages, out, rows = refs[:count], refs[count], refs[count + 1]
    seq, _, _ = place()
    capacity = packages[0].shape[0]
    heads = offsets.shape[0]
    width = heads * 3 * HEAD_WIDTH
    for d, package in enumerate(packages):
        rows[at(seq ^ d, capacity), :] = package[:, :width]
    far = [package[:, width:] for package in packages]
    half = capacity // 2
    far_keys = jnp.concatenate([f[:half] for f in far], axis=0)
    far_values = jnp.concatenate([f[half:] for f in far], axis=0)
    residue = lax.broadcasted_iota(jnp.int32, (1, out.shape[1]), 1) % DILATION_STEP
    scale_factor = HEAD_WIDTH ** (-0.5)

    local = out.shape[1]
    for h in range(heads):
        query, key, value = (
            rows[:, pl.ds((3 * h + i) * HEAD_WIDTH, HEAD_WIDTH)] for i in range(3)
        )
        span = slice(h * HEAD_WIDTH, (h + 1) * HEAD_WIDTH)
        keys = jnp.concatenate([key, far_keys[:, span]], axis=0)
        values = jnp.concatenate([value, far_values[:, span]], axis=0)
        scores = lax.dot_general(
            keys, query, (((1,), (1,)), ((), ())), preferred_element_type=jnp.float32
        )
        weights = jnp.exp(scores * scale_factor)
        dilated = jnp.where(residue == offsets[h], weights[local:], 0.0)
        weights = jnp.concatenate([weights[:local], dilated], axis=0)
        numer = lax.dot_general(
            values,
            weights.astype(jnp.bfloat16),
            (((0,), (0,)), ((), ())),
            preferred_element_type=jnp.float32,
        )
        denom = jnp.sum(weights, axis=0, keepdims=True)
        out[span, :] = (numer / denom).astype(jnp.bfloat16)


def spread_mp(own, beside=None):
    far = swap(own, "mp", 2)
    relayed = far if beside is None else lax.optimization_barrier((far, beside))[0]
    return far, swap(own, "mp", 1), swap(relayed, "mp", 1)


def split_hidden_plan(
    tiles, counts, dest, gain_enc, w_gate, w_up, w_down, gain_slide, w_qkv, offsets
):
    count, mp_size = lax.axis_size("seq"), lax.axis_size("mp")
    seq, mp = lax.axis_index("seq"), lax.axis_index("mp")
    capacity = ENCODER_SLOTS // count
    tile_rows = tiles.shape[0]
    features = D_ENC // mp_size
    depth = w_gate.shape[0]
    units = w_gate.shape[1] // count
    heads = offsets.shape[0]
    bf16 = jnp.bfloat16
    vmem, smem = pltpu.VMEM, pltpu.SMEM

    first_out, second_out, quarter, normed = call(
        functools.partial(cut_first_body, count),
        [
            ((tile_rows, features + 4 * units), bf16),
            ((tile_rows, features + 2 * units), bf16),
            ((tile_rows, features), bf16),
            ((tile_rows, D_ENC), bf16),
        ],
        (tiles, w_gate, w_up, gain_enc[None, :]),
        spaces=[pltpu.HBM] * 3 + [vmem],
        copies=7,
        scratch=[pltpu.VMEM((tile_rows, D_ENC), bf16)],
        megabytes=57,
    )
    third_out, kept, down_near, down_far = call(
        functools.partial(cut_second_body, count),
        [
            ((tile_rows, 2 * units), bf16),
            ((depth, 2 * units), bf16),
            ((3 * units // 2, features), bf16),
            ((3 * units // 2, features), bf16),
        ],
        (w_gate, w_up, w_down),
        spaces=[pltpu.HBM] * 3,
        copies=8,
        megabytes=57,
    )
    routes = call(
        functools.partial(routes_body, count),
        [((ENCODER_SLOTS + heads * ENCODER_SLOTS // DILATION_STEP, tile_rows), bf16)],
        (counts, offsets, dest, dest.reshape(1, tile_rows)),
        spaces=[smem, smem, vmem, vmem],
    )[0]

    arrived = swap(first_out, "seq", 1), swap(second_out, "seq", 2), swap(quarter, "seq", 3)
    from_far = swap(down_far, "mp", 2)
    arrived, from_far, routes = lax.optimization_barrier((arrived, from_far, routes))
    own, columns = call(
        restack_body,
        [
            ((count - 1, tile_rows, features), bf16),
            ((tile_rows, 2 * units), bf16),
        ],
        arrived,
    )
    third_out, down_near, _ = lax.optimization_barrier((third_out, down_near, own))
    down_send = call(
        pair_body,
        [((2, units // 2, features), bf16), ((2, units, features), bf16)],
        (down_near, from_far),
    )
    third, others, far, near, down_send = lax.optimization_barrier(
        (
            swap(third_out, "seq", 3),
            swap(columns, "groups", 1),
            swap(own, "mp", 2),
            swap(own, "mp", 1),
            down_send,
        )
    )
    halves = columns, others, third, swap(third, "groups", 1)
    spread = far, near, swap(far, "mp", 1)
    parts = []
    for j in range(2):
        perm = []
        for s in range(count):
            for m in range(mp_size):
                k = m ^ j
                user = (s ^ 2 * k) if k < 2 else (s + 2 * k - 5) % count
                perm.append((s * mp_size + m, user * mp_size + k))
        parts.append(lax.ppermute(down_send[j], ("seq", "mp"), perm))
    spread, parts[0] = lax.optimization_barrier((spread, parts[0]))
    hidden = call(
        functools.partial(hidden_body, count),
        [((count * tile_rows, units), bf16)],
        (normed, own, *spread, kept, arrived[0], *halves),
        scratch=[
            pltpu.VMEM((2, count, depth, units), bf16),
        ],
    )[0]
    even, odd = parts
    even_other = swap(even, "groups", 1)
    sums = call(
        down_body,
        [((tile_rows, features), kind) for kind in (jnp.float32, bf16, bf16, bf16)],
        (hidden, *spread_mp(hidden, even_other), even, even_other, odd),
    )
    holder = [0, 2, 1, 3]

    def to_owner(part, d):
        perm = []
        for s in range(count):
            for m in range(mp_size):
                owner = s ^ d
                perm.append((s * mp_size + m, owner * mp_size + holder[(s + holder[m] - owner) % count]))
        return lax.ppermute(part, ("seq", "mp"), perm)

    arrived = [to_owner(sums[d], d) for d in (2, 3, 1)]
    embedded_cols = (
        block_at(tiles, column_block(seq, mp), features, 1).astype(jnp.float32)
        + (sums[0] + sum(part.astype(jnp.float32) for part in arrived))
    ).astype(bf16)

    packages = call(
        functools.partial(project_body, count),
        [((capacity, 4 * heads * HEAD_WIDTH), bf16)] * count,
        (gain_slide[None, :], routes, w_qkv.T, embedded_cols, *spread_mp(embedded_cols)),
    )
    packages = [packages[0]] + [swap(packages[d], "seq", d) for d in range(1, count)]
    return call(
        functools.partial(attend_body, count),
        [((heads * HEAD_WIDTH, ENCODER_SLOTS), bf16)],
        (offsets, *packages),
        spaces=[smem] + [vmem] * count,
        scratch=[pltpu.VMEM((ENCODER_SLOTS, 3 * heads * HEAD_WIDTH), bf16)],
    )[0].T


def on_device(*arrays):
    sizes = lax.axis_size("groups"), lax.axis_size("seq"), lax.axis_size("mp")
    if sizes == (2, 4, 4):
        return split_hidden_plan(*arrays)
    return gathered_plan(*arrays)


def solution(mesh):
    return jax.shard_map(
        on_device,
        mesh=mesh,
        in_specs=(
            P(("groups", "seq"), None),
            P(("groups", "seq")),
            P(("groups", "seq"), None),
            P(),
            P("seq", "mp"),
            P("seq", "mp"),
            P("mp", "seq"),
            P(),
            P(None, "mp"),
            P("mp"),
        ),
        out_specs=P(("groups", "seq"), "mp"),
        check_vma=False,
    )
```

```python
import functools

import jax
import jax.numpy as jnp
from jax import lax
from jax.experimental import pallas as pl
from jax.experimental.pallas import tpu as pltpu
from jax.sharding import PartitionSpec as P

D_ENC = 1536
HEAD_WIDTH = 64
DILATION_STEP = 8
ENCODER_SLOTS = 256


epsilon = 1e-05


def gather_seq(package):
    count = lax.axis_size("seq")
    if count & (count - 1) == 0 and count <= 4:
        return jnp.concatenate([package] + [swap(package, "seq", d) for d in range(1, count)])
    return lax.all_gather(package, "seq", axis=0, tiled=True)


def gathered_plan(tiles, counts, dest, gain_enc, w_gate, w_up, w_down, gain_slide, w_qkv, offsets):
    seq_count = lax.axis_size("seq")
    capacity = ENCODER_SLOTS // seq_count
    tile_rows = tiles.shape[0]
    target = dest[:, 0]
    live_rows = jnp.arange(tile_rows, dtype=jnp.int32) < counts[0]
    chosen = (
        (target[:, None] == jnp.arange(seq_count, dtype=jnp.int32)[None, :]) & live_rows[:, None]
    ).astype(jnp.int32)
    arrival = jnp.sum((jnp.cumsum(chosen, axis=0) - chosen) * chosen, axis=1)
    slot_index = jnp.where(live_rows, target * capacity + arrival, ENCODER_SLOTS)
    outgoing = (
        jnp.zeros((ENCODER_SLOTS, D_ENC), jnp.bfloat16).at[slot_index].set(tiles, mode="drop")
    )
    arrived = lax.all_to_all(outgoing, "seq", split_axis=0, concat_axis=0, tiled=True)
    arrived_f = arrived.astype(jnp.float32)
    inverse = lax.rsqrt(jnp.mean(arrived_f * arrived_f, axis=-1, keepdims=True) + epsilon)
    normed = (arrived_f * inverse * gain_enc).astype(jnp.bfloat16)

    def add_rows(portion):
        return jnp.dot(normed, portion, preferred_element_type=jnp.float32)

    gate_act = add_rows(lax.all_gather(w_gate, "seq", axis=0, tiled=True))
    up_act = add_rows(lax.all_gather(w_up, "seq", axis=0, tiled=True))
    hidden = (jax.nn.silu(gate_act) * up_act).astype(jnp.bfloat16)
    partial_out = jnp.dot(
        hidden,
        lax.all_gather(w_down, "seq", axis=1, tiled=True),
        preferred_element_type=jnp.float32,
    )
    share = lax.psum_scatter(partial_out, "mp", scatter_dimension=1, tiled=True)
    share_width = share.shape[1]
    own_cols = lax.dynamic_slice_in_dim(
        arrived_f, lax.axis_index("mp") * share_width, share_width, 1
    )
    embedded_cols = (own_cols + share).astype(jnp.bfloat16)
    embedded = lax.all_gather(embedded_cols, "mp", axis=1, tiled=True)
    return slide_layer(embedded, gain_slide, w_qkv, offsets)


def slide_layer(embedded, gain_slide, w_qkv, offsets):
    portion_f = embedded.astype(jnp.float32)
    accumulated = jnp.dot(
        (portion_f * gain_slide).astype(jnp.bfloat16), w_qkv, preferred_element_type=jnp.float32
    )
    accumulated, squares = (accumulated, jnp.sum(portion_f * portion_f, axis=1))
    projected = accumulated * lax.rsqrt(squares / D_ENC + epsilon)[:, None]
    qkv_act = projected.astype(jnp.bfloat16)
    local_head_output = offsets.shape[0]
    fields = qkv_act.reshape(ENCODER_SLOTS, local_head_output, 3, HEAD_WIDTH)
    query_rows = fields[:, :, 0, :]
    keys_local = fields[:, :, 1, :]
    values_local = fields[:, :, 2, :]
    scale_factor = HEAD_WIDTH ** (-0.5)
    row_selector = (jnp.arange(DILATION_STEP, dtype=jnp.int32)[None, :] == offsets[:, None]).astype(
        jnp.float32
    )
    selected_rows = ENCODER_SLOTS // DILATION_STEP

    def select_rows(slide_field):
        reshaped_rows = slide_field.astype(jnp.float32).reshape(
            selected_rows, DILATION_STEP, local_head_output, HEAD_WIDTH
        )
        return jnp.einsum("rdhe,hd->rhe", reshaped_rows, row_selector).astype(jnp.bfloat16)

    query_sel = select_rows(query_rows)
    package = jnp.concatenate([select_rows(keys_local), select_rows(values_local)], axis=2).reshape(
        selected_rows, local_head_output * 2 * HEAD_WIDTH
    )
    portion = gather_seq(package)
    parts_kv = portion.reshape(portion.shape[0], local_head_output, 2, HEAD_WIDTH)
    scores = (
        jnp.einsum(
            "qhe,khe->hqk", query_sel, parts_kv[:, :, 0, :], preferred_element_type=jnp.float32
        )
        * scale_factor
    )
    weights = jnp.exp(scores)
    numer = jnp.einsum(
        "hqk,khe->hqe",
        weights.astype(jnp.bfloat16),
        parts_kv[:, :, 1, :],
        preferred_element_type=jnp.float32,
    )
    remote_den = jnp.sum(weights, axis=-1)
    scores = (
        jnp.einsum("qhe,khe->hqk", query_rows, keys_local, preferred_element_type=jnp.float32)
        * scale_factor
    )
    weights = jnp.exp(scores)
    local_num = jnp.einsum(
        "hqk,khe->hqe",
        weights.astype(jnp.bfloat16),
        values_local,
        preferred_element_type=jnp.float32,
    )
    local_den = jnp.sum(weights, axis=-1)
    spread_num = jnp.einsum("hre,hd->hrde", numer, row_selector).reshape(
        local_head_output, ENCODER_SLOTS, HEAD_WIDTH
    )
    spread_den = jnp.einsum("hr,hd->hrd", remote_den, row_selector).reshape(
        local_head_output, ENCODER_SLOTS
    )
    result = (local_num + spread_num) / (local_den + spread_den)[..., None]
    return (
        jnp.transpose(result, (1, 0, 2))
        .reshape(ENCODER_SLOTS, local_head_output * HEAD_WIDTH)
        .astype(jnp.bfloat16)
    )


def swap(array, axis, distance):
    size = lax.axis_size(axis)
    return lax.ppermute(array, axis, [(i, i ^ distance) for i in range(size)])


def block_at(array, index, size, axis):
    return lax.dynamic_slice_in_dim(array, index * size, size, axis)


def call(body, outs, inputs, spaces=None, scratch=(), copies=0, megabytes=40):
    spaces = spaces or [pltpu.VMEM] * len(inputs)
    scratch = list(scratch)
    if copies:
        scratch.append(pltpu.SemaphoreType.DMA((copies,)))
    return pl.pallas_call(
        body,
        out_shape=[jax.ShapeDtypeStruct(shape, kind) for shape, kind in outs],
        in_specs=[pl.BlockSpec(memory_space=space) for space in spaces],
        out_specs=[pl.BlockSpec(memory_space=pltpu.VMEM)] * len(outs),
        scratch_shapes=scratch,
        compiler_params=pltpu.CompilerParams(vmem_limit_bytes=megabytes * 1024 * 1024),
    )(*inputs)


def at(index, size):
    return pl.ds(pl.multiple_of(index * size, size), size)


def place():
    return tuple(lax.axis_index(name) for name in ("seq", "mp", "groups"))


def column_block(seq, mp):
    step = jnp.where(mp == 2, seq + 1, seq + 3) & 3
    return jnp.where(mp < 2, seq ^ (2 * mp), step)


def column_user(seq, mp):
    step = jnp.where(mp == 2, seq + 3, seq + 1) & 3
    return jnp.where(mp < 2, seq ^ (2 * mp), step)


def copier(sems, group):
    copies, used = [], [0]

    def copy(source, target, other=None):
        started = pltpu.make_async_copy(source, target, sems.at[used[0]])
        if other is None:
            started.start()
        else:
            second = pltpu.make_async_copy(other, target, sems.at[used[0]])
            pl.when(group == 0)(started.start)
            pl.when(group != 0)(second.start)
        copies.append(started)
        used[0] += 1

    return copies, copy


def normalise(rows, part, gain):
    values = rows[...].astype(jnp.float32)
    squares = jnp.sum(values * values, axis=1, keepdims=True)
    inverse = lax.rsqrt(squares * (1.0 / D_ENC) + epsilon)
    return (part.astype(jnp.float32) * inverse * gain[None, :]).astype(jnp.bfloat16)


def cut_first_body(
    count, tiles, w_gate, w_up, gain, first_out, second_out, quarter, held, sems
):
    seq, mp, group = place()
    copies, copy = copier(sems, group)
    half, units = w_gate.shape[0] // 2, w_gate.shape[1] // count
    features = quarter.shape[1]
    copy(tiles, held)
    for i in range(2):
        span = pl.ds(i * half, half), at(seq ^ 2, units)
        columns = pl.ds(features + i * units, units)
        copy(w_gate.at[span], second_out.at[:, columns], w_up.at[span])
        span = pl.ds(i * half, half), at(seq ^ 1, units)
        for k, weight in enumerate((w_gate, w_up)):
            columns = pl.ds(features + (2 * i + k) * units, units)
            copy(weight.at[span], first_out.at[:, columns])
    copies.pop(0).wait()
    columns = at(mp, features)
    own_columns = normalise(held, held[:, columns], gain[columns])
    second_out[:, :features] = own_columns
    first_out[:, :features] = own_columns
    quarter[...] = own_columns
    for started in copies:
        started.wait()


def cut_second_body(
    count, tiles, w_gate, w_up, w_down, gain, third_out, kept, near, far, normed, residual, held, sems
):
    seq, mp, group = place()
    copies, copy = copier(sems, group)
    half, units = w_gate.shape[0] // 2, w_gate.shape[1] // count
    copy(tiles, held)
    part = units // 2
    for j, target in ((2, far), (0, near)):
        rows = at(column_user(seq, mp ^ j) * 2 + group, part)
        copy(w_down.at[rows, :], target.at[pl.ds(0, part), :])
        rows = at(column_user(seq, mp ^ (j + 1)), units)
        copy(w_down.at[rows, :], target.at[pl.ds(part, units), :])
    for i in range(2):
        span = pl.ds(i * half, half), at(seq ^ 3, units)
        copy(w_gate.at[span], third_out.at[:, pl.ds(i * units, units)], w_up.at[span])
    for i, weight in enumerate((w_gate, w_up)):
        copy(weight.at[:, at(seq, units)], kept.at[:, pl.ds(i * units, units)])
    copies.pop(0).wait()
    normed[...] = normalise(held, held[...], gain[...])
    residual[...] = held[:, at(column_block(seq, mp), residual.shape[1])]
    for started in copies:
        started.wait()


def restack_body(first, second, third, stacked, columns):
    features = stacked.shape[2]
    stacked[0] = first[:, :features]
    stacked[1] = second[:, :features]
    stacked[2] = third[...]
    columns[...] = second[:, features:]


def pair_body(near, far, even, odd):
    for i, rows in enumerate((near, far)):
        even[i] = rows[: even.shape[1], :]
        odd[i] = rows[even.shape[1] :, :]


def routes_body(count, counts, offsets, dest, dest_row, routes):
    seq, _, _ = place()
    rows = dest_row.shape[1]
    capacity = ENCODER_SLOTS // count
    later = lax.broadcasted_iota(jnp.int32, (rows, rows), 1)
    earlier = lax.broadcasted_iota(jnp.int32, (rows, rows), 0)
    same = (dest[...] == dest_row[...]) & (earlier < later)
    rank = jnp.sum(jnp.where(same, 1, 0), axis=0, keepdims=True)
    live = lax.broadcasted_iota(jnp.int32, (1, rows), 1) < counts[0]
    codes = jnp.where(live, dest_row[...] * capacity + rank, -1)

    def chosen(wanted):
        return jnp.where(codes == wanted, 1.0, 0.0).astype(jnp.bfloat16)

    slot = lax.broadcasted_iota(jnp.int32, (capacity, rows), 0)
    for d in range(count):
        routes[pl.ds(d * capacity, capacity), :] = chosen((seq ^ d) * capacity + slot)
    per_block = capacity // DILATION_STEP
    spread = count * per_block
    index = lax.broadcasted_iota(jnp.int32, (spread, rows), 0)
    wanted = (index // per_block) * capacity + (index % per_block) * DILATION_STEP
    for h in range(offsets.shape[0]):
        routes[pl.ds(count * capacity + h * spread, spread), :] = chosen(wanted + offsets[h])


def hidden_body(count, normed, own, far, near, near_far, kept, next_in, *refs):
    (second, second_other, third, third_other), (out, weights) = refs[:4], refs[4:]
    seq, mp, group = place()
    depth, units = weights.shape[2:]
    half = depth // 2
    rows = normed.shape[0]
    for k in range(2):
        weights[k, seq] = kept[:, k * units : (k + 1) * units]
        for i in range(2):
            start = own.shape[2] + (2 * i + k) * units
            span = pl.ds(i * half, half)
            weights[k, seq ^ 1, span, :] = next_in[:, start : start + units]
    for d, mine, other in ((2, second, second_other), (3, third, third_other)):
        for i in range(2):
            span, columns = pl.ds(i * half, half), slice(i * units, (i + 1) * units)
            weights[group, seq ^ d, span, :] = mine[:, columns]
            weights[1 - group, seq ^ d, span, :] = other[:, columns]
    for d in range(count):
        if d == 0:
            pieces = [(normed[:, q * depth : (q + 1) * depth], q) for q in range(count)]
        else:
            pieces = [(own[d - 1], mp), (near[d - 1], mp ^ 1)]
            pieces += [(far[d - 1], mp ^ 2), (near_far[d - 1], mp ^ 3)]
        gate_act, up_act = (
            sum(
                jnp.dot(piece, weights[k, index], preferred_element_type=jnp.float32)
                for piece, index in pieces
            )
            for k in range(2)
        )
        gated = gate_act * jax.nn.sigmoid(gate_act) * up_act
        out[pl.ds(d * rows, rows), :] = gated.astype(jnp.bfloat16)


def down_body(residual, own, far, near, near_far, even, even_other, odd, *outs):
    _, _, group = place()
    rows = outs[0].shape[0]
    weights = [None, odd[0], None, odd[1]]
    for j in range(2):
        mine, other = even[j], even_other[j]
        low, high = jnp.where(group == 0, mine, other), jnp.where(group == 0, other, mine)
        weights[2 * j] = jnp.concatenate([low, high], axis=0)
    for i, out in enumerate(outs):
        total = residual[...].astype(jnp.float32) if i == 0 else 0.0
        for j, piece in enumerate((own, near, far, near_far)):
            total += jnp.dot(
                piece[pl.ds(i * rows, rows), :], weights[j], preferred_element_type=jnp.float32
            )
        out[...] = total.astype(out.dtype)


def sum_body(own, *refs):
    parts, out = refs[:-1], refs[-1]
    total = own[...] + sum(part[...].astype(jnp.float32) for part in parts)
    out[...] = total.astype(out.dtype)


def project_body(count, gain, routes, w_qkv_t, own, far, near, near_far, *outs):
    seq, mp, _ = place()
    features = own.shape[1]
    capacity = outs[0].shape[0]
    heads = w_qkv_t.shape[0] // (3 * HEAD_WIDTH)
    squares, total = 0.0, 0.0
    for j, piece in enumerate((own, near, far, near_far)):
        index = column_block(seq, mp ^ j)
        v = piece[...].astype(jnp.float32)
        squares += jnp.sum(v * v, axis=1, keepdims=True)
        scaled = (v * gain[:, at(index, features)]).astype(jnp.bfloat16)
        total += lax.dot_general(
            scaled,
            w_qkv_t[:, at(index, features)],
            (((1,), (1,)), ((), ())),
            preferred_element_type=jnp.float32,
        )
    projected = (total * lax.rsqrt(squares * (1.0 / D_ENC) + epsilon)).astype(jnp.bfloat16)
    routed = jnp.dot(routes[...], projected, preferred_element_type=jnp.float32)
    routed = routed.astype(jnp.bfloat16)
    width = projected.shape[1]
    spread = capacity // 2
    for d, out in enumerate(outs):
        out[:, :width] = routed[d * capacity : (d + 1) * capacity]
    for h in range(heads):
        first = count * capacity + h * spread
        for i in range(2):
            start = (3 * h + 1 + i) * HEAD_WIDTH
            piece = routed[first : first + spread, start : start + HEAD_WIDTH]
            for out in outs:
                span = slice(width + h * HEAD_WIDTH, width + (h + 1) * HEAD_WIDTH)
                out[i * spread : (i + 1) * spread, span] = piece


def attend_body(count, offsets, *refs):
    packages, out, rows = refs[:count], refs[count], refs[count + 1]
    seq, _, _ = place()
    capacity = packages[0].shape[0]
    heads = offsets.shape[0]
    width = heads * 3 * HEAD_WIDTH
    for d, package in enumerate(packages):
        rows[at(seq ^ d, capacity), :] = package[:, :width]
    far = [package[:, width:] for package in packages]
    half = capacity // 2
    far_keys = jnp.concatenate([f[:half] for f in far], axis=0)
    far_values = jnp.concatenate([f[half:] for f in far], axis=0)
    residue = lax.broadcasted_iota(jnp.int32, (1, out.shape[1]), 1) % DILATION_STEP
    scale_factor = HEAD_WIDTH ** (-0.5)

    local = out.shape[1]
    for h in range(heads):
        query, key, value = (
            rows[:, pl.ds((3 * h + i) * HEAD_WIDTH, HEAD_WIDTH)] for i in range(3)
        )
        span = slice(h * HEAD_WIDTH, (h + 1) * HEAD_WIDTH)
        keys = jnp.concatenate([key, far_keys[:, span]], axis=0)
        values = jnp.concatenate([value, far_values[:, span]], axis=0)
        scores = lax.dot_general(
            keys, query, (((1,), (1,)), ((), ())), preferred_element_type=jnp.float32
        )
        weights = jnp.exp(scores * scale_factor)
        dilated = jnp.where(residue == offsets[h], weights[local:], 0.0)
        weights = jnp.concatenate([weights[:local], dilated], axis=0)
        numer = lax.dot_general(
            values,
            weights.astype(jnp.bfloat16),
            (((0,), (0,)), ((), ())),
            preferred_element_type=jnp.float32,
        )
        denom = jnp.sum(weights, axis=0, keepdims=True)
        out[span, :] = (numer / denom).astype(jnp.bfloat16)


def spread_mp(own, beside=None):
    far = swap(own, "mp", 2)
    relayed = far if beside is None else lax.optimization_barrier((far, beside))[0]
    return far, swap(own, "mp", 1), swap(relayed, "mp", 1)


def split_hidden_plan(
    tiles, counts, dest, gain_enc, w_gate, w_up, w_down, gain_slide, w_qkv, offsets
):
    count, mp_size = lax.axis_size("seq"), lax.axis_size("mp")
    seq, mp = lax.axis_index("seq"), lax.axis_index("mp")
    capacity = ENCODER_SLOTS // count
    tile_rows = tiles.shape[0]
    features = D_ENC // mp_size
    depth = w_gate.shape[0]
    units = w_gate.shape[1] // count
    heads = offsets.shape[0]
    bf16 = jnp.bfloat16
    vmem, smem = pltpu.VMEM, pltpu.SMEM

    first_out, second_out, quarter = call(
        functools.partial(cut_first_body, count),
        [
            ((tile_rows, features + 4 * units), bf16),
            ((tile_rows, features + 2 * units), bf16),
            ((tile_rows, features), bf16),
        ],
        (tiles, w_gate, w_up, gain_enc),
        spaces=[pltpu.HBM] * 3 + [vmem],
        copies=7,
        scratch=[pltpu.VMEM((tile_rows, D_ENC), bf16)],
        megabytes=57,
    )
    third_out, kept, down_near, down_far, normed, residual = call(
        functools.partial(cut_second_body, count),
        [
            ((tile_rows, 2 * units), bf16),
            ((depth, 2 * units), bf16),
            ((3 * units // 2, features), bf16),
            ((3 * units // 2, features), bf16),
            ((tile_rows, D_ENC), bf16),
            ((tile_rows, features), bf16),
        ],
        (tiles, w_gate, w_up, w_down, gain_enc),
        spaces=[pltpu.HBM] * 4 + [vmem],
        scratch=[pltpu.VMEM((tile_rows, D_ENC), bf16)],
        copies=9,
        megabytes=57,
    )
    routes = call(
        functools.partial(routes_body, count),
        [((ENCODER_SLOTS + heads * ENCODER_SLOTS // DILATION_STEP, tile_rows), bf16)],
        (counts, offsets, dest, dest.reshape(1, tile_rows)),
        spaces=[smem, smem, vmem, vmem],
    )[0]

    second_in, third_in = swap(second_out, "seq", 2), swap(quarter, "seq", 3)
    arrived = swap(first_out, "seq", 1), second_in, third_in
    from_far = swap(down_far, "mp", 2)
    arrived, from_far, routes = lax.optimization_barrier((arrived, from_far, routes))
    own, columns = call(
        restack_body,
        [
            ((count - 1, tile_rows, features), bf16),
            ((tile_rows, 2 * units), bf16),
        ],
        arrived,
    )
    third_out, down_near, _ = lax.optimization_barrier((third_out, down_near, own))
    down_send = call(
        pair_body,
        [((2, units // 2, features), bf16), ((2, units, features), bf16)],
        (down_near, from_far),
    )
    third, others, far, near, down_send = lax.optimization_barrier(
        (
            swap(third_out, "seq", 3),
            swap(columns, "groups", 1),
            swap(own, "mp", 2),
            swap(own, "mp", 1),
            down_send,
        )
    )
    halves = columns, others, third, swap(third, "groups", 1)
    spread = far, near, swap(far, "mp", 1)
    parts = []
    for j in range(2):
        perm = []
        for s in range(count):
            for m in range(mp_size):
                k = m ^ j
                user = (s ^ 2 * k) if k < 2 else (s + 2 * k - 5) % count
                perm.append((s * mp_size + m, user * mp_size + k))
        parts.append(lax.ppermute(down_send[j], ("seq", "mp"), perm))
    spread, parts[0] = lax.optimization_barrier((spread, parts[0]))
    hidden = call(
        functools.partial(hidden_body, count),
        [((count * tile_rows, units), bf16)],
        (normed, own, *spread, kept, arrived[0], *halves),
        scratch=[
            pltpu.VMEM((2, count, depth, units), bf16),
        ],
    )[0]
    even, odd = parts
    even_other = swap(even, "groups", 1)
    sums = call(
        down_body,
        [((tile_rows, features), kind) for kind in (jnp.float32, bf16, bf16, bf16)],
        (residual, hidden, *spread_mp(hidden, even_other), even, even_other, odd),
    )
    holder = [0, 2, 1, 3]

    def to_owner(part, d):
        perm = []
        for s in range(count):
            for m in range(mp_size):
                owner = s ^ d
                perm.append((s * mp_size + m, owner * mp_size + holder[(s + holder[m] - owner) % count]))
        return lax.ppermute(part, ("seq", "mp"), perm)

    arrived = [to_owner(sums[d], d) for d in (2, 3, 1)]
    embedded_cols = call(
        sum_body, [((tile_rows, features), bf16)], (sums[0], *arrived)
    )[0]

    packages = call(
        functools.partial(project_body, count),
        [((capacity, 4 * heads * HEAD_WIDTH), bf16)] * count,
        (gain_slide[None, :], routes, w_qkv.T, embedded_cols, *spread_mp(embedded_cols)),
    )
    packages = [packages[0]] + [swap(packages[d], "seq", d) for d in range(1, count)]
    return call(
        functools.partial(attend_body, count),
        [((heads * HEAD_WIDTH, ENCODER_SLOTS), bf16)],
        (offsets, *packages),
        spaces=[smem] + [vmem] * count,
        scratch=[pltpu.VMEM((ENCODER_SLOTS, 3 * heads * HEAD_WIDTH), bf16)],
    )[0].T


def on_device(*arrays):
    sizes = lax.axis_size("groups"), lax.axis_size("seq"), lax.axis_size("mp")
    if sizes == (2, 4, 4):
        return split_hidden_plan(*arrays)
    return gathered_plan(*arrays)


def solution(mesh):
    return jax.shard_map(
        on_device,
        mesh=mesh,
        in_specs=(
            P(("groups", "seq"), None),
            P(("groups", "seq")),
            P(("groups", "seq"), None),
            P(),
            P("seq", "mp"),
            P("seq", "mp"),
            P("mp", "seq"),
            P(),
            P(None, "mp"),
            P("mp"),
        ),
        out_specs=P(("groups", "seq"), "mp"),
        check_vma=False,
    )
```

```python
import functools

import jax
import jax.numpy as jnp
from jax import lax
from jax.experimental import pallas as pl
from jax.experimental.pallas import tpu as pltpu
from jax.sharding import PartitionSpec as P

D_ENC = 1536
HEAD_WIDTH = 64
DILATION_STEP = 8
ENCODER_SLOTS = 256
ORDER = (2, 3, 1, 0)


epsilon = 1e-05


def gather_seq(package):
    count = lax.axis_size("seq")
    if count & (count - 1) == 0 and count <= 4:
        return jnp.concatenate([package] + [swap(package, "seq", d) for d in range(1, count)])
    return lax.all_gather(package, "seq", axis=0, tiled=True)


def gathered_plan(tiles, counts, dest, gain_enc, w_gate, w_up, w_down, gain_slide, w_qkv, offsets):
    seq_count = lax.axis_size("seq")
    capacity = ENCODER_SLOTS // seq_count
    tile_rows = tiles.shape[0]
    target = dest[:, 0]
    live_rows = jnp.arange(tile_rows, dtype=jnp.int32) < counts[0]
    chosen = (
        (target[:, None] == jnp.arange(seq_count, dtype=jnp.int32)[None, :]) & live_rows[:, None]
    ).astype(jnp.int32)
    arrival = jnp.sum((jnp.cumsum(chosen, axis=0) - chosen) * chosen, axis=1)
    slot_index = jnp.where(live_rows, target * capacity + arrival, ENCODER_SLOTS)
    outgoing = (
        jnp.zeros((ENCODER_SLOTS, D_ENC), jnp.bfloat16).at[slot_index].set(tiles, mode="drop")
    )
    arrived = lax.all_to_all(outgoing, "seq", split_axis=0, concat_axis=0, tiled=True)
    arrived_f = arrived.astype(jnp.float32)
    inverse = lax.rsqrt(jnp.mean(arrived_f * arrived_f, axis=-1, keepdims=True) + epsilon)
    normed = (arrived_f * inverse * gain_enc).astype(jnp.bfloat16)

    def add_rows(portion):
        return jnp.dot(normed, portion, preferred_element_type=jnp.float32)

    gate_act = add_rows(lax.all_gather(w_gate, "seq", axis=0, tiled=True))
    up_act = add_rows(lax.all_gather(w_up, "seq", axis=0, tiled=True))
    hidden = (jax.nn.silu(gate_act) * up_act).astype(jnp.bfloat16)
    partial_out = jnp.dot(
        hidden,
        lax.all_gather(w_down, "seq", axis=1, tiled=True),
        preferred_element_type=jnp.float32,
    )
    share = lax.psum_scatter(partial_out, "mp", scatter_dimension=1, tiled=True)
    share_width = share.shape[1]
    own_cols = lax.dynamic_slice_in_dim(
        arrived_f, lax.axis_index("mp") * share_width, share_width, 1
    )
    embedded_cols = (own_cols + share).astype(jnp.bfloat16)
    embedded = lax.all_gather(embedded_cols, "mp", axis=1, tiled=True)
    return slide_layer(embedded, gain_slide, w_qkv, offsets)


def slide_layer(embedded, gain_slide, w_qkv, offsets):
    portion_f = embedded.astype(jnp.float32)
    accumulated = jnp.dot(
        (portion_f * gain_slide).astype(jnp.bfloat16), w_qkv, preferred_element_type=jnp.float32
    )
    accumulated, squares = (accumulated, jnp.sum(portion_f * portion_f, axis=1))
    projected = accumulated * lax.rsqrt(squares / D_ENC + epsilon)[:, None]
    qkv_act = projected.astype(jnp.bfloat16)
    local_head_output = offsets.shape[0]
    fields = qkv_act.reshape(ENCODER_SLOTS, local_head_output, 3, HEAD_WIDTH)
    query_rows = fields[:, :, 0, :]
    keys_local = fields[:, :, 1, :]
    values_local = fields[:, :, 2, :]
    scale_factor = HEAD_WIDTH ** (-0.5)
    row_selector = (jnp.arange(DILATION_STEP, dtype=jnp.int32)[None, :] == offsets[:, None]).astype(
        jnp.float32
    )
    selected_rows = ENCODER_SLOTS // DILATION_STEP

    def select_rows(slide_field):
        reshaped_rows = slide_field.astype(jnp.float32).reshape(
            selected_rows, DILATION_STEP, local_head_output, HEAD_WIDTH
        )
        return jnp.einsum("rdhe,hd->rhe", reshaped_rows, row_selector).astype(jnp.bfloat16)

    query_sel = select_rows(query_rows)
    package = jnp.concatenate([select_rows(keys_local), select_rows(values_local)], axis=2).reshape(
        selected_rows, local_head_output * 2 * HEAD_WIDTH
    )
    portion = gather_seq(package)
    parts_kv = portion.reshape(portion.shape[0], local_head_output, 2, HEAD_WIDTH)
    scores = (
        jnp.einsum(
            "qhe,khe->hqk", query_sel, parts_kv[:, :, 0, :], preferred_element_type=jnp.float32
        )
        * scale_factor
    )
    weights = jnp.exp(scores)
    numer = jnp.einsum(
        "hqk,khe->hqe",
        weights.astype(jnp.bfloat16),
        parts_kv[:, :, 1, :],
        preferred_element_type=jnp.float32,
    )
    remote_den = jnp.sum(weights, axis=-1)
    scores = (
        jnp.einsum("qhe,khe->hqk", query_rows, keys_local, preferred_element_type=jnp.float32)
        * scale_factor
    )
    weights = jnp.exp(scores)
    local_num = jnp.einsum(
        "hqk,khe->hqe",
        weights.astype(jnp.bfloat16),
        values_local,
        preferred_element_type=jnp.float32,
    )
    local_den = jnp.sum(weights, axis=-1)
    spread_num = jnp.einsum("hre,hd->hrde", numer, row_selector).reshape(
        local_head_output, ENCODER_SLOTS, HEAD_WIDTH
    )
    spread_den = jnp.einsum("hr,hd->hrd", remote_den, row_selector).reshape(
        local_head_output, ENCODER_SLOTS
    )
    result = (local_num + spread_num) / (local_den + spread_den)[..., None]
    return (
        jnp.transpose(result, (1, 0, 2))
        .reshape(ENCODER_SLOTS, local_head_output * HEAD_WIDTH)
        .astype(jnp.bfloat16)
    )


def swap(array, axis, distance):
    size = lax.axis_size(axis)
    return lax.ppermute(array, axis, [(i, i ^ distance) for i in range(size)])


def block_at(array, index, size, axis):
    return lax.dynamic_slice_in_dim(array, index * size, size, axis)


def call(body, outs, inputs, spaces=None, scratch=(), copies=0, megabytes=40):
    spaces = spaces or [pltpu.VMEM] * len(inputs)
    scratch = list(scratch)
    if copies:
        scratch.append(pltpu.SemaphoreType.DMA((copies,)))
    return pl.pallas_call(
        body,
        out_shape=[jax.ShapeDtypeStruct(shape, kind) for shape, kind in outs],
        in_specs=[pl.BlockSpec(memory_space=space) for space in spaces],
        out_specs=[pl.BlockSpec(memory_space=pltpu.VMEM)] * len(outs),
        scratch_shapes=scratch,
        compiler_params=pltpu.CompilerParams(vmem_limit_bytes=megabytes * 1024 * 1024),
    )(*inputs)


def at(index, size):
    return pl.ds(pl.multiple_of(index * size, size), size)


def place():
    return tuple(lax.axis_index(name) for name in ("seq", "mp", "groups"))


def column_block(seq, mp):
    step = jnp.where(mp == 2, seq + 1, seq + 3) & 3
    return jnp.where(mp < 2, seq ^ (2 * mp), step)


def column_user(seq, mp):
    step = jnp.where(mp == 2, seq + 3, seq + 1) & 3
    return jnp.where(mp < 2, seq ^ (2 * mp), step)


def copier(sems, group):
    copies, used = [], [0]

    def copy(source, target, other=None):
        started = pltpu.make_async_copy(source, target, sems.at[used[0]])
        if other is None:
            started.start()
        else:
            second = pltpu.make_async_copy(other, target, sems.at[used[0]])
            pl.when(group == 0)(started.start)
            pl.when(group != 0)(second.start)
        copies.append(started)
        used[0] += 1

    return copies, copy


def normalise(rows, part, gain):
    values = rows[...].astype(jnp.float32)
    squares = jnp.sum(values * values, axis=1, keepdims=True)
    inverse = lax.rsqrt(squares * (1.0 / D_ENC) + epsilon)
    return (part.astype(jnp.float32) * inverse * gain[None, :]).astype(jnp.bfloat16)


def cut_first_body(
    count, tiles, w_gate, w_up, gain, first_out, second_out, quarter, held, sems
):
    seq, mp, group = place()
    copies, copy = copier(sems, group)
    half, units = w_gate.shape[0] // 2, w_gate.shape[1] // count
    features = quarter.shape[1]
    copy(tiles, held)
    for i in range(2):
        span = pl.ds(i * half, half), at(seq ^ 2, units)
        columns = pl.ds(features + i * units, units)
        copy(w_gate.at[span], second_out.at[:, columns], w_up.at[span])
        span = pl.ds(i * half, half), at(seq ^ 1, units)
        for k, weight in enumerate((w_gate, w_up)):
            columns = pl.ds(features + (2 * i + k) * units, units)
            copy(weight.at[span], first_out.at[:, columns])
    copies.pop(0).wait()
    columns = at(mp, features)
    own_columns = normalise(held, held[:, columns], gain[columns])
    second_out[:, :features] = own_columns
    first_out[:, :features] = own_columns
    quarter[...] = own_columns
    for started in copies:
        started.wait()


def cut_second_body(
    count, tiles, w_gate, w_up, w_down, gain, third_out, kept, near, far, normed, residual, held, sems
):
    seq, mp, group = place()
    copies, copy = copier(sems, group)
    half, units = w_gate.shape[0] // 2, w_gate.shape[1] // count
    copy(tiles, held)
    part = units // 2
    for j, target in ((2, far), (0, near)):
        rows = at(column_user(seq, mp ^ j) * 2 + group, part)
        copy(w_down.at[rows, :], target.at[pl.ds(0, part), :])
        rows = at(column_user(seq, mp ^ (j + 1)), units)
        copy(w_down.at[rows, :], target.at[pl.ds(part, units), :])
    for i in range(2):
        span = pl.ds(i * half, half), at(seq ^ 3, units)
        copy(w_gate.at[span], third_out.at[:, pl.ds(i * units, units)], w_up.at[span])
    for i, weight in enumerate((w_gate, w_up)):
        copy(weight.at[:, at(seq, units)], kept.at[:, pl.ds(i * units, units)])
    copies.pop(0).wait()
    normed[...] = normalise(held, held[...], gain[...])
    residual[...] = held[:, at(column_block(seq, mp), residual.shape[1])]
    for started in copies:
        started.wait()


def restack_body(second, third, first, stacked, columns):
    features = stacked.shape[2]
    stacked[0] = first[:, :features]
    stacked[1] = second[:, :features]
    stacked[2] = third[...]
    columns[...] = second[:, features:]


def pair_body(near, far, even, odd):
    for i, rows in enumerate((near, far)):
        even[i] = rows[: even.shape[1], :]
        odd[i] = rows[even.shape[1] :, :]


def routes_body(count, counts, offsets, dest, dest_row, routes):
    seq, _, _ = place()
    rows = dest_row.shape[1]
    capacity = ENCODER_SLOTS // count
    later = lax.broadcasted_iota(jnp.int32, (rows, rows), 1)
    earlier = lax.broadcasted_iota(jnp.int32, (rows, rows), 0)
    same = (dest[...] == dest_row[...]) & (earlier < later)
    rank = jnp.sum(jnp.where(same, 1, 0), axis=0, keepdims=True)
    live = lax.broadcasted_iota(jnp.int32, (1, rows), 1) < counts[0]
    codes = jnp.where(live, dest_row[...] * capacity + rank, -1)

    def chosen(wanted):
        return jnp.where(codes == wanted, 1.0, 0.0).astype(jnp.bfloat16)

    slot = lax.broadcasted_iota(jnp.int32, (capacity, rows), 0)
    for d in range(count):
        routes[pl.ds(d * capacity, capacity), :] = chosen((seq ^ d) * capacity + slot)
    per_block = capacity // DILATION_STEP
    spread = count * per_block
    index = lax.broadcasted_iota(jnp.int32, (spread, rows), 0)
    wanted = (index // per_block) * capacity + (index % per_block) * DILATION_STEP
    for h in range(offsets.shape[0]):
        routes[pl.ds(count * capacity + h * spread, spread), :] = chosen(wanted + offsets[h])


def hidden_body(count, normed, own, far, near, near_far, kept, next_in, *refs):
    (second, second_other, third, third_other), (out, weights) = refs[:4], refs[4:]
    seq, mp, group = place()
    depth, units = weights.shape[2:]
    half = depth // 2
    rows = normed.shape[0]
    for k in range(2):
        weights[k, seq] = kept[:, k * units : (k + 1) * units]
        for i in range(2):
            start = own.shape[2] + (2 * i + k) * units
            span = pl.ds(i * half, half)
            weights[k, seq ^ 1, span, :] = next_in[:, start : start + units]
    for d, mine, other in ((2, second, second_other), (3, third, third_other)):
        for i in range(2):
            span, columns = pl.ds(i * half, half), slice(i * units, (i + 1) * units)
            weights[group, seq ^ d, span, :] = mine[:, columns]
            weights[1 - group, seq ^ d, span, :] = other[:, columns]
    for d in range(count):
        if d == 0:
            pieces = [(normed[:, q * depth : (q + 1) * depth], q) for q in range(count)]
        else:
            pieces = [(own[d - 1], mp), (near[d - 1], mp ^ 1)]
            pieces += [(far[d - 1], mp ^ 2), (near_far[d - 1], mp ^ 3)]
        gate_act, up_act = (
            sum(
                jnp.dot(piece, weights[k, index], preferred_element_type=jnp.float32)
                for piece, index in pieces
            )
            for k in range(2)
        )
        gated = gate_act * jax.nn.sigmoid(gate_act) * up_act
        out[pl.ds(d * rows, rows), :] = gated.astype(jnp.bfloat16)


def down_body(residual, own, far, near, near_far, even, even_other, odd, *outs):
    _, _, group = place()
    rows = outs[0].shape[0]
    weights = [None, odd[0], None, odd[1]]
    for j in range(2):
        mine, other = even[j], even_other[j]
        low, high = jnp.where(group == 0, mine, other), jnp.where(group == 0, other, mine)
        weights[2 * j] = jnp.concatenate([low, high], axis=0)
    for i, out in enumerate(outs):
        total = residual[...].astype(jnp.float32) if i == 0 else 0.0
        for j, piece in enumerate((own, near, far, near_far)):
            total += jnp.dot(
                piece[pl.ds(i * rows, rows), :], weights[j], preferred_element_type=jnp.float32
            )
        out[...] = total.astype(out.dtype)


def sum_body(own, *refs):
    parts, out = refs[:-1], refs[-1]
    total = own[...] + sum(part[...].astype(jnp.float32) for part in parts)
    out[...] = total.astype(out.dtype)


def project_body(count, gain, routes, w_qkv_t, own, far, near, near_far, *outs):
    seq, mp, _ = place()
    features = own.shape[1]
    capacity = outs[0].shape[0]
    heads = w_qkv_t.shape[0] // (3 * HEAD_WIDTH)
    squares, total = 0.0, 0.0
    for j, piece in enumerate((own, near, far, near_far)):
        index = column_block(seq, mp ^ j)
        v = piece[...].astype(jnp.float32)
        squares += jnp.sum(v * v, axis=1, keepdims=True)
        scaled = (v * gain[:, at(index, features)]).astype(jnp.bfloat16)
        total += lax.dot_general(
            scaled,
            w_qkv_t[:, at(index, features)],
            (((1,), (1,)), ((), ())),
            preferred_element_type=jnp.float32,
        )
    projected = (total * lax.rsqrt(squares * (1.0 / D_ENC) + epsilon)).astype(jnp.bfloat16)
    routed = jnp.dot(routes[...], projected, preferred_element_type=jnp.float32)
    routed = routed.astype(jnp.bfloat16)
    width = projected.shape[1]
    spread = capacity // 2
    for d, out in enumerate(outs):
        out[:, :width] = routed[d * capacity : (d + 1) * capacity]
    for h in range(heads):
        first = count * capacity + h * spread
        for i in range(2):
            start = (3 * h + 1 + i) * HEAD_WIDTH
            piece = routed[first : first + spread, start : start + HEAD_WIDTH]
            for out in outs:
                span = slice(width + h * HEAD_WIDTH, width + (h + 1) * HEAD_WIDTH)
                out[i * spread : (i + 1) * spread, span] = piece


def attend_body(count, offsets, *refs):
    packages, out, rows = refs[:count], refs[count], refs[count + 1]
    seq, _, _ = place()
    capacity = packages[0].shape[0]
    heads = offsets.shape[0]
    width = heads * 3 * HEAD_WIDTH
    for d, package in zip(ORDER, packages):
        rows[at(seq ^ d, capacity), :] = package[:, :width]
    far = [package[:, width:] for package in packages]
    half = capacity // 2
    far_keys = jnp.concatenate([f[:half] for f in far], axis=0)
    far_values = jnp.concatenate([f[half:] for f in far], axis=0)
    residue = lax.broadcasted_iota(jnp.int32, (1, out.shape[1]), 1) % DILATION_STEP
    scale_factor = HEAD_WIDTH ** (-0.5)

    local = out.shape[1]
    for h in range(heads):
        query, key, value = (
            rows[:, pl.ds((3 * h + i) * HEAD_WIDTH, HEAD_WIDTH)] for i in range(3)
        )
        span = slice(h * HEAD_WIDTH, (h + 1) * HEAD_WIDTH)
        keys = jnp.concatenate([key, far_keys[:, span]], axis=0)
        values = jnp.concatenate([value, far_values[:, span]], axis=0)
        scores = lax.dot_general(
            keys, query, (((1,), (1,)), ((), ())), preferred_element_type=jnp.float32
        )
        weights = jnp.exp(scores * scale_factor)
        dilated = jnp.where(residue == offsets[h], weights[local:], 0.0)
        weights = jnp.concatenate([weights[:local], dilated], axis=0)
        numer = lax.dot_general(
            values,
            weights.astype(jnp.bfloat16),
            (((0,), (0,)), ((), ())),
            preferred_element_type=jnp.float32,
        )
        denom = jnp.sum(weights, axis=0, keepdims=True)
        out[span, :] = (numer / denom).astype(jnp.bfloat16)


def spread_mp(own, beside=None):
    far = swap(own, "mp", 2)
    relayed = far if beside is None else lax.optimization_barrier((far, beside))[0]
    return far, swap(own, "mp", 1), swap(relayed, "mp", 1)


def split_hidden_plan(
    tiles, counts, dest, gain_enc, w_gate, w_up, w_down, gain_slide, w_qkv, offsets
):
    count, mp_size = lax.axis_size("seq"), lax.axis_size("mp")
    seq, mp = lax.axis_index("seq"), lax.axis_index("mp")
    capacity = ENCODER_SLOTS // count
    tile_rows = tiles.shape[0]
    features = D_ENC // mp_size
    depth = w_gate.shape[0]
    units = w_gate.shape[1] // count
    heads = offsets.shape[0]
    bf16 = jnp.bfloat16
    vmem, smem = pltpu.VMEM, pltpu.SMEM

    first_out, second_out, quarter = call(
        functools.partial(cut_first_body, count),
        [
            ((tile_rows, features + 4 * units), bf16),
            ((tile_rows, features + 2 * units), bf16),
            ((tile_rows, features), bf16),
        ],
        (tiles, w_gate, w_up, gain_enc),
        spaces=[pltpu.HBM] * 3 + [vmem],
        copies=7,
        scratch=[pltpu.VMEM((tile_rows, D_ENC), bf16)],
        megabytes=57,
    )
    third_out, kept, down_near, down_far, normed, residual = call(
        functools.partial(cut_second_body, count),
        [
            ((tile_rows, 2 * units), bf16),
            ((depth, 2 * units), bf16),
            ((3 * units // 2, features), bf16),
            ((3 * units // 2, features), bf16),
            ((tile_rows, D_ENC), bf16),
            ((tile_rows, features), bf16),
        ],
        (tiles, w_gate, w_up, w_down, gain_enc),
        spaces=[pltpu.HBM] * 4 + [vmem],
        scratch=[pltpu.VMEM((tile_rows, D_ENC), bf16)],
        copies=9,
        megabytes=57,
    )
    routes = call(
        functools.partial(routes_body, count),
        [((ENCODER_SLOTS + heads * ENCODER_SLOTS // DILATION_STEP, tile_rows), bf16)],
        (counts, offsets, dest, dest.reshape(1, tile_rows)),
        spaces=[smem, smem, vmem, vmem],
    )[0]

    second_in, third_in = swap(second_out, "seq", 2), swap(quarter, "seq", 3)
    arrived = second_in, third_in, swap(first_out, "seq", 1)
    from_far = swap(down_far, "mp", 2)
    arrived, from_far, routes = lax.optimization_barrier((arrived, from_far, routes))
    own, columns = call(
        restack_body,
        [
            ((count - 1, tile_rows, features), bf16),
            ((tile_rows, 2 * units), bf16),
        ],
        arrived,
    )
    third_out, down_near, _ = lax.optimization_barrier((third_out, down_near, own))
    down_send = call(
        pair_body,
        [((2, units // 2, features), bf16), ((2, units, features), bf16)],
        (down_near, from_far),
    )
    third, others, far, near, down_send = lax.optimization_barrier(
        (
            swap(third_out, "seq", 3),
            swap(columns, "groups", 1),
            swap(own, "mp", 2),
            swap(own, "mp", 1),
            down_send,
        )
    )
    halves = columns, others, third, swap(third, "groups", 1)
    spread = far, near, swap(far, "mp", 1)
    down_send = lax.optimization_barrier((down_send[0], spread[2]))[0], down_send[1]
    parts = []
    for j in range(2):
        perm = []
        for s in range(count):
            for m in range(mp_size):
                k = m ^ j
                user = (s ^ 2 * k) if k < 2 else (s + 2 * k - 5) % count
                perm.append((s * mp_size + m, user * mp_size + k))
        parts.append(lax.ppermute(down_send[j], ("seq", "mp"), perm))
    halves, spread, parts[0] = lax.optimization_barrier((halves, spread, parts[0]))
    hidden = call(
        functools.partial(hidden_body, count),
        [((count * tile_rows, units), bf16)],
        (normed, own, *spread, kept, arrived[2], *halves),
        scratch=[
            pltpu.VMEM((2, count, depth, units), bf16),
        ],
    )[0]
    even, odd = parts
    even_other = swap(even, "groups", 1)
    sums = call(
        down_body,
        [((tile_rows, features), kind) for kind in (jnp.float32, bf16, bf16, bf16)],
        (residual, hidden, *spread_mp(hidden, even_other), even, even_other, odd),
    )
    holder = [0, 2, 1, 3]

    def to_owner(part, d):
        perm = []
        for s in range(count):
            for m in range(mp_size):
                owner = s ^ d
                perm.append((s * mp_size + m, owner * mp_size + holder[(s + holder[m] - owner) % count]))
        return lax.ppermute(part, ("seq", "mp"), perm)

    arrived = [to_owner(sums[d], d) for d in (2, 3, 1)]
    embedded_cols = call(
        sum_body, [((tile_rows, features), bf16)], (sums[0], *arrived)
    )[0]

    packages = call(
        functools.partial(project_body, count),
        [((capacity, 4 * heads * HEAD_WIDTH), bf16)] * count,
        (gain_slide[None, :], routes, w_qkv.T, embedded_cols, *spread_mp(embedded_cols)),
    )
    packages = [swap(packages[d], "seq", d) for d in ORDER[:-1]] + [packages[0]]
    return call(
        functools.partial(attend_body, count),
        [((heads * HEAD_WIDTH, ENCODER_SLOTS), bf16)],
        (offsets, *packages),
        spaces=[smem] + [vmem] * count,
        scratch=[pltpu.VMEM((ENCODER_SLOTS, 3 * heads * HEAD_WIDTH), bf16)],
    )[0].T


def on_device(*arrays):
    sizes = lax.axis_size("groups"), lax.axis_size("seq"), lax.axis_size("mp")
    if sizes == (2, 4, 4):
        return split_hidden_plan(*arrays)
    return gathered_plan(*arrays)


def solution(mesh):
    return jax.shard_map(
        on_device,
        mesh=mesh,
        in_specs=(
            P(("groups", "seq"), None),
            P(("groups", "seq")),
            P(("groups", "seq"), None),
            P(),
            P("seq", "mp"),
            P("seq", "mp"),
            P("mp", "seq"),
            P(),
            P(None, "mp"),
            P("mp"),
        ),
        out_specs=P(("groups", "seq"), "mp"),
        check_vma=False,
    )
```

```python
import functools

import jax
import jax.numpy as jnp
from jax import lax
from jax.experimental import pallas as pl
from jax.experimental.pallas import tpu as pltpu
from jax.sharding import PartitionSpec as P

D_ENC = 1536
HEAD_WIDTH = 64
DILATION_STEP = 8
ENCODER_SLOTS = 256
ORDER = (2, 3, 1, 0)


epsilon = 1e-05


def gather_seq(package):
    count = lax.axis_size("seq")
    if count & (count - 1) == 0 and count <= 4:
        return jnp.concatenate([package] + [swap(package, "seq", d) for d in range(1, count)])
    return lax.all_gather(package, "seq", axis=0, tiled=True)


def gathered_plan(tiles, counts, dest, gain_enc, w_gate, w_up, w_down, gain_slide, w_qkv, offsets):
    seq_count = lax.axis_size("seq")
    capacity = ENCODER_SLOTS // seq_count
    tile_rows = tiles.shape[0]
    target = dest[:, 0]
    live_rows = jnp.arange(tile_rows, dtype=jnp.int32) < counts[0]
    chosen = (
        (target[:, None] == jnp.arange(seq_count, dtype=jnp.int32)[None, :]) & live_rows[:, None]
    ).astype(jnp.int32)
    arrival = jnp.sum((jnp.cumsum(chosen, axis=0) - chosen) * chosen, axis=1)
    slot_index = jnp.where(live_rows, target * capacity + arrival, ENCODER_SLOTS)
    outgoing = (
        jnp.zeros((ENCODER_SLOTS, D_ENC), jnp.bfloat16).at[slot_index].set(tiles, mode="drop")
    )
    arrived = lax.all_to_all(outgoing, "seq", split_axis=0, concat_axis=0, tiled=True)
    arrived_f = arrived.astype(jnp.float32)
    inverse = lax.rsqrt(jnp.mean(arrived_f * arrived_f, axis=-1, keepdims=True) + epsilon)
    normed = (arrived_f * inverse * gain_enc).astype(jnp.bfloat16)

    def add_rows(portion):
        return jnp.dot(normed, portion, preferred_element_type=jnp.float32)

    gate_act = add_rows(lax.all_gather(w_gate, "seq", axis=0, tiled=True))
    up_act = add_rows(lax.all_gather(w_up, "seq", axis=0, tiled=True))
    hidden = (jax.nn.silu(gate_act) * up_act).astype(jnp.bfloat16)
    partial_out = jnp.dot(
        hidden,
        lax.all_gather(w_down, "seq", axis=1, tiled=True),
        preferred_element_type=jnp.float32,
    )
    share = lax.psum_scatter(partial_out, "mp", scatter_dimension=1, tiled=True)
    share_width = share.shape[1]
    own_cols = lax.dynamic_slice_in_dim(
        arrived_f, lax.axis_index("mp") * share_width, share_width, 1
    )
    embedded_cols = (own_cols + share).astype(jnp.bfloat16)
    embedded = lax.all_gather(embedded_cols, "mp", axis=1, tiled=True)
    return slide_layer(embedded, gain_slide, w_qkv, offsets)


def slide_layer(embedded, gain_slide, w_qkv, offsets):
    portion_f = embedded.astype(jnp.float32)
    accumulated = jnp.dot(
        (portion_f * gain_slide).astype(jnp.bfloat16), w_qkv, preferred_element_type=jnp.float32
    )
    accumulated, squares = (accumulated, jnp.sum(portion_f * portion_f, axis=1))
    projected = accumulated * lax.rsqrt(squares / D_ENC + epsilon)[:, None]
    qkv_act = projected.astype(jnp.bfloat16)
    local_head_output = offsets.shape[0]
    fields = qkv_act.reshape(ENCODER_SLOTS, local_head_output, 3, HEAD_WIDTH)
    query_rows = fields[:, :, 0, :]
    keys_local = fields[:, :, 1, :]
    values_local = fields[:, :, 2, :]
    scale_factor = HEAD_WIDTH ** (-0.5)
    row_selector = (jnp.arange(DILATION_STEP, dtype=jnp.int32)[None, :] == offsets[:, None]).astype(
        jnp.float32
    )
    selected_rows = ENCODER_SLOTS // DILATION_STEP

    def select_rows(slide_field):
        reshaped_rows = slide_field.astype(jnp.float32).reshape(
            selected_rows, DILATION_STEP, local_head_output, HEAD_WIDTH
        )
        return jnp.einsum("rdhe,hd->rhe", reshaped_rows, row_selector).astype(jnp.bfloat16)

    query_sel = select_rows(query_rows)
    package = jnp.concatenate([select_rows(keys_local), select_rows(values_local)], axis=2).reshape(
        selected_rows, local_head_output * 2 * HEAD_WIDTH
    )
    portion = gather_seq(package)
    parts_kv = portion.reshape(portion.shape[0], local_head_output, 2, HEAD_WIDTH)
    scores = (
        jnp.einsum(
            "qhe,khe->hqk", query_sel, parts_kv[:, :, 0, :], preferred_element_type=jnp.float32
        )
        * scale_factor
    )
    weights = jnp.exp(scores)
    numer = jnp.einsum(
        "hqk,khe->hqe",
        weights.astype(jnp.bfloat16),
        parts_kv[:, :, 1, :],
        preferred_element_type=jnp.float32,
    )
    remote_den = jnp.sum(weights, axis=-1)
    scores = (
        jnp.einsum("qhe,khe->hqk", query_rows, keys_local, preferred_element_type=jnp.float32)
        * scale_factor
    )
    weights = jnp.exp(scores)
    local_num = jnp.einsum(
        "hqk,khe->hqe",
        weights.astype(jnp.bfloat16),
        values_local,
        preferred_element_type=jnp.float32,
    )
    local_den = jnp.sum(weights, axis=-1)
    spread_num = jnp.einsum("hre,hd->hrde", numer, row_selector).reshape(
        local_head_output, ENCODER_SLOTS, HEAD_WIDTH
    )
    spread_den = jnp.einsum("hr,hd->hrd", remote_den, row_selector).reshape(
        local_head_output, ENCODER_SLOTS
    )
    result = (local_num + spread_num) / (local_den + spread_den)[..., None]
    return (
        jnp.transpose(result, (1, 0, 2))
        .reshape(ENCODER_SLOTS, local_head_output * HEAD_WIDTH)
        .astype(jnp.bfloat16)
    )


def swap(array, axis, distance):
    size = lax.axis_size(axis)
    return lax.ppermute(array, axis, [(i, i ^ distance) for i in range(size)])


def block_at(array, index, size, axis):
    return lax.dynamic_slice_in_dim(array, index * size, size, axis)


def call(body, outs, inputs, spaces=None, scratch=(), copies=0, megabytes=40):
    spaces = spaces or [pltpu.VMEM] * len(inputs)
    scratch = list(scratch)
    if copies:
        scratch.append(pltpu.SemaphoreType.DMA((copies,)))
    return pl.pallas_call(
        body,
        out_shape=[jax.ShapeDtypeStruct(shape, kind) for shape, kind in outs],
        in_specs=[pl.BlockSpec(memory_space=space) for space in spaces],
        out_specs=[pl.BlockSpec(memory_space=pltpu.VMEM)] * len(outs),
        scratch_shapes=scratch,
        compiler_params=pltpu.CompilerParams(vmem_limit_bytes=megabytes * 1024 * 1024),
    )(*inputs)


def at(index, size):
    return pl.ds(pl.multiple_of(index * size, size), size)


def place():
    return tuple(lax.axis_index(name) for name in ("seq", "mp", "groups"))


def column_block(seq, mp):
    step = jnp.where(mp == 2, seq + 1, seq + 3) & 3
    return jnp.where(mp < 2, seq ^ (2 * mp), step)


def column_user(seq, mp):
    step = jnp.where(mp == 2, seq + 3, seq + 1) & 3
    return jnp.where(mp < 2, seq ^ (2 * mp), step)


def copier(sems, group):
    copies, used = [], [0]

    def copy(source, target, other=None):
        started = pltpu.make_async_copy(source, target, sems.at[used[0]])
        if other is None:
            started.start()
        else:
            second = pltpu.make_async_copy(other, target, sems.at[used[0]])
            pl.when(group == 0)(started.start)
            pl.when(group != 0)(second.start)
        copies.append(started)
        used[0] += 1

    return copies, copy


def normalise(rows, part, gain):
    values = rows[...].astype(jnp.float32)
    squares = jnp.sum(values * values, axis=1, keepdims=True)
    inverse = lax.rsqrt(squares * (1.0 / D_ENC) + epsilon)
    return (part.astype(jnp.float32) * inverse * gain[None, :]).astype(jnp.bfloat16)


def cut_first_body(
    count, tiles, w_gate, w_up, w_down, gain, first_out, second_out, third_out, near, far, held, sems
):
    seq, mp, group = place()
    copies, copy = copier(sems, group)
    half, units = w_gate.shape[0] // 2, w_gate.shape[1] // count
    features = D_ENC // count
    copy(tiles, held)
    for i in range(2):
        for d, target in ((2, second_out), (3, third_out)):
            span = pl.ds(i * half, half), at(seq ^ d, units)
            columns = pl.ds(features + i * units, units)
            copy(w_gate.at[span], target.at[:, columns], w_up.at[span])
        span = pl.ds(i * half, half), at(seq ^ 1, units)
        for k, weight in enumerate((w_gate, w_up)):
            columns = pl.ds(features + (2 * i + k) * units, units)
            copy(weight.at[span], first_out.at[:, columns])
    for j in range(4):
        rows = at(column_user(seq, mp ^ j), units)
        copy(w_down.at[rows, :], (far if j >= 2 else near).at[j % 2])
    copies.pop(0).wait()
    columns = at(mp, features)
    own_columns = normalise(held, held[:, columns], gain[columns])
    for target in (second_out, third_out, first_out):
        target[:, :features] = own_columns
    for started in copies:
        started.wait()


def cut_second_body(
    count, tiles, w_gate, w_up, gain, kept, normed, residual, held, sems
):
    seq, mp, group = place()
    copies, copy = copier(sems, group)
    units = w_gate.shape[1] // count
    copy(tiles, held)
    for i, weight in enumerate((w_gate, w_up)):
        copy(weight.at[:, at(seq, units)], kept.at[:, pl.ds(i * units, units)])
    copies.pop(0).wait()
    normed[...] = normalise(held, held[...], gain[...])
    residual[...] = held[:, at(column_block(seq, mp), residual.shape[1])]
    for started in copies:
        started.wait()


def restack_body(first, second, third, stacked, columns):
    features = stacked.shape[2]
    stacked[0] = first[:, :features]
    stacked[1] = second[:, :features]
    stacked[2] = third[:, :features]
    columns[0] = second[:, features:]
    columns[1] = third[:, features:]


def pair_body(near, far, even, odd):
    for i, rows in enumerate((near, far)):
        even[i] = rows[0]
        odd[i] = rows[1]


def routes_body(count, counts, offsets, dest, dest_row, routes):
    seq, _, _ = place()
    rows = dest_row.shape[1]
    capacity = ENCODER_SLOTS // count
    later = lax.broadcasted_iota(jnp.int32, (rows, rows), 1)
    earlier = lax.broadcasted_iota(jnp.int32, (rows, rows), 0)
    same = (dest[...] == dest_row[...]) & (earlier < later)
    rank = jnp.sum(jnp.where(same, 1, 0), axis=0, keepdims=True)
    live = lax.broadcasted_iota(jnp.int32, (1, rows), 1) < counts[0]
    codes = jnp.where(live, dest_row[...] * capacity + rank, -1)

    def chosen(wanted):
        return jnp.where(codes == wanted, 1.0, 0.0).astype(jnp.bfloat16)

    slot = lax.broadcasted_iota(jnp.int32, (capacity, rows), 0)
    for d in range(count):
        routes[pl.ds(d * capacity, capacity), :] = chosen((seq ^ d) * capacity + slot)
    per_block = capacity // DILATION_STEP
    spread = count * per_block
    index = lax.broadcasted_iota(jnp.int32, (spread, rows), 0)
    wanted = (index // per_block) * capacity + (index % per_block) * DILATION_STEP
    for h in range(offsets.shape[0]):
        routes[pl.ds(count * capacity + h * spread, spread), :] = chosen(wanted + offsets[h])


def hidden_body(count, normed, own, far, near, near_far, kept, next_in, *refs):
    columns, others, out, weights = refs
    seq, mp, group = place()
    depth, units = weights.shape[2:]
    half = depth // 2
    rows = normed.shape[0]
    for k in range(2):
        weights[k, seq] = kept[:, k * units : (k + 1) * units]
        for i in range(2):
            start = own.shape[2] + (2 * i + k) * units
            span = pl.ds(i * half, half)
            weights[k, seq ^ 1, span, :] = next_in[:, start : start + units]
    for j in range(2):
        for i in range(2):
            span, half_columns = pl.ds(i * half, half), slice(i * units, (i + 1) * units)
            weights[group, seq ^ (2 + j), span, :] = columns[j, :, half_columns]
            weights[1 - group, seq ^ (2 + j), span, :] = others[j, :, half_columns]
    for d in range(count):
        if d == 0:
            pieces = [(normed[:, q * depth : (q + 1) * depth], q) for q in range(count)]
        else:
            pieces = [(own[d - 1], mp), (near[d - 1], mp ^ 1)]
            pieces += [(far[d - 1], mp ^ 2), (near_far[d - 1], mp ^ 3)]
        gate_act, up_act = (
            sum(
                jnp.dot(piece, weights[k, index], preferred_element_type=jnp.float32)
                for piece, index in pieces
            )
            for k in range(2)
        )
        gated = gate_act * jax.nn.sigmoid(gate_act) * up_act
        out[pl.ds(d * rows, rows), :] = gated.astype(jnp.bfloat16)


def down_body(residual, own, far, near, near_far, even, odd, *outs):
    rows = outs[0].shape[0]
    weights = [even[0], odd[0], even[1], odd[1]]
    for i, out in enumerate(outs):
        total = residual[...].astype(jnp.float32) if i == 0 else 0.0
        for j, piece in enumerate((own, near, far, near_far)):
            total += jnp.dot(
                piece[pl.ds(i * rows, rows), :], weights[j], preferred_element_type=jnp.float32
            )
        out[...] = total.astype(out.dtype)


def sum_body(own, *refs):
    parts, out = refs[:-1], refs[-1]
    total = own[...] + sum(part[...].astype(jnp.float32) for part in parts)
    out[...] = total.astype(out.dtype)


def project_body(count, gain, routes, w_qkv_t, own, far, near, near_far, *outs):
    seq, mp, _ = place()
    features = own.shape[1]
    capacity = outs[0].shape[0]
    heads = w_qkv_t.shape[0] // (3 * HEAD_WIDTH)
    squares, total = 0.0, 0.0
    for j, piece in enumerate((own, near, far, near_far)):
        index = column_block(seq, mp ^ j)
        v = piece[...].astype(jnp.float32)
        squares += jnp.sum(v * v, axis=1, keepdims=True)
        scaled = (v * gain[:, at(index, features)]).astype(jnp.bfloat16)
        total += lax.dot_general(
            scaled,
            w_qkv_t[:, at(index, features)],
            (((1,), (1,)), ((), ())),
            preferred_element_type=jnp.float32,
        )
    projected = (total * lax.rsqrt(squares * (1.0 / D_ENC) + epsilon)).astype(jnp.bfloat16)
    routed = jnp.dot(routes[...], projected, preferred_element_type=jnp.float32)
    routed = routed.astype(jnp.bfloat16)
    width = projected.shape[1]
    spread = capacity // 2
    for d, out in enumerate(outs):
        out[:, :width] = routed[d * capacity : (d + 1) * capacity]
    for h in range(heads):
        first = count * capacity + h * spread
        for i in range(2):
            start = (3 * h + 1 + i) * HEAD_WIDTH
            piece = routed[first : first + spread, start : start + HEAD_WIDTH]
            for out in outs:
                span = slice(width + h * HEAD_WIDTH, width + (h + 1) * HEAD_WIDTH)
                out[i * spread : (i + 1) * spread, span] = piece


def attend_body(count, offsets, *refs):
    packages, out, rows = refs[:count], refs[count], refs[count + 1]
    seq, _, _ = place()
    capacity = packages[0].shape[0]
    heads = offsets.shape[0]
    width = heads * 3 * HEAD_WIDTH
    for d, package in zip(ORDER, packages):
        rows[at(seq ^ d, capacity), :] = package[:, :width]
    far = [package[:, width:] for package in packages]
    half = capacity // 2
    far_keys = jnp.concatenate([f[:half] for f in far], axis=0)
    far_values = jnp.concatenate([f[half:] for f in far], axis=0)
    residue = lax.broadcasted_iota(jnp.int32, (1, out.shape[1]), 1) % DILATION_STEP
    scale_factor = HEAD_WIDTH ** (-0.5)

    local = out.shape[1]
    for h in range(heads):
        query, key, value = (
            rows[:, pl.ds((3 * h + i) * HEAD_WIDTH, HEAD_WIDTH)] for i in range(3)
        )
        span = slice(h * HEAD_WIDTH, (h + 1) * HEAD_WIDTH)
        keys = jnp.concatenate([key, far_keys[:, span]], axis=0)
        values = jnp.concatenate([value, far_values[:, span]], axis=0)
        scores = lax.dot_general(
            keys, query, (((1,), (1,)), ((), ())), preferred_element_type=jnp.float32
        )
        weights = jnp.exp(scores * scale_factor)
        dilated = jnp.where(residue == offsets[h], weights[local:], 0.0)
        weights = jnp.concatenate([weights[:local], dilated], axis=0)
        numer = lax.dot_general(
            values,
            weights.astype(jnp.bfloat16),
            (((0,), (0,)), ((), ())),
            preferred_element_type=jnp.float32,
        )
        denom = jnp.sum(weights, axis=0, keepdims=True)
        out[span, :] = (numer / denom).astype(jnp.bfloat16)


def spread_mp(own, beside=None):
    far = swap(own, "mp", 2)
    relayed = far if beside is None else lax.optimization_barrier((far, beside))[0]
    return far, swap(own, "mp", 1), swap(relayed, "mp", 1)


def split_hidden_plan(
    tiles, counts, dest, gain_enc, w_gate, w_up, w_down, gain_slide, w_qkv, offsets
):
    count, mp_size = lax.axis_size("seq"), lax.axis_size("mp")
    seq, mp = lax.axis_index("seq"), lax.axis_index("mp")
    capacity = ENCODER_SLOTS // count
    tile_rows = tiles.shape[0]
    features = D_ENC // mp_size
    depth = w_gate.shape[0]
    units = w_gate.shape[1] // count
    heads = offsets.shape[0]
    bf16 = jnp.bfloat16
    vmem, smem = pltpu.VMEM, pltpu.SMEM

    *outgoing, down_near, down_far = call(
        functools.partial(cut_first_body, count),
        [
            ((tile_rows, features + 4 * units), bf16),
            ((tile_rows, features + 2 * units), bf16),
            ((tile_rows, features + 2 * units), bf16),
            ((2, units, features), bf16),
            ((2, units, features), bf16),
        ],
        (tiles, w_gate, w_up, w_down, gain_enc),
        spaces=[pltpu.HBM] * 4 + [vmem],
        copies=13,
        scratch=[pltpu.VMEM((tile_rows, D_ENC), bf16)],
        megabytes=57,
    )
    kept, normed, residual = call(
        functools.partial(cut_second_body, count),
        [
            ((depth, 2 * units), bf16),
            ((tile_rows, D_ENC), bf16),
            ((tile_rows, features), bf16),
        ],
        (tiles, w_gate, w_up, gain_enc),
        spaces=[pltpu.HBM] * 3 + [vmem],
        scratch=[pltpu.VMEM((tile_rows, D_ENC), bf16)],
        copies=3,
        megabytes=57,
    )
    routes = call(
        functools.partial(routes_body, count),
        [((ENCODER_SLOTS + heads * ENCODER_SLOTS // DILATION_STEP, tile_rows), bf16)],
        (counts, offsets, dest, dest.reshape(1, tile_rows)),
        spaces=[smem, smem, vmem, vmem],
    )[0]

    arrived = [swap(outgoing[d - 1], "seq", d) for d in (1, 2, 3)]
    from_far = swap(down_far, "mp", 2)
    down_send = call(pair_body, [((2, units, features), bf16)] * 2, (down_near, from_far))
    arrived, down_send, routes, kept, normed, residual = lax.optimization_barrier(
        (arrived, down_send, routes, kept, normed, residual)
    )
    own, columns = call(
        restack_body,
        [
            ((count - 1, tile_rows, features), bf16),
            ((count - 2, tile_rows, 2 * units), bf16),
        ],
        arrived,
    )
    others = swap(columns, "groups", 1)
    down_send, _ = lax.optimization_barrier((down_send, own))
    parts = []
    for j in range(2):
        perm = []
        for s in range(count):
            for m in range(mp_size):
                k = m ^ j
                user = (s ^ 2 * k) if k < 2 else (s + 2 * k - 5) % count
                perm.append((s * mp_size + m, user * mp_size + k))
        parts.append(lax.ppermute(down_send[j], ("seq", "mp"), perm))
    even, odd = parts
    spread = spread_mp(own, (others, even))
    hidden = call(
        functools.partial(hidden_body, count),
        [((count * tile_rows, units), bf16)],
        (normed, own, *spread, kept, arrived[0], columns, others),
        scratch=[
            pltpu.VMEM((2, count, depth, units), bf16),
        ],
    )[0]
    sums = call(
        down_body,
        [((tile_rows, features), kind) for kind in (jnp.float32, bf16, bf16, bf16)],
        (residual, hidden, *spread_mp(hidden), even, odd),
    )
    holder = [0, 2, 1, 3]

    def to_owner(part, d):
        perm = []
        for s in range(count):
            for m in range(mp_size):
                owner = s ^ d
                perm.append((s * mp_size + m, owner * mp_size + holder[(s + holder[m] - owner) % count]))
        return lax.ppermute(part, ("seq", "mp"), perm)

    arrived = [to_owner(sums[d], d) for d in (2, 3, 1)]
    embedded_cols = call(
        sum_body, [((tile_rows, features), bf16)], (sums[0], *arrived)
    )[0]

    packages = call(
        functools.partial(project_body, count),
        [((capacity, 4 * heads * HEAD_WIDTH), bf16)] * count,
        (gain_slide[None, :], routes, w_qkv.T, embedded_cols, *spread_mp(embedded_cols)),
    )
    packages = [swap(packages[d], "seq", d) for d in ORDER[:-1]] + [packages[0]]
    return call(
        functools.partial(attend_body, count),
        [((heads * HEAD_WIDTH, ENCODER_SLOTS), bf16)],
        (offsets, *packages),
        spaces=[smem] + [vmem] * count,
        scratch=[pltpu.VMEM((ENCODER_SLOTS, 3 * heads * HEAD_WIDTH), bf16)],
    )[0].T


def on_device(*arrays):
    sizes = lax.axis_size("groups"), lax.axis_size("seq"), lax.axis_size("mp")
    if sizes == (2, 4, 4):
        return split_hidden_plan(*arrays)
    return gathered_plan(*arrays)


def solution(mesh):
    return jax.shard_map(
        on_device,
        mesh=mesh,
        in_specs=(
            P(("groups", "seq"), None),
            P(("groups", "seq")),
            P(("groups", "seq"), None),
            P(),
            P("seq", "mp"),
            P("seq", "mp"),
            P("mp", "seq"),
            P(),
            P(None, "mp"),
            P("mp"),
        ),
        out_specs=P(("groups", "seq"), "mp"),
        check_vma=False,
    )
```

```python
import functools

import jax
import jax.numpy as jnp
from jax import lax
from jax.experimental import pallas as pl
from jax.experimental.pallas import tpu as pltpu
from jax.sharding import PartitionSpec as P

D_ENC = 1536
HEAD_WIDTH = 64
DILATION_STEP = 8
ENCODER_SLOTS = 256
ORDER = (2, 3, 1, 0)


epsilon = 1e-05


def gather_seq(package):
    count = lax.axis_size("seq")
    if count & (count - 1) == 0 and count <= 4:
        return jnp.concatenate([package] + [swap(package, "seq", d) for d in range(1, count)])
    return lax.all_gather(package, "seq", axis=0, tiled=True)


def gathered_plan(tiles, counts, dest, gain_enc, w_gate, w_up, w_down, gain_slide, w_qkv, offsets):
    seq_count = lax.axis_size("seq")
    capacity = ENCODER_SLOTS // seq_count
    tile_rows = tiles.shape[0]
    target = dest[:, 0]
    live_rows = jnp.arange(tile_rows, dtype=jnp.int32) < counts[0]
    chosen = (
        (target[:, None] == jnp.arange(seq_count, dtype=jnp.int32)[None, :]) & live_rows[:, None]
    ).astype(jnp.int32)
    arrival = jnp.sum((jnp.cumsum(chosen, axis=0) - chosen) * chosen, axis=1)
    slot_index = jnp.where(live_rows, target * capacity + arrival, ENCODER_SLOTS)
    outgoing = (
        jnp.zeros((ENCODER_SLOTS, D_ENC), jnp.bfloat16).at[slot_index].set(tiles, mode="drop")
    )
    arrived = lax.all_to_all(outgoing, "seq", split_axis=0, concat_axis=0, tiled=True)
    arrived_f = arrived.astype(jnp.float32)
    inverse = lax.rsqrt(jnp.mean(arrived_f * arrived_f, axis=-1, keepdims=True) + epsilon)
    normed = (arrived_f * inverse * gain_enc).astype(jnp.bfloat16)

    def add_rows(portion):
        return jnp.dot(normed, portion, preferred_element_type=jnp.float32)

    gate_act = add_rows(lax.all_gather(w_gate, "seq", axis=0, tiled=True))
    up_act = add_rows(lax.all_gather(w_up, "seq", axis=0, tiled=True))
    hidden = (jax.nn.silu(gate_act) * up_act).astype(jnp.bfloat16)
    partial_out = jnp.dot(
        hidden,
        lax.all_gather(w_down, "seq", axis=1, tiled=True),
        preferred_element_type=jnp.float32,
    )
    share = lax.psum_scatter(partial_out, "mp", scatter_dimension=1, tiled=True)
    share_width = share.shape[1]
    own_cols = lax.dynamic_slice_in_dim(
        arrived_f, lax.axis_index("mp") * share_width, share_width, 1
    )
    embedded_cols = (own_cols + share).astype(jnp.bfloat16)
    embedded = lax.all_gather(embedded_cols, "mp", axis=1, tiled=True)
    return slide_layer(embedded, gain_slide, w_qkv, offsets)


def slide_layer(embedded, gain_slide, w_qkv, offsets):
    portion_f = embedded.astype(jnp.float32)
    accumulated = jnp.dot(
        (portion_f * gain_slide).astype(jnp.bfloat16), w_qkv, preferred_element_type=jnp.float32
    )
    accumulated, squares = (accumulated, jnp.sum(portion_f * portion_f, axis=1))
    projected = accumulated * lax.rsqrt(squares / D_ENC + epsilon)[:, None]
    qkv_act = projected.astype(jnp.bfloat16)
    local_head_output = offsets.shape[0]
    fields = qkv_act.reshape(ENCODER_SLOTS, local_head_output, 3, HEAD_WIDTH)
    query_rows = fields[:, :, 0, :]
    keys_local = fields[:, :, 1, :]
    values_local = fields[:, :, 2, :]
    scale_factor = HEAD_WIDTH ** (-0.5)
    row_selector = (jnp.arange(DILATION_STEP, dtype=jnp.int32)[None, :] == offsets[:, None]).astype(
        jnp.float32
    )
    selected_rows = ENCODER_SLOTS // DILATION_STEP

    def select_rows(slide_field):
        reshaped_rows = slide_field.astype(jnp.float32).reshape(
            selected_rows, DILATION_STEP, local_head_output, HEAD_WIDTH
        )
        return jnp.einsum("rdhe,hd->rhe", reshaped_rows, row_selector).astype(jnp.bfloat16)

    query_sel = select_rows(query_rows)
    package = jnp.concatenate([select_rows(keys_local), select_rows(values_local)], axis=2).reshape(
        selected_rows, local_head_output * 2 * HEAD_WIDTH
    )
    portion = gather_seq(package)
    parts_kv = portion.reshape(portion.shape[0], local_head_output, 2, HEAD_WIDTH)
    scores = (
        jnp.einsum(
            "qhe,khe->hqk", query_sel, parts_kv[:, :, 0, :], preferred_element_type=jnp.float32
        )
        * scale_factor
    )
    weights = jnp.exp(scores)
    numer = jnp.einsum(
        "hqk,khe->hqe",
        weights.astype(jnp.bfloat16),
        parts_kv[:, :, 1, :],
        preferred_element_type=jnp.float32,
    )
    remote_den = jnp.sum(weights, axis=-1)
    scores = (
        jnp.einsum("qhe,khe->hqk", query_rows, keys_local, preferred_element_type=jnp.float32)
        * scale_factor
    )
    weights = jnp.exp(scores)
    local_num = jnp.einsum(
        "hqk,khe->hqe",
        weights.astype(jnp.bfloat16),
        values_local,
        preferred_element_type=jnp.float32,
    )
    local_den = jnp.sum(weights, axis=-1)
    spread_num = jnp.einsum("hre,hd->hrde", numer, row_selector).reshape(
        local_head_output, ENCODER_SLOTS, HEAD_WIDTH
    )
    spread_den = jnp.einsum("hr,hd->hrd", remote_den, row_selector).reshape(
        local_head_output, ENCODER_SLOTS
    )
    result = (local_num + spread_num) / (local_den + spread_den)[..., None]
    return (
        jnp.transpose(result, (1, 0, 2))
        .reshape(ENCODER_SLOTS, local_head_output * HEAD_WIDTH)
        .astype(jnp.bfloat16)
    )


def swap(array, axis, distance):
    size = lax.axis_size(axis)
    return lax.ppermute(array, axis, [(i, i ^ distance) for i in range(size)])


def block_at(array, index, size, axis):
    return lax.dynamic_slice_in_dim(array, index * size, size, axis)


def call(body, outs, inputs, spaces=None, scratch=(), copies=0, megabytes=40):
    spaces = spaces or [pltpu.VMEM] * len(inputs)
    scratch = list(scratch)
    if copies:
        scratch.append(pltpu.SemaphoreType.DMA((copies,)))
    return pl.pallas_call(
        body,
        out_shape=[jax.ShapeDtypeStruct(shape, kind) for shape, kind in outs],
        in_specs=[pl.BlockSpec(memory_space=space) for space in spaces],
        out_specs=[pl.BlockSpec(memory_space=pltpu.VMEM)] * len(outs),
        scratch_shapes=scratch,
        compiler_params=pltpu.CompilerParams(vmem_limit_bytes=megabytes * 1024 * 1024),
    )(*inputs)


def at(index, size):
    return pl.ds(pl.multiple_of(index * size, size), size)


def place():
    return tuple(lax.axis_index(name) for name in ("seq", "mp", "groups"))


def column_block(seq, mp):
    step = jnp.where(mp == 2, seq + 1, seq + 3) & 3
    return jnp.where(mp < 2, seq ^ (2 * mp), step)


def column_user(seq, mp):
    step = jnp.where(mp == 2, seq + 3, seq + 1) & 3
    return jnp.where(mp < 2, seq ^ (2 * mp), step)


def copier(sems, group):
    copies, used = [], [0]

    def copy(source, target, other=None):
        started = pltpu.make_async_copy(source, target, sems.at[used[0]])
        if other is None:
            started.start()
        else:
            second = pltpu.make_async_copy(other, target, sems.at[used[0]])
            pl.when(group == 0)(started.start)
            pl.when(group != 0)(second.start)
        copies.append(started)
        used[0] += 1

    return copies, copy


def normalise(rows, part, gain):
    values = rows[...].astype(jnp.float32)
    squares = jnp.sum(values * values, axis=1, keepdims=True)
    inverse = lax.rsqrt(squares * (1.0 / D_ENC) + epsilon)
    return (part.astype(jnp.float32) * inverse * gain[None, :]).astype(jnp.bfloat16)


def cut_first_body(
    count, tiles, w_gate, w_up, gain, first_out, second_out, quarter, held, sems
):
    seq, mp, group = place()
    copies, copy = copier(sems, group)
    half, units = w_gate.shape[0] // 2, w_gate.shape[1] // count
    features = quarter.shape[1]
    copy(tiles, held)
    for i in range(2):
        span = pl.ds(i * half, half), at(seq ^ 2, units)
        columns = pl.ds(features + i * units, units)
        copy(w_gate.at[span], second_out.at[:, columns], w_up.at[span])
        span = pl.ds(i * half, half), at(seq ^ 1, units)
        for k, weight in enumerate((w_gate, w_up)):
            columns = pl.ds(features + (2 * i + k) * units, units)
            copy(weight.at[span], first_out.at[:, columns])
    copies.pop(0).wait()
    columns = at(mp, features)
    own_columns = normalise(held, held[:, columns], gain[columns])
    second_out[:, :features] = own_columns
    first_out[:, :features] = own_columns
    quarter[...] = own_columns
    for started in copies:
        started.wait()


def cut_second_body(
    count, tiles, w_gate, w_up, w_down, gain, third_out, kept, near, far, normed, residual, held, sems
):
    seq, mp, group = place()
    copies, copy = copier(sems, group)
    half, units = w_gate.shape[0] // 2, w_gate.shape[1] // count
    copy(tiles, held)
    part = units // 2
    for j, target in ((2, far), (0, near)):
        rows = at(column_user(seq, mp ^ j) * 2 + group, part)
        copy(w_down.at[rows, :], target.at[pl.ds(0, part), :])
        rows = at(column_user(seq, mp ^ (j + 1)), units)
        copy(w_down.at[rows, :], target.at[pl.ds(part, units), :])
    for i in range(2):
        span = pl.ds(i * half, half), at(seq ^ 3, units)
        copy(w_gate.at[span], third_out.at[:, pl.ds(i * units, units)], w_up.at[span])
    for i, weight in enumerate((w_gate, w_up)):
        copy(weight.at[:, at(seq, units)], kept.at[:, pl.ds(i * units, units)])
    copies.pop(0).wait()
    normed[...] = normalise(held, held[...], gain[...])
    residual[...] = held[:, at(column_block(seq, mp), residual.shape[1])]
    for started in copies:
        started.wait()


def restack_body(second, third, first, stacked, columns):
    features = stacked.shape[2]
    stacked[0] = first[:, :features]
    stacked[1] = second[:, :features]
    stacked[2] = third[...]
    columns[...] = second[:, features:]


def pair_body(near, far, even, odd):
    for i, rows in enumerate((near, far)):
        even[i] = rows[: even.shape[1], :]
        odd[i] = rows[even.shape[1] :, :]


def routes_body(count, counts, offsets, dest, dest_row, routes):
    seq, _, _ = place()
    rows = dest_row.shape[1]
    capacity = ENCODER_SLOTS // count
    later = lax.broadcasted_iota(jnp.int32, (rows, rows), 1)
    earlier = lax.broadcasted_iota(jnp.int32, (rows, rows), 0)
    same = (dest[...] == dest_row[...]) & (earlier < later)
    rank = jnp.sum(jnp.where(same, 1, 0), axis=0, keepdims=True)
    live = lax.broadcasted_iota(jnp.int32, (1, rows), 1) < counts[0]
    codes = jnp.where(live, dest_row[...] * capacity + rank, -1)

    def chosen(wanted):
        return jnp.where(codes == wanted, 1.0, 0.0).astype(jnp.bfloat16)

    slot = lax.broadcasted_iota(jnp.int32, (capacity, rows), 0)
    for d in range(count):
        routes[pl.ds(d * capacity, capacity), :] = chosen((seq ^ d) * capacity + slot)
    per_block = capacity // DILATION_STEP
    spread = count * per_block
    index = lax.broadcasted_iota(jnp.int32, (spread, rows), 0)
    wanted = (index // per_block) * capacity + (index % per_block) * DILATION_STEP
    for h in range(offsets.shape[0]):
        routes[pl.ds(count * capacity + h * spread, spread), :] = chosen(wanted + offsets[h])


def hidden_body(count, normed, own, far, near, near_far, kept, next_in, *refs):
    (second, second_other, third, third_other), (out, weights) = refs[:4], refs[4:]
    seq, mp, group = place()
    depth, units = weights.shape[2:]
    half = depth // 2
    rows = normed.shape[0]
    for k in range(2):
        weights[k, seq] = kept[:, k * units : (k + 1) * units]
        for i in range(2):
            start = own.shape[2] + (2 * i + k) * units
            span = pl.ds(i * half, half)
            weights[k, seq ^ 1, span, :] = next_in[:, start : start + units]
    for d, mine, other in ((2, second, second_other), (3, third, third_other)):
        for i in range(2):
            span, columns = pl.ds(i * half, half), slice(i * units, (i + 1) * units)
            weights[group, seq ^ d, span, :] = mine[:, columns]
            weights[1 - group, seq ^ d, span, :] = other[:, columns]
    for d in range(count):
        if d == 0:
            pieces = [(normed[:, q * depth : (q + 1) * depth], q) for q in range(count)]
        else:
            pieces = [(own[d - 1], mp), (near[d - 1], mp ^ 1)]
            pieces += [(far[d - 1], mp ^ 2), (near_far[d - 1], mp ^ 3)]
        gate_act, up_act = (
            sum(
                jnp.dot(piece, weights[k, index], preferred_element_type=jnp.float32)
                for piece, index in pieces
            )
            for k in range(2)
        )
        gated = gate_act * jax.nn.sigmoid(gate_act) * up_act
        out[pl.ds(d * rows, rows), :] = gated.astype(jnp.bfloat16)


def down_body(residual, own, far, near, near_far, even, even_other, odd, *outs):
    _, _, group = place()
    rows = outs[0].shape[0]
    weights = [None, odd[0], None, odd[1]]
    for j in range(2):
        mine, other = even[j], even_other[j]
        low, high = jnp.where(group == 0, mine, other), jnp.where(group == 0, other, mine)
        weights[2 * j] = jnp.concatenate([low, high], axis=0)
    for i, out in enumerate(outs):
        total = residual[...].astype(jnp.float32) if i == 0 else 0.0
        for j, piece in enumerate((own, near, far, near_far)):
            total += jnp.dot(
                piece[pl.ds(i * rows, rows), :], weights[j], preferred_element_type=jnp.float32
            )
        out[...] = total.astype(out.dtype)


def sum_body(own, *refs):
    parts, out = refs[:-1], refs[-1]
    total = own[...] + sum(part[...].astype(jnp.float32) for part in parts)
    out[...] = total.astype(out.dtype)


def project_body(count, gain, routes, w_qkv_t, own, far, near, near_far, *outs):
    seq, mp, _ = place()
    features = own.shape[1]
    capacity = outs[0].shape[0]
    heads = w_qkv_t.shape[0] // (3 * HEAD_WIDTH)
    squares, total = 0.0, 0.0
    for j, piece in enumerate((own, near, far, near_far)):
        index = column_block(seq, mp ^ j)
        v = piece[...].astype(jnp.float32)
        squares += jnp.sum(v * v, axis=1, keepdims=True)
        scaled = (v * gain[:, at(index, features)]).astype(jnp.bfloat16)
        total += lax.dot_general(
            scaled,
            w_qkv_t[:, at(index, features)],
            (((1,), (1,)), ((), ())),
            preferred_element_type=jnp.float32,
        )
    projected = (total * lax.rsqrt(squares * (1.0 / D_ENC) + epsilon)).astype(jnp.bfloat16)
    routed = jnp.dot(routes[...], projected, preferred_element_type=jnp.float32)
    routed = routed.astype(jnp.bfloat16)
    width = projected.shape[1]
    spread = capacity // 2
    for d, out in enumerate(outs):
        out[:, :width] = routed[d * capacity : (d + 1) * capacity]
    for h in range(heads):
        first = count * capacity + h * spread
        for i in range(2):
            start = (3 * h + 1 + i) * HEAD_WIDTH
            piece = routed[first : first + spread, start : start + HEAD_WIDTH]
            for out in outs:
                span = slice(width + h * HEAD_WIDTH, width + (h + 1) * HEAD_WIDTH)
                out[i * spread : (i + 1) * spread, span] = piece


def attend_body(count, offsets, *refs):
    packages, out, rows = refs[:count], refs[count], refs[count + 1]
    seq, _, _ = place()
    capacity = packages[0].shape[0]
    heads = offsets.shape[0]
    width = heads * 3 * HEAD_WIDTH
    for d, package in zip(ORDER, packages):
        rows[at(seq ^ d, capacity), :] = package[:, :width]
    far = [package[:, width:] for package in packages]
    half = capacity // 2
    far_keys = jnp.concatenate([f[:half] for f in far], axis=0)
    far_values = jnp.concatenate([f[half:] for f in far], axis=0)
    residue = lax.broadcasted_iota(jnp.int32, (1, out.shape[1]), 1) % DILATION_STEP
    scale_factor = HEAD_WIDTH ** (-0.5)

    local = out.shape[1]
    for h in range(heads):
        query, key, value = (
            rows[:, pl.ds((3 * h + i) * HEAD_WIDTH, HEAD_WIDTH)] for i in range(3)
        )
        span = slice(h * HEAD_WIDTH, (h + 1) * HEAD_WIDTH)
        keys = jnp.concatenate([key, far_keys[:, span]], axis=0)
        values = jnp.concatenate([value, far_values[:, span]], axis=0)
        scores = lax.dot_general(
            keys, query, (((1,), (1,)), ((), ())), preferred_element_type=jnp.float32
        )
        weights = jnp.exp(scores * scale_factor)
        dilated = jnp.where(residue == offsets[h], weights[local:], 0.0)
        weights = jnp.concatenate([weights[:local], dilated], axis=0)
        numer = lax.dot_general(
            values,
            weights.astype(jnp.bfloat16),
            (((0,), (0,)), ((), ())),
            preferred_element_type=jnp.float32,
        )
        denom = jnp.sum(weights, axis=0, keepdims=True)
        out[span, :] = (numer / denom).astype(jnp.bfloat16)


def spread_mp(own, beside=None):
    far = swap(own, "mp", 2)
    relayed = far if beside is None else lax.optimization_barrier((far, beside))[0]
    return far, swap(own, "mp", 1), swap(relayed, "mp", 1)


def split_hidden_plan(
    tiles, counts, dest, gain_enc, w_gate, w_up, w_down, gain_slide, w_qkv, offsets
):
    count, mp_size = lax.axis_size("seq"), lax.axis_size("mp")
    seq, mp = lax.axis_index("seq"), lax.axis_index("mp")
    capacity = ENCODER_SLOTS // count
    tile_rows = tiles.shape[0]
    features = D_ENC // mp_size
    depth = w_gate.shape[0]
    units = w_gate.shape[1] // count
    heads = offsets.shape[0]
    bf16 = jnp.bfloat16
    vmem, smem = pltpu.VMEM, pltpu.SMEM

    first_out, second_out, quarter = call(
        functools.partial(cut_first_body, count),
        [
            ((tile_rows, features + 4 * units), bf16),
            ((tile_rows, features + 2 * units), bf16),
            ((tile_rows, features), bf16),
        ],
        (tiles, w_gate, w_up, gain_enc),
        spaces=[pltpu.HBM] * 3 + [vmem],
        copies=7,
        scratch=[pltpu.VMEM((tile_rows, D_ENC), bf16)],
        megabytes=57,
    )
    third_out, kept, down_near, down_far, normed, residual = call(
        functools.partial(cut_second_body, count),
        [
            ((tile_rows, 2 * units), bf16),
            ((depth, 2 * units), bf16),
            ((3 * units // 2, features), bf16),
            ((3 * units // 2, features), bf16),
            ((tile_rows, D_ENC), bf16),
            ((tile_rows, features), bf16),
        ],
        (tiles, w_gate, w_up, w_down, gain_enc),
        spaces=[pltpu.HBM] * 4 + [vmem],
        scratch=[pltpu.VMEM((tile_rows, D_ENC), bf16)],
        copies=9,
        megabytes=57,
    )
    routes = call(
        functools.partial(routes_body, count),
        [((ENCODER_SLOTS + heads * ENCODER_SLOTS // DILATION_STEP, tile_rows), bf16)],
        (counts, offsets, dest, dest.reshape(1, tile_rows)),
        spaces=[smem, smem, vmem, vmem],
    )[0]

    second_in, third_in = swap(second_out, "seq", 2), swap(quarter, "seq", 3)
    arrived = second_in, third_in, swap(first_out, "seq", 1)
    from_far = swap(down_far, "mp", 2)
    arrived, from_far, routes = lax.optimization_barrier((arrived, from_far, routes))
    own, columns = call(
        restack_body,
        [
            ((count - 1, tile_rows, features), bf16),
            ((tile_rows, 2 * units), bf16),
        ],
        arrived,
    )
    third_out, down_near, _ = lax.optimization_barrier((third_out, down_near, own))
    down_send = call(
        pair_body,
        [((2, units // 2, features), bf16), ((2, units, features), bf16)],
        (down_near, from_far),
    )
    third, others, far, near, down_send = lax.optimization_barrier(
        (
            swap(third_out, "seq", 3),
            swap(columns, "groups", 1),
            swap(own, "mp", 2),
            swap(own, "mp", 1),
            down_send,
        )
    )
    halves = columns, others, third, swap(third, "groups", 1)
    spread = far, near, swap(far, "mp", 1)
    parts = []
    for j in range(2):
        perm = []
        for s in range(count):
            for m in range(mp_size):
                k = m ^ j
                user = (s ^ 2 * k) if k < 2 else (s + 2 * k - 5) % count
                perm.append((s * mp_size + m, user * mp_size + k))
        parts.append(lax.ppermute(down_send[j], ("seq", "mp"), perm))
    hidden = call(
        functools.partial(hidden_body, count),
        [((count * tile_rows, units), bf16)],
        (normed, own, *spread, kept, arrived[2], *halves),
        scratch=[
            pltpu.VMEM((2, count, depth, units), bf16),
        ],
    )[0]
    even, odd = parts
    even_other = swap(even, "groups", 1)
    sums = call(
        down_body,
        [((tile_rows, features), kind) for kind in (jnp.float32, bf16, bf16, bf16)],
        (residual, hidden, *spread_mp(hidden, even_other), even, even_other, odd),
    )
    holder = [0, 2, 1, 3]

    def to_owner(part, d):
        perm = []
        for s in range(count):
            for m in range(mp_size):
                owner = s ^ d
                perm.append((s * mp_size + m, owner * mp_size + holder[(s + holder[m] - owner) % count]))
        return lax.ppermute(part, ("seq", "mp"), perm)

    arrived = [to_owner(sums[d], d) for d in (2, 3, 1)]
    embedded_cols = call(
        sum_body, [((tile_rows, features), bf16)], (sums[0], *arrived)
    )[0]

    packages = call(
        functools.partial(project_body, count),
        [((capacity, 4 * heads * HEAD_WIDTH), bf16)] * count,
        (gain_slide[None, :], routes, w_qkv.T, embedded_cols, *spread_mp(embedded_cols)),
    )
    packages = [swap(packages[d], "seq", d) for d in ORDER[:-1]] + [packages[0]]
    return call(
        functools.partial(attend_body, count),
        [((heads * HEAD_WIDTH, ENCODER_SLOTS), bf16)],
        (offsets, *packages),
        spaces=[smem] + [vmem] * count,
        scratch=[pltpu.VMEM((ENCODER_SLOTS, 3 * heads * HEAD_WIDTH), bf16)],
    )[0].T


def on_device(*arrays):
    sizes = lax.axis_size("groups"), lax.axis_size("seq"), lax.axis_size("mp")
    if sizes == (2, 4, 4):
        return split_hidden_plan(*arrays)
    return gathered_plan(*arrays)


def solution(mesh):
    return jax.shard_map(
        on_device,
        mesh=mesh,
        in_specs=(
            P(("groups", "seq"), None),
            P(("groups", "seq")),
            P(("groups", "seq"), None),
            P(),
            P("seq", "mp"),
            P("seq", "mp"),
            P("mp", "seq"),
            P(),
            P(None, "mp"),
            P("mp"),
        ),
        out_specs=P(("groups", "seq"), "mp"),
        check_vma=False,
    )
```

```python
import functools

import jax
import jax.numpy as jnp
from jax import lax
from jax.experimental import pallas as pl
from jax.experimental.pallas import tpu as pltpu
from jax.sharding import PartitionSpec as P

D_ENC = 1536
HEAD_WIDTH = 64
DILATION_STEP = 8
ENCODER_SLOTS = 256
ORDER = (2, 1, 3, 0)


epsilon = 1e-05


def gather_seq(package):
    count = lax.axis_size("seq")
    if count & (count - 1) == 0 and count <= 4:
        return jnp.concatenate([package] + [swap(package, "seq", d) for d in range(1, count)])
    return lax.all_gather(package, "seq", axis=0, tiled=True)


def gathered_plan(tiles, counts, dest, gain_enc, w_gate, w_up, w_down, gain_slide, w_qkv, offsets):
    seq_count = lax.axis_size("seq")
    capacity = ENCODER_SLOTS // seq_count
    tile_rows = tiles.shape[0]
    target = dest[:, 0]
    live_rows = jnp.arange(tile_rows, dtype=jnp.int32) < counts[0]
    chosen = (
        (target[:, None] == jnp.arange(seq_count, dtype=jnp.int32)[None, :]) & live_rows[:, None]
    ).astype(jnp.int32)
    arrival = jnp.sum((jnp.cumsum(chosen, axis=0) - chosen) * chosen, axis=1)
    slot_index = jnp.where(live_rows, target * capacity + arrival, ENCODER_SLOTS)
    outgoing = (
        jnp.zeros((ENCODER_SLOTS, D_ENC), jnp.bfloat16).at[slot_index].set(tiles, mode="drop")
    )
    arrived = lax.all_to_all(outgoing, "seq", split_axis=0, concat_axis=0, tiled=True)
    arrived_f = arrived.astype(jnp.float32)
    inverse = lax.rsqrt(jnp.mean(arrived_f * arrived_f, axis=-1, keepdims=True) + epsilon)
    normed = (arrived_f * inverse * gain_enc).astype(jnp.bfloat16)

    def add_rows(portion):
        return jnp.dot(normed, portion, preferred_element_type=jnp.float32)

    gate_act = add_rows(lax.all_gather(w_gate, "seq", axis=0, tiled=True))
    up_act = add_rows(lax.all_gather(w_up, "seq", axis=0, tiled=True))
    hidden = (jax.nn.silu(gate_act) * up_act).astype(jnp.bfloat16)
    partial_out = jnp.dot(
        hidden,
        lax.all_gather(w_down, "seq", axis=1, tiled=True),
        preferred_element_type=jnp.float32,
    )
    share = lax.psum_scatter(partial_out, "mp", scatter_dimension=1, tiled=True)
    share_width = share.shape[1]
    own_cols = lax.dynamic_slice_in_dim(
        arrived_f, lax.axis_index("mp") * share_width, share_width, 1
    )
    embedded_cols = (own_cols + share).astype(jnp.bfloat16)
    embedded = lax.all_gather(embedded_cols, "mp", axis=1, tiled=True)
    return slide_layer(embedded, gain_slide, w_qkv, offsets)


def slide_layer(embedded, gain_slide, w_qkv, offsets):
    portion_f = embedded.astype(jnp.float32)
    accumulated = jnp.dot(
        (portion_f * gain_slide).astype(jnp.bfloat16), w_qkv, preferred_element_type=jnp.float32
    )
    accumulated, squares = (accumulated, jnp.sum(portion_f * portion_f, axis=1))
    projected = accumulated * lax.rsqrt(squares / D_ENC + epsilon)[:, None]
    qkv_act = projected.astype(jnp.bfloat16)
    local_head_output = offsets.shape[0]
    fields = qkv_act.reshape(ENCODER_SLOTS, local_head_output, 3, HEAD_WIDTH)
    query_rows = fields[:, :, 0, :]
    keys_local = fields[:, :, 1, :]
    values_local = fields[:, :, 2, :]
    scale_factor = HEAD_WIDTH ** (-0.5)
    row_selector = (jnp.arange(DILATION_STEP, dtype=jnp.int32)[None, :] == offsets[:, None]).astype(
        jnp.float32
    )
    selected_rows = ENCODER_SLOTS // DILATION_STEP

    def select_rows(slide_field):
        reshaped_rows = slide_field.astype(jnp.float32).reshape(
            selected_rows, DILATION_STEP, local_head_output, HEAD_WIDTH
        )
        return jnp.einsum("rdhe,hd->rhe", reshaped_rows, row_selector).astype(jnp.bfloat16)

    query_sel = select_rows(query_rows)
    package = jnp.concatenate([select_rows(keys_local), select_rows(values_local)], axis=2).reshape(
        selected_rows, local_head_output * 2 * HEAD_WIDTH
    )
    portion = gather_seq(package)
    parts_kv = portion.reshape(portion.shape[0], local_head_output, 2, HEAD_WIDTH)
    scores = (
        jnp.einsum(
            "qhe,khe->hqk", query_sel, parts_kv[:, :, 0, :], preferred_element_type=jnp.float32
        )
        * scale_factor
    )
    weights = jnp.exp(scores)
    numer = jnp.einsum(
        "hqk,khe->hqe",
        weights.astype(jnp.bfloat16),
        parts_kv[:, :, 1, :],
        preferred_element_type=jnp.float32,
    )
    remote_den = jnp.sum(weights, axis=-1)
    scores = (
        jnp.einsum("qhe,khe->hqk", query_rows, keys_local, preferred_element_type=jnp.float32)
        * scale_factor
    )
    weights = jnp.exp(scores)
    local_num = jnp.einsum(
        "hqk,khe->hqe",
        weights.astype(jnp.bfloat16),
        values_local,
        preferred_element_type=jnp.float32,
    )
    local_den = jnp.sum(weights, axis=-1)
    spread_num = jnp.einsum("hre,hd->hrde", numer, row_selector).reshape(
        local_head_output, ENCODER_SLOTS, HEAD_WIDTH
    )
    spread_den = jnp.einsum("hr,hd->hrd", remote_den, row_selector).reshape(
        local_head_output, ENCODER_SLOTS
    )
    result = (local_num + spread_num) / (local_den + spread_den)[..., None]
    return (
        jnp.transpose(result, (1, 0, 2))
        .reshape(ENCODER_SLOTS, local_head_output * HEAD_WIDTH)
        .astype(jnp.bfloat16)
    )


def swap(array, axis, distance):
    size = lax.axis_size(axis)
    return lax.ppermute(array, axis, [(i, i ^ distance) for i in range(size)])


def block_at(array, index, size, axis):
    return lax.dynamic_slice_in_dim(array, index * size, size, axis)


def call(body, outs, inputs, spaces=None, scratch=(), copies=0, megabytes=40):
    spaces = spaces or [pltpu.VMEM] * len(inputs)
    scratch = list(scratch)
    if copies:
        scratch.append(pltpu.SemaphoreType.DMA((copies,)))
    return pl.pallas_call(
        body,
        out_shape=[jax.ShapeDtypeStruct(shape, kind) for shape, kind in outs],
        in_specs=[pl.BlockSpec(memory_space=space) for space in spaces],
        out_specs=[pl.BlockSpec(memory_space=pltpu.VMEM)] * len(outs),
        scratch_shapes=scratch,
        compiler_params=pltpu.CompilerParams(vmem_limit_bytes=megabytes * 1024 * 1024),
    )(*inputs)


def at(index, size):
    return pl.ds(pl.multiple_of(index * size, size), size)


def place():
    return tuple(lax.axis_index(name) for name in ("seq", "mp", "groups"))


def column_block(seq, mp):
    step = jnp.where(mp == 2, seq + 1, seq + 3) & 3
    return jnp.where(mp < 2, seq ^ (2 * mp), step)


def column_user(seq, mp):
    step = jnp.where(mp == 2, seq + 3, seq + 1) & 3
    return jnp.where(mp < 2, seq ^ (2 * mp), step)


def copier(sems, group):
    copies, used = [], [0]

    def copy(source, target, other=None):
        started = pltpu.make_async_copy(source, target, sems.at[used[0]])
        if other is None:
            started.start()
        else:
            second = pltpu.make_async_copy(other, target, sems.at[used[0]])
            pl.when(group == 0)(started.start)
            pl.when(group != 0)(second.start)
        copies.append(started)
        used[0] += 1

    return copies, copy


def normalise(rows, part, gain):
    values = rows[...].astype(jnp.float32)
    squares = jnp.sum(values * values, axis=1, keepdims=True)
    inverse = lax.rsqrt(squares * (1.0 / D_ENC) + epsilon)
    return (part.astype(jnp.float32) * inverse * gain[None, :]).astype(jnp.bfloat16)


def cut_first_body(
    count, tiles, w_gate, w_up, gain, first_out, second_out, quarter, held, sems
):
    seq, mp, group = place()
    copies, copy = copier(sems, group)
    half, units = w_gate.shape[0] // 2, w_gate.shape[1] // count
    features = quarter.shape[1]
    copy(tiles, held)
    for i in range(2):
        span = pl.ds(i * half, half), at(seq ^ 2, units)
        columns = pl.ds(features + i * units, units)
        copy(w_gate.at[span], second_out.at[:, columns], w_up.at[span])
        span = pl.ds(i * half, half), at(seq ^ 1, units)
        for k, weight in enumerate((w_gate, w_up)):
            columns = pl.ds(features + (2 * i + k) * units, units)
            copy(weight.at[span], first_out.at[:, columns])
    copies.pop(0).wait()
    columns = at(mp, features)
    own_columns = normalise(held, held[:, columns], gain[columns])
    second_out[:, :features] = own_columns
    first_out[:, :features] = own_columns
    quarter[...] = own_columns
    for started in copies:
        started.wait()


def cut_second_body(
    count, tiles, w_gate, w_up, w_down, gain, third_out, kept, near, far, normed, residual, held, sems
):
    seq, mp, group = place()
    copies, copy = copier(sems, group)
    half, units = w_gate.shape[0] // 2, w_gate.shape[1] // count
    copy(tiles, held)
    part = units // 2
    for j, target in ((2, far), (0, near)):
        rows = at(column_user(seq, mp ^ j) * 2 + group, part)
        copy(w_down.at[rows, :], target.at[pl.ds(0, part), :])
        rows = at(column_user(seq, mp ^ (j + 1)), units)
        copy(w_down.at[rows, :], target.at[pl.ds(part, units), :])
    for i in range(2):
        span = pl.ds(i * half, half), at(seq ^ 3, units)
        copy(w_gate.at[span], third_out.at[:, pl.ds(i * units, units)], w_up.at[span])
    for i, weight in enumerate((w_gate, w_up)):
        copy(weight.at[:, at(seq, units)], kept.at[:, pl.ds(i * units, units)])
    copies.pop(0).wait()
    normed[...] = normalise(held, held[...], gain[...])
    residual[...] = held[:, at(column_block(seq, mp), residual.shape[1])]
    for started in copies:
        started.wait()


def restack_body(second, third, first, stacked, columns):
    features = stacked.shape[2]
    stacked[0] = first[:, :features]
    stacked[1] = second[:, :features]
    stacked[2] = third[...]
    columns[...] = second[:, features:]


def pair_body(near, far, even, odd):
    for i, rows in enumerate((near, far)):
        even[i] = rows[: even.shape[1], :]
        odd[i] = rows[even.shape[1] :, :]


def routes_body(count, counts, offsets, dest, dest_row, routes):
    seq, _, _ = place()
    rows = dest_row.shape[1]
    capacity = ENCODER_SLOTS // count
    later = lax.broadcasted_iota(jnp.int32, (rows, rows), 1)
    earlier = lax.broadcasted_iota(jnp.int32, (rows, rows), 0)
    same = (dest[...] == dest_row[...]) & (earlier < later)
    rank = jnp.sum(jnp.where(same, 1, 0), axis=0, keepdims=True)
    live = lax.broadcasted_iota(jnp.int32, (1, rows), 1) < counts[0]
    codes = jnp.where(live, dest_row[...] * capacity + rank, -1)

    def chosen(wanted):
        return jnp.where(codes == wanted, 1.0, 0.0).astype(jnp.bfloat16)

    slot = lax.broadcasted_iota(jnp.int32, (capacity, rows), 0)
    for d in range(count):
        routes[pl.ds(d * capacity, capacity), :] = chosen((seq ^ d) * capacity + slot)
    per_block = capacity // DILATION_STEP
    spread = count * per_block
    index = lax.broadcasted_iota(jnp.int32, (spread, rows), 0)
    wanted = (index // per_block) * capacity + (index % per_block) * DILATION_STEP
    for h in range(offsets.shape[0]):
        routes[pl.ds(count * capacity + h * spread, spread), :] = chosen(wanted + offsets[h])


def hidden_body(count, normed, own, far, near, near_far, kept, next_in, *refs):
    (second, second_other, third, third_other), (out, weights) = refs[:4], refs[4:]
    seq, mp, group = place()
    depth, units = weights.shape[2:]
    half = depth // 2
    rows = normed.shape[0]
    for k in range(2):
        weights[k, seq] = kept[:, k * units : (k + 1) * units]
        for i in range(2):
            start = own.shape[2] + (2 * i + k) * units
            span = pl.ds(i * half, half)
            weights[k, seq ^ 1, span, :] = next_in[:, start : start + units]
    for d, mine, other in ((2, second, second_other), (3, third, third_other)):
        for i in range(2):
            span, columns = pl.ds(i * half, half), slice(i * units, (i + 1) * units)
            weights[group, seq ^ d, span, :] = mine[:, columns]
            weights[1 - group, seq ^ d, span, :] = other[:, columns]
    for d in range(count):
        if d == 0:
            pieces = [(normed[:, q * depth : (q + 1) * depth], q) for q in range(count)]
        else:
            pieces = [(own[d - 1], mp), (near[d - 1], mp ^ 1)]
            pieces += [(far[d - 1], mp ^ 2), (near_far[d - 1], mp ^ 3)]
        gate_act, up_act = (
            sum(
                jnp.dot(piece, weights[k, index], preferred_element_type=jnp.float32)
                for piece, index in pieces
            )
            for k in range(2)
        )
        gated = gate_act * jax.nn.sigmoid(gate_act) * up_act
        out[pl.ds(d * rows, rows), :] = gated.astype(jnp.bfloat16)


def down_body(residual, own, far, near, near_far, even, even_other, odd, *outs):
    _, _, group = place()
    rows = outs[0].shape[0]
    weights = [None, odd[0], None, odd[1]]
    for j in range(2):
        mine, other = even[j], even_other[j]
        low, high = jnp.where(group == 0, mine, other), jnp.where(group == 0, other, mine)
        weights[2 * j] = jnp.concatenate([low, high], axis=0)
    for i, out in enumerate(outs):
        total = residual[...].astype(jnp.float32) if i == 0 else 0.0
        for j, piece in enumerate((own, near, far, near_far)):
            total += jnp.dot(
                piece[pl.ds(i * rows, rows), :], weights[j], preferred_element_type=jnp.float32
            )
        out[...] = total.astype(out.dtype)


def sum_body(own, *refs):
    parts, out = refs[:-1], refs[-1]
    total = own[...] + sum(part[...].astype(jnp.float32) for part in parts)
    out[...] = total.astype(out.dtype)


def project_body(count, gain, routes, w_qkv_t, own, far, near, near_far, *outs):
    seq, mp, _ = place()
    features = own.shape[1]
    capacity = outs[0].shape[0]
    heads = w_qkv_t.shape[0] // (3 * HEAD_WIDTH)
    squares, total = 0.0, 0.0
    for j, piece in enumerate((own, near, far, near_far)):
        index = column_block(seq, mp ^ j)
        v = piece[...].astype(jnp.float32)
        squares += jnp.sum(v * v, axis=1, keepdims=True)
        scaled = (v * gain[:, at(index, features)]).astype(jnp.bfloat16)
        total += lax.dot_general(
            scaled,
            w_qkv_t[:, at(index, features)],
            (((1,), (1,)), ((), ())),
            preferred_element_type=jnp.float32,
        )
    projected = (total * lax.rsqrt(squares * (1.0 / D_ENC) + epsilon)).astype(jnp.bfloat16)
    routed = jnp.dot(routes[...], projected, preferred_element_type=jnp.float32)
    routed = routed.astype(jnp.bfloat16)
    width = projected.shape[1]
    spread = capacity // 2
    for d, out in enumerate(outs):
        out[:, :width] = routed[d * capacity : (d + 1) * capacity]
    for h in range(heads):
        first = count * capacity + h * spread
        for i in range(2):
            start = (3 * h + 1 + i) * HEAD_WIDTH
            piece = routed[first : first + spread, start : start + HEAD_WIDTH]
            for out in outs:
                span = slice(width + h * HEAD_WIDTH, width + (h + 1) * HEAD_WIDTH)
                out[i * spread : (i + 1) * spread, span] = piece


def attend_body(count, offsets, *refs):
    packages, out, rows = refs[:count], refs[count], refs[count + 1]
    seq, _, _ = place()
    capacity = packages[0].shape[0]
    heads = offsets.shape[0]
    width = heads * 3 * HEAD_WIDTH
    for d, package in zip(ORDER, packages):
        rows[at(seq ^ d, capacity), :] = package[:, :width]
    far = [package[:, width:] for package in packages]
    half = capacity // 2
    far_keys = jnp.concatenate([f[:half] for f in far], axis=0)
    far_values = jnp.concatenate([f[half:] for f in far], axis=0)
    residue = lax.broadcasted_iota(jnp.int32, (1, out.shape[1]), 1) % DILATION_STEP
    scale_factor = HEAD_WIDTH ** (-0.5)

    local = out.shape[1]
    for h in range(heads):
        query, key, value = (
            rows[:, pl.ds((3 * h + i) * HEAD_WIDTH, HEAD_WIDTH)] for i in range(3)
        )
        span = slice(h * HEAD_WIDTH, (h + 1) * HEAD_WIDTH)
        keys = jnp.concatenate([key, far_keys[:, span]], axis=0)
        values = jnp.concatenate([value, far_values[:, span]], axis=0)
        scores = lax.dot_general(
            keys, query, (((1,), (1,)), ((), ())), preferred_element_type=jnp.float32
        )
        weights = jnp.exp(scores * scale_factor)
        dilated = jnp.where(residue == offsets[h], weights[local:], 0.0)
        weights = jnp.concatenate([weights[:local], dilated], axis=0)
        numer = lax.dot_general(
            values,
            weights.astype(jnp.bfloat16),
            (((0,), (0,)), ((), ())),
            preferred_element_type=jnp.float32,
        )
        denom = jnp.sum(weights, axis=0, keepdims=True)
        out[span, :] = (numer / denom).astype(jnp.bfloat16)


def spread_mp(own, beside=None):
    far = swap(own, "mp", 2)
    relayed = far if beside is None else lax.optimization_barrier((far, beside))[0]
    return far, swap(own, "mp", 1), swap(relayed, "mp", 1)


def split_hidden_plan(
    tiles, counts, dest, gain_enc, w_gate, w_up, w_down, gain_slide, w_qkv, offsets
):
    count, mp_size = lax.axis_size("seq"), lax.axis_size("mp")
    seq, mp = lax.axis_index("seq"), lax.axis_index("mp")
    capacity = ENCODER_SLOTS // count
    tile_rows = tiles.shape[0]
    features = D_ENC // mp_size
    depth = w_gate.shape[0]
    units = w_gate.shape[1] // count
    heads = offsets.shape[0]
    bf16 = jnp.bfloat16
    vmem, smem = pltpu.VMEM, pltpu.SMEM

    first_out, second_out, quarter = call(
        functools.partial(cut_first_body, count),
        [
            ((tile_rows, features + 4 * units), bf16),
            ((tile_rows, features + 2 * units), bf16),
            ((tile_rows, features), bf16),
        ],
        (tiles, w_gate, w_up, gain_enc),
        spaces=[pltpu.HBM] * 3 + [vmem],
        copies=7,
        scratch=[pltpu.VMEM((tile_rows, D_ENC), bf16)],
        megabytes=57,
    )
    third_out, kept, down_near, down_far, normed, residual = call(
        functools.partial(cut_second_body, count),
        [
            ((tile_rows, 2 * units), bf16),
            ((depth, 2 * units), bf16),
            ((3 * units // 2, features), bf16),
            ((3 * units // 2, features), bf16),
            ((tile_rows, D_ENC), bf16),
            ((tile_rows, features), bf16),
        ],
        (tiles, w_gate, w_up, w_down, gain_enc),
        spaces=[pltpu.HBM] * 4 + [vmem],
        scratch=[pltpu.VMEM((tile_rows, D_ENC), bf16)],
        copies=9,
        megabytes=57,
    )
    routes = call(
        functools.partial(routes_body, count),
        [((ENCODER_SLOTS + heads * ENCODER_SLOTS // DILATION_STEP, tile_rows), bf16)],
        (counts, offsets, dest, dest.reshape(1, tile_rows)),
        spaces=[smem, smem, vmem, vmem],
    )[0]

    second_in, third_in = swap(second_out, "seq", 2), swap(quarter, "seq", 3)
    arrived = second_in, third_in, swap(first_out, "seq", 1)
    from_far = swap(down_far, "mp", 2)
    arrived, from_far, routes = lax.optimization_barrier((arrived, from_far, routes))
    own, columns = call(
        restack_body,
        [
            ((count - 1, tile_rows, features), bf16),
            ((tile_rows, 2 * units), bf16),
        ],
        arrived,
    )
    third_out, down_near, _ = lax.optimization_barrier((third_out, down_near, own))
    down_send = call(
        pair_body,
        [((2, units // 2, features), bf16), ((2, units, features), bf16)],
        (down_near, from_far),
    )
    third, others, far, near, down_send = lax.optimization_barrier(
        (
            swap(third_out, "seq", 3),
            swap(columns, "groups", 1),
            swap(own, "mp", 2),
            swap(own, "mp", 1),
            down_send,
        )
    )
    halves = columns, others, third, swap(third, "groups", 1)
    spread = far, near, swap(far, "mp", 1)
    parts = []
    for j in range(2):
        perm = []
        for s in range(count):
            for m in range(mp_size):
                k = m ^ j
                user = (s ^ 2 * k) if k < 2 else (s + 2 * k - 5) % count
                perm.append((s * mp_size + m, user * mp_size + k))
        parts.append(lax.ppermute(down_send[j], ("seq", "mp"), perm))
    hidden = call(
        functools.partial(hidden_body, count),
        [((count * tile_rows, units), bf16)],
        (normed, own, *spread, kept, arrived[2], *halves),
        scratch=[
            pltpu.VMEM((2, count, depth, units), bf16),
        ],
    )[0]
    even, odd = parts
    even_other = swap(even, "groups", 1)
    sums = call(
        down_body,
        [((tile_rows, features), kind) for kind in (jnp.float32, bf16, bf16, bf16)],
        (residual, hidden, *spread_mp(hidden, even_other), even, even_other, odd),
    )
    holder = [0, 2, 1, 3]

    def to_owner(part, d):
        perm = []
        for s in range(count):
            for m in range(mp_size):
                owner = s ^ d
                perm.append((s * mp_size + m, owner * mp_size + holder[(s + holder[m] - owner) % count]))
        return lax.ppermute(part, ("seq", "mp"), perm)

    arrived = [to_owner(sums[d], d) for d in (2, 1, 3)]
    embedded_cols = call(
        sum_body, [((tile_rows, features), bf16)], (sums[0], *arrived)
    )[0]

    packages = call(
        functools.partial(project_body, count),
        [((capacity, 4 * heads * HEAD_WIDTH), bf16)] * count,
        (gain_slide[None, :], routes, w_qkv.T, embedded_cols, *spread_mp(embedded_cols)),
    )
    packages = [swap(packages[d], "seq", d) for d in ORDER[:-1]] + [packages[0]]
    return call(
        functools.partial(attend_body, count),
        [((heads * HEAD_WIDTH, ENCODER_SLOTS), bf16)],
        (offsets, *packages),
        spaces=[smem] + [vmem] * count,
        scratch=[pltpu.VMEM((ENCODER_SLOTS, 3 * heads * HEAD_WIDTH), bf16)],
    )[0].T


def on_device(*arrays):
    sizes = lax.axis_size("groups"), lax.axis_size("seq"), lax.axis_size("mp")
    if sizes == (2, 4, 4):
        return split_hidden_plan(*arrays)
    return gathered_plan(*arrays)


def solution(mesh):
    return jax.shard_map(
        on_device,
        mesh=mesh,
        in_specs=(
            P(("groups", "seq"), None),
            P(("groups", "seq")),
            P(("groups", "seq"), None),
            P(),
            P("seq", "mp"),
            P("seq", "mp"),
            P("mp", "seq"),
            P(),
            P(None, "mp"),
            P("mp"),
        ),
        out_specs=P(("groups", "seq"), "mp"),
        check_vma=False,
    )
```

```python
import functools

import jax
import jax.numpy as jnp
from jax import lax
from jax.experimental import pallas as pl
from jax.experimental.pallas import tpu as pltpu
from jax.sharding import PartitionSpec as P

D_ENC = 1536
HEAD_WIDTH = 64
DILATION_STEP = 8
ENCODER_SLOTS = 256
ORDER = (2, 1, 3, 0)


epsilon = 1e-05


def gather_seq(package):
    count = lax.axis_size("seq")
    if count & (count - 1) == 0 and count <= 4:
        return jnp.concatenate([package] + [swap(package, "seq", d) for d in range(1, count)])
    return lax.all_gather(package, "seq", axis=0, tiled=True)


def gathered_plan(tiles, counts, dest, gain_enc, w_gate, w_up, w_down, gain_slide, w_qkv, offsets):
    seq_count = lax.axis_size("seq")
    capacity = ENCODER_SLOTS // seq_count
    tile_rows = tiles.shape[0]
    target = dest[:, 0]
    live_rows = jnp.arange(tile_rows, dtype=jnp.int32) < counts[0]
    chosen = (
        (target[:, None] == jnp.arange(seq_count, dtype=jnp.int32)[None, :]) & live_rows[:, None]
    ).astype(jnp.int32)
    arrival = jnp.sum((jnp.cumsum(chosen, axis=0) - chosen) * chosen, axis=1)
    slot_index = jnp.where(live_rows, target * capacity + arrival, ENCODER_SLOTS)
    outgoing = (
        jnp.zeros((ENCODER_SLOTS, D_ENC), jnp.bfloat16).at[slot_index].set(tiles, mode="drop")
    )
    arrived = lax.all_to_all(outgoing, "seq", split_axis=0, concat_axis=0, tiled=True)
    arrived_f = arrived.astype(jnp.float32)
    inverse = lax.rsqrt(jnp.mean(arrived_f * arrived_f, axis=-1, keepdims=True) + epsilon)
    normed = (arrived_f * inverse * gain_enc).astype(jnp.bfloat16)

    def add_rows(portion):
        return jnp.dot(normed, portion, preferred_element_type=jnp.float32)

    gate_act = add_rows(lax.all_gather(w_gate, "seq", axis=0, tiled=True))
    up_act = add_rows(lax.all_gather(w_up, "seq", axis=0, tiled=True))
    hidden = (jax.nn.silu(gate_act) * up_act).astype(jnp.bfloat16)
    partial_out = jnp.dot(
        hidden,
        lax.all_gather(w_down, "seq", axis=1, tiled=True),
        preferred_element_type=jnp.float32,
    )
    share = lax.psum_scatter(partial_out, "mp", scatter_dimension=1, tiled=True)
    share_width = share.shape[1]
    own_cols = lax.dynamic_slice_in_dim(
        arrived_f, lax.axis_index("mp") * share_width, share_width, 1
    )
    embedded_cols = (own_cols + share).astype(jnp.bfloat16)
    embedded = lax.all_gather(embedded_cols, "mp", axis=1, tiled=True)
    return slide_layer(embedded, gain_slide, w_qkv, offsets)


def slide_layer(embedded, gain_slide, w_qkv, offsets):
    portion_f = embedded.astype(jnp.float32)
    accumulated = jnp.dot(
        (portion_f * gain_slide).astype(jnp.bfloat16), w_qkv, preferred_element_type=jnp.float32
    )
    accumulated, squares = (accumulated, jnp.sum(portion_f * portion_f, axis=1))
    projected = accumulated * lax.rsqrt(squares / D_ENC + epsilon)[:, None]
    qkv_act = projected.astype(jnp.bfloat16)
    local_head_output = offsets.shape[0]
    fields = qkv_act.reshape(ENCODER_SLOTS, local_head_output, 3, HEAD_WIDTH)
    query_rows = fields[:, :, 0, :]
    keys_local = fields[:, :, 1, :]
    values_local = fields[:, :, 2, :]
    scale_factor = HEAD_WIDTH ** (-0.5)
    row_selector = (jnp.arange(DILATION_STEP, dtype=jnp.int32)[None, :] == offsets[:, None]).astype(
        jnp.float32
    )
    selected_rows = ENCODER_SLOTS // DILATION_STEP

    def select_rows(slide_field):
        reshaped_rows = slide_field.astype(jnp.float32).reshape(
            selected_rows, DILATION_STEP, local_head_output, HEAD_WIDTH
        )
        return jnp.einsum("rdhe,hd->rhe", reshaped_rows, row_selector).astype(jnp.bfloat16)

    query_sel = select_rows(query_rows)
    package = jnp.concatenate([select_rows(keys_local), select_rows(values_local)], axis=2).reshape(
        selected_rows, local_head_output * 2 * HEAD_WIDTH
    )
    portion = gather_seq(package)
    parts_kv = portion.reshape(portion.shape[0], local_head_output, 2, HEAD_WIDTH)
    scores = (
        jnp.einsum(
            "qhe,khe->hqk", query_sel, parts_kv[:, :, 0, :], preferred_element_type=jnp.float32
        )
        * scale_factor
    )
    weights = jnp.exp(scores)
    numer = jnp.einsum(
        "hqk,khe->hqe",
        weights.astype(jnp.bfloat16),
        parts_kv[:, :, 1, :],
        preferred_element_type=jnp.float32,
    )
    remote_den = jnp.sum(weights, axis=-1)
    scores = (
        jnp.einsum("qhe,khe->hqk", query_rows, keys_local, preferred_element_type=jnp.float32)
        * scale_factor
    )
    weights = jnp.exp(scores)
    local_num = jnp.einsum(
        "hqk,khe->hqe",
        weights.astype(jnp.bfloat16),
        values_local,
        preferred_element_type=jnp.float32,
    )
    local_den = jnp.sum(weights, axis=-1)
    spread_num = jnp.einsum("hre,hd->hrde", numer, row_selector).reshape(
        local_head_output, ENCODER_SLOTS, HEAD_WIDTH
    )
    spread_den = jnp.einsum("hr,hd->hrd", remote_den, row_selector).reshape(
        local_head_output, ENCODER_SLOTS
    )
    result = (local_num + spread_num) / (local_den + spread_den)[..., None]
    return (
        jnp.transpose(result, (1, 0, 2))
        .reshape(ENCODER_SLOTS, local_head_output * HEAD_WIDTH)
        .astype(jnp.bfloat16)
    )


def swap(array, axis, distance):
    size = lax.axis_size(axis)
    return lax.ppermute(array, axis, [(i, i ^ distance) for i in range(size)])


def block_at(array, index, size, axis):
    return lax.dynamic_slice_in_dim(array, index * size, size, axis)


def call(body, outs, inputs, spaces=None, scratch=(), copies=0, megabytes=40):
    spaces = spaces or [pltpu.VMEM] * len(inputs)
    scratch = list(scratch)
    if copies:
        scratch.append(pltpu.SemaphoreType.DMA((copies,)))
    return pl.pallas_call(
        body,
        out_shape=[jax.ShapeDtypeStruct(shape, kind) for shape, kind in outs],
        in_specs=[pl.BlockSpec(memory_space=space) for space in spaces],
        out_specs=[pl.BlockSpec(memory_space=pltpu.VMEM)] * len(outs),
        scratch_shapes=scratch,
        compiler_params=pltpu.CompilerParams(vmem_limit_bytes=megabytes * 1024 * 1024),
    )(*inputs)


def at(index, size):
    return pl.ds(pl.multiple_of(index * size, size), size)


def place():
    return tuple(lax.axis_index(name) for name in ("seq", "mp", "groups"))


def column_block(seq, mp):
    step = jnp.where(mp == 2, seq + 1, seq + 3) & 3
    return jnp.where(mp < 2, seq ^ (2 * mp), step)


def column_user(seq, mp):
    step = jnp.where(mp == 2, seq + 3, seq + 1) & 3
    return jnp.where(mp < 2, seq ^ (2 * mp), step)


def copier(sems, group):
    copies, used = [], [0]

    def copy(source, target, other=None):
        started = pltpu.make_async_copy(source, target, sems.at[used[0]])
        if other is None:
            started.start()
        else:
            second = pltpu.make_async_copy(other, target, sems.at[used[0]])
            pl.when(group == 0)(started.start)
            pl.when(group != 0)(second.start)
        copies.append(started)
        used[0] += 1

    return copies, copy


def normalise(rows, part, gain):
    values = rows[...].astype(jnp.float32)
    squares = jnp.sum(values * values, axis=1, keepdims=True)
    inverse = lax.rsqrt(squares * (1.0 / D_ENC) + epsilon)
    return (part.astype(jnp.float32) * inverse * gain[None, :]).astype(jnp.bfloat16)


def cut_first_body(
    count, tiles, w_gate, w_up, gain, first_out, second_out, quarter, held, sems
):
    seq, mp, group = place()
    copies, copy = copier(sems, group)
    half, units = w_gate.shape[0] // 2, w_gate.shape[1] // count
    features = quarter.shape[1]
    copy(tiles, held)
    for i in range(2):
        span = pl.ds(i * half, half), at(seq ^ 2, units)
        columns = pl.ds(features + i * units, units)
        copy(w_gate.at[span], second_out.at[:, columns], w_up.at[span])
        span = pl.ds(i * half, half), at(seq ^ 1, units)
        for k, weight in enumerate((w_gate, w_up)):
            columns = pl.ds(features + (2 * i + k) * units, units)
            copy(weight.at[span], first_out.at[:, columns])
    copies.pop(0).wait()
    columns = at(mp, features)
    own_columns = normalise(held, held[:, columns], gain[columns])
    second_out[:, :features] = own_columns
    first_out[:, :features] = own_columns
    quarter[...] = own_columns
    for started in copies:
        started.wait()


def cut_second_body(
    count, tiles, w_gate, w_up, w_down, gain, third_out, kept, near, far, normed, residual, held, sems
):
    seq, mp, group = place()
    copies, copy = copier(sems, group)
    half, units = w_gate.shape[0] // 2, w_gate.shape[1] // count
    copy(tiles, held)
    part = units // 2
    for j, target in ((2, far), (0, near)):
        rows = at(column_user(seq, mp ^ j) * 2 + group, part)
        copy(w_down.at[rows, :], target.at[pl.ds(0, part), :])
        rows = at(column_user(seq, mp ^ (j + 1)), units)
        copy(w_down.at[rows, :], target.at[pl.ds(part, units), :])
    for i in range(2):
        span = pl.ds(i * half, half), at(seq ^ 3, units)
        copy(w_gate.at[span], third_out.at[:, pl.ds(i * units, units)], w_up.at[span])
    for i, weight in enumerate((w_gate, w_up)):
        copy(weight.at[:, at(seq, units)], kept.at[:, pl.ds(i * units, units)])
    copies.pop(0).wait()
    normed[...] = normalise(held, held[...], gain[...])
    residual[...] = held[:, at(column_block(seq, mp), residual.shape[1])]
    for started in copies:
        started.wait()


def restack_body(second, third, first, stacked, columns):
    features = stacked.shape[2]
    stacked[0] = first[:, :features]
    stacked[1] = second[:, :features]
    stacked[2] = third[...]
    columns[...] = second[:, features:]


def pair_body(near, far, even, odd):
    for i, rows in enumerate((near, far)):
        even[i] = rows[: even.shape[1], :]
        odd[i] = rows[even.shape[1] :, :]


def routes_body(count, counts, offsets, dest, dest_row, routes):
    seq, _, _ = place()
    rows = dest_row.shape[1]
    capacity = ENCODER_SLOTS // count
    later = lax.broadcasted_iota(jnp.int32, (rows, rows), 1)
    earlier = lax.broadcasted_iota(jnp.int32, (rows, rows), 0)
    same = (dest[...] == dest_row[...]) & (earlier < later)
    rank = jnp.sum(jnp.where(same, 1, 0), axis=0, keepdims=True)
    live = lax.broadcasted_iota(jnp.int32, (1, rows), 1) < counts[0]
    codes = jnp.where(live, dest_row[...] * capacity + rank, -1)

    def chosen(wanted):
        return jnp.where(codes == wanted, 1.0, 0.0).astype(jnp.bfloat16)

    slot = lax.broadcasted_iota(jnp.int32, (capacity, rows), 0)
    for d in range(count):
        routes[pl.ds(d * capacity, capacity), :] = chosen((seq ^ d) * capacity + slot)
    per_block = capacity // DILATION_STEP
    spread = count * per_block
    index = lax.broadcasted_iota(jnp.int32, (spread, rows), 0)
    wanted = (index // per_block) * capacity + (index % per_block) * DILATION_STEP
    for h in range(offsets.shape[0]):
        routes[pl.ds(count * capacity + h * spread, spread), :] = chosen(wanted + offsets[h])


def hidden_body(count, normed, own, far, near, near_far, kept, next_in, *refs):
    (second, second_other, third, third_other), (out, weights) = refs[:4], refs[4:]
    seq, mp, group = place()
    depth, units = weights.shape[2:]
    half = depth // 2
    rows = normed.shape[0]
    for k in range(2):
        weights[k, seq] = kept[:, k * units : (k + 1) * units]
        for i in range(2):
            start = own.shape[2] + (2 * i + k) * units
            span = pl.ds(i * half, half)
            weights[k, seq ^ 1, span, :] = next_in[:, start : start + units]
    for d, mine, other in ((2, second, second_other), (3, third, third_other)):
        for i in range(2):
            span, columns = pl.ds(i * half, half), slice(i * units, (i + 1) * units)
            weights[group, seq ^ d, span, :] = mine[:, columns]
            weights[1 - group, seq ^ d, span, :] = other[:, columns]
    for d in range(count):
        if d == 0:
            pieces = [(normed[:, q * depth : (q + 1) * depth], q) for q in range(count)]
        else:
            pieces = [(own[d - 1], mp), (near[d - 1], mp ^ 1)]
            pieces += [(far[d - 1], mp ^ 2), (near_far[d - 1], mp ^ 3)]
        gate_act, up_act = (
            sum(
                jnp.dot(piece, weights[k, index], preferred_element_type=jnp.float32)
                for piece, index in pieces
            )
            for k in range(2)
        )
        gated = gate_act * jax.nn.sigmoid(gate_act) * up_act
        out[pl.ds(d * rows, rows), :] = gated.astype(jnp.bfloat16)


def down_body(residual, own, far, near, near_far, even, even_other, odd, *outs):
    _, _, group = place()
    rows = outs[0].shape[0]
    weights = [None, odd[0], None, odd[1]]
    for j in range(2):
        mine, other = even[j], even_other[j]
        low, high = jnp.where(group == 0, mine, other), jnp.where(group == 0, other, mine)
        weights[2 * j] = jnp.concatenate([low, high], axis=0)
    for i, out in enumerate(outs):
        total = residual[...].astype(jnp.float32) if i == 0 else 0.0
        for j, piece in enumerate((own, near, far, near_far)):
            total += jnp.dot(
                piece[pl.ds(i * rows, rows), :], weights[j], preferred_element_type=jnp.float32
            )
        out[...] = total.astype(out.dtype)


def sum_body(own, *refs):
    parts, out = refs[:-1], refs[-1]
    total = own[...] + sum(part[...].astype(jnp.float32) for part in parts)
    out[...] = total.astype(out.dtype)


def project_body(count, gain, routes, w_qkv_t, own, far, near, near_far, *outs):
    seq, mp, _ = place()
    features = own.shape[1]
    capacity = outs[0].shape[0]
    heads = w_qkv_t.shape[0] // (3 * HEAD_WIDTH)
    squares, total = 0.0, 0.0
    for j, piece in enumerate((own, near, far, near_far)):
        index = column_block(seq, mp ^ j)
        v = piece[...].astype(jnp.float32)
        squares += jnp.sum(v * v, axis=1, keepdims=True)
        scaled = (v * gain[:, at(index, features)]).astype(jnp.bfloat16)
        total += lax.dot_general(
            scaled,
            w_qkv_t[:, at(index, features)],
            (((1,), (1,)), ((), ())),
            preferred_element_type=jnp.float32,
        )
    projected = (total * lax.rsqrt(squares * (1.0 / D_ENC) + epsilon)).astype(jnp.bfloat16)
    routed = jnp.dot(routes[...], projected, preferred_element_type=jnp.float32)
    routed = routed.astype(jnp.bfloat16)
    width = projected.shape[1]
    spread = capacity // 2
    for d, out in enumerate(outs):
        out[:, :width] = routed[d * capacity : (d + 1) * capacity]
    for h in range(heads):
        first = count * capacity + h * spread
        for i in range(2):
            start = (3 * h + 1 + i) * HEAD_WIDTH
            piece = routed[first : first + spread, start : start + HEAD_WIDTH]
            for out in outs:
                span = slice(width + h * HEAD_WIDTH, width + (h + 1) * HEAD_WIDTH)
                out[i * spread : (i + 1) * spread, span] = piece


def attend_body(count, offsets, *refs):
    packages, out, rows = refs[:count], refs[count], refs[count + 1]
    seq, _, _ = place()
    capacity = packages[0].shape[0]
    heads = offsets.shape[0]
    width = heads * 3 * HEAD_WIDTH
    for d, package in zip(ORDER, packages):
        rows[at(seq ^ d, capacity), :] = package[:, :width]
    far = [package[:, width:] for package in packages]
    half = capacity // 2
    far_keys = jnp.concatenate([f[:half] for f in far], axis=0)
    far_values = jnp.concatenate([f[half:] for f in far], axis=0)
    residue = lax.broadcasted_iota(jnp.int32, (1, out.shape[1]), 1) % DILATION_STEP
    scale_factor = HEAD_WIDTH ** (-0.5)

    local = out.shape[1]
    for h in range(heads):
        query, key, value = (
            rows[:, pl.ds((3 * h + i) * HEAD_WIDTH, HEAD_WIDTH)] for i in range(3)
        )
        span = slice(h * HEAD_WIDTH, (h + 1) * HEAD_WIDTH)
        keys = jnp.concatenate([key, far_keys[:, span]], axis=0)
        values = jnp.concatenate([value, far_values[:, span]], axis=0)
        scores = lax.dot_general(
            keys, query, (((1,), (1,)), ((), ())), preferred_element_type=jnp.float32
        )
        weights = jnp.exp(scores * scale_factor)
        dilated = jnp.where(residue == offsets[h], weights[local:], 0.0)
        weights = jnp.concatenate([weights[:local], dilated], axis=0)
        numer = lax.dot_general(
            values,
            weights.astype(jnp.bfloat16),
            (((0,), (0,)), ((), ())),
            preferred_element_type=jnp.float32,
        )
        denom = jnp.sum(weights, axis=0, keepdims=True)
        out[span, :] = (numer / denom).astype(jnp.bfloat16)


def spread_mp(own, beside=None):
    far = swap(own, "mp", 2)
    relayed = far if beside is None else lax.optimization_barrier((far, beside))[0]
    return far, swap(own, "mp", 1), swap(relayed, "mp", 1)


def split_hidden_plan(
    tiles, counts, dest, gain_enc, w_gate, w_up, w_down, gain_slide, w_qkv, offsets
):
    count, mp_size = lax.axis_size("seq"), lax.axis_size("mp")
    seq, mp = lax.axis_index("seq"), lax.axis_index("mp")
    capacity = ENCODER_SLOTS // count
    tile_rows = tiles.shape[0]
    features = D_ENC // mp_size
    depth = w_gate.shape[0]
    units = w_gate.shape[1] // count
    heads = offsets.shape[0]
    bf16 = jnp.bfloat16
    vmem, smem = pltpu.VMEM, pltpu.SMEM

    first_out, second_out, quarter = call(
        functools.partial(cut_first_body, count),
        [
            ((tile_rows, features + 4 * units), bf16),
            ((tile_rows, features + 2 * units), bf16),
            ((tile_rows, features), bf16),
        ],
        (tiles, w_gate, w_up, gain_enc),
        spaces=[pltpu.HBM] * 3 + [vmem],
        copies=7,
        scratch=[pltpu.VMEM((tile_rows, D_ENC), bf16)],
        megabytes=57,
    )
    third_out, kept, down_near, down_far, normed, residual = call(
        functools.partial(cut_second_body, count),
        [
            ((tile_rows, 2 * units), bf16),
            ((depth, 2 * units), bf16),
            ((3 * units // 2, features), bf16),
            ((3 * units // 2, features), bf16),
            ((tile_rows, D_ENC), bf16),
            ((tile_rows, features), bf16),
        ],
        (tiles, w_gate, w_up, w_down, gain_enc),
        spaces=[pltpu.HBM] * 4 + [vmem],
        scratch=[pltpu.VMEM((tile_rows, D_ENC), bf16)],
        copies=9,
        megabytes=57,
    )
    routes = call(
        functools.partial(routes_body, count),
        [((ENCODER_SLOTS + heads * ENCODER_SLOTS // DILATION_STEP, tile_rows), bf16)],
        (counts, offsets, dest, dest.reshape(1, tile_rows)),
        spaces=[smem, smem, vmem, vmem],
    )[0]

    second_in, third_in = swap(second_out, "seq", 2), swap(quarter, "seq", 3)
    arrived = second_in, third_in, swap(first_out, "seq", 1)
    from_far = swap(down_far, "mp", 2)
    arrived, from_far, routes = lax.optimization_barrier((arrived, from_far, routes))
    own, columns = call(
        restack_body,
        [
            ((count - 1, tile_rows, features), bf16),
            ((tile_rows, 2 * units), bf16),
        ],
        arrived,
    )
    third_out, _ = lax.optimization_barrier((third_out, arrived[0]))
    down_near, _ = lax.optimization_barrier((down_near, own))
    down_send = call(
        pair_body,
        [((2, units // 2, features), bf16), ((2, units, features), bf16)],
        (down_near, from_far),
    )
    third, others, far, near, down_send = lax.optimization_barrier(
        (
            swap(third_out, "seq", 3),
            swap(columns, "groups", 1),
            swap(own, "mp", 2),
            swap(own, "mp", 1),
            down_send,
        )
    )
    halves = columns, others, third, swap(third, "groups", 1)
    spread = far, near, swap(far, "mp", 1)
    parts = []
    for j in range(2):
        perm = []
        for s in range(count):
            for m in range(mp_size):
                k = m ^ j
                user = (s ^ 2 * k) if k < 2 else (s + 2 * k - 5) % count
                perm.append((s * mp_size + m, user * mp_size + k))
        parts.append(lax.ppermute(down_send[j], ("seq", "mp"), perm))
    hidden = call(
        functools.partial(hidden_body, count),
        [((count * tile_rows, units), bf16)],
        (normed, own, *spread, kept, arrived[2], *halves),
        scratch=[
            pltpu.VMEM((2, count, depth, units), bf16),
        ],
    )[0]
    even, odd = parts
    even_other = swap(even, "groups", 1)
    sums = call(
        down_body,
        [((tile_rows, features), kind) for kind in (jnp.float32, bf16, bf16, bf16)],
        (residual, hidden, *spread_mp(hidden, even_other), even, even_other, odd),
    )
    holder = [0, 2, 1, 3]

    def to_owner(part, d):
        perm = []
        for s in range(count):
            for m in range(mp_size):
                owner = s ^ d
                perm.append((s * mp_size + m, owner * mp_size + holder[(s + holder[m] - owner) % count]))
        return lax.ppermute(part, ("seq", "mp"), perm)

    arrived = [to_owner(sums[d], d) for d in (2, 1, 3)]
    embedded_cols = call(
        sum_body, [((tile_rows, features), bf16)], (sums[0], *arrived)
    )[0]

    packages = call(
        functools.partial(project_body, count),
        [((capacity, 4 * heads * HEAD_WIDTH), bf16)] * count,
        (gain_slide[None, :], routes, w_qkv.T, embedded_cols, *spread_mp(embedded_cols)),
    )
    packages = [swap(packages[d], "seq", d) for d in ORDER[:-1]] + [packages[0]]
    return call(
        functools.partial(attend_body, count),
        [((heads * HEAD_WIDTH, ENCODER_SLOTS), bf16)],
        (offsets, *packages),
        spaces=[smem] + [vmem] * count,
        scratch=[pltpu.VMEM((ENCODER_SLOTS, 3 * heads * HEAD_WIDTH), bf16)],
    )[0].T


def on_device(*arrays):
    sizes = lax.axis_size("groups"), lax.axis_size("seq"), lax.axis_size("mp")
    if sizes == (2, 4, 4):
        return split_hidden_plan(*arrays)
    return gathered_plan(*arrays)


def solution(mesh):
    return jax.shard_map(
        on_device,
        mesh=mesh,
        in_specs=(
            P(("groups", "seq"), None),
            P(("groups", "seq")),
            P(("groups", "seq"), None),
            P(),
            P("seq", "mp"),
            P("seq", "mp"),
            P("mp", "seq"),
            P(),
            P(None, "mp"),
            P("mp"),
        ),
        out_specs=P(("groups", "seq"), "mp"),
        check_vma=False,
    )
```

```python
import functools

import jax
import jax.numpy as jnp
from jax import lax
from jax.experimental import pallas as pl
from jax.experimental.pallas import tpu as pltpu
from jax.sharding import PartitionSpec as P

D_ENC = 1536
HEAD_WIDTH = 64
DILATION_STEP = 8
ENCODER_SLOTS = 256
ORDER = (2, 1, 3, 0)


epsilon = 1e-05


def gather_seq(package):
    count = lax.axis_size("seq")
    if count & (count - 1) == 0 and count <= 4:
        return jnp.concatenate([package] + [swap(package, "seq", d) for d in range(1, count)])
    return lax.all_gather(package, "seq", axis=0, tiled=True)


def gathered_plan(tiles, counts, dest, gain_enc, w_gate, w_up, w_down, gain_slide, w_qkv, offsets):
    seq_count = lax.axis_size("seq")
    capacity = ENCODER_SLOTS // seq_count
    tile_rows = tiles.shape[0]
    target = dest[:, 0]
    live_rows = jnp.arange(tile_rows, dtype=jnp.int32) < counts[0]
    chosen = (
        (target[:, None] == jnp.arange(seq_count, dtype=jnp.int32)[None, :]) & live_rows[:, None]
    ).astype(jnp.int32)
    arrival = jnp.sum((jnp.cumsum(chosen, axis=0) - chosen) * chosen, axis=1)
    slot_index = jnp.where(live_rows, target * capacity + arrival, ENCODER_SLOTS)
    outgoing = (
        jnp.zeros((ENCODER_SLOTS, D_ENC), jnp.bfloat16).at[slot_index].set(tiles, mode="drop")
    )
    arrived = lax.all_to_all(outgoing, "seq", split_axis=0, concat_axis=0, tiled=True)
    arrived_f = arrived.astype(jnp.float32)
    inverse = lax.rsqrt(jnp.mean(arrived_f * arrived_f, axis=-1, keepdims=True) + epsilon)
    normed = (arrived_f * inverse * gain_enc).astype(jnp.bfloat16)

    def add_rows(portion):
        return jnp.dot(normed, portion, preferred_element_type=jnp.float32)

    gate_act = add_rows(lax.all_gather(w_gate, "seq", axis=0, tiled=True))
    up_act = add_rows(lax.all_gather(w_up, "seq", axis=0, tiled=True))
    hidden = (jax.nn.silu(gate_act) * up_act).astype(jnp.bfloat16)
    partial_out = jnp.dot(
        hidden,
        lax.all_gather(w_down, "seq", axis=1, tiled=True),
        preferred_element_type=jnp.float32,
    )
    share = lax.psum_scatter(partial_out, "mp", scatter_dimension=1, tiled=True)
    share_width = share.shape[1]
    own_cols = lax.dynamic_slice_in_dim(
        arrived_f, lax.axis_index("mp") * share_width, share_width, 1
    )
    embedded_cols = (own_cols + share).astype(jnp.bfloat16)
    embedded = lax.all_gather(embedded_cols, "mp", axis=1, tiled=True)
    return slide_layer(embedded, gain_slide, w_qkv, offsets)


def slide_layer(embedded, gain_slide, w_qkv, offsets):
    portion_f = embedded.astype(jnp.float32)
    accumulated = jnp.dot(
        (portion_f * gain_slide).astype(jnp.bfloat16), w_qkv, preferred_element_type=jnp.float32
    )
    accumulated, squares = (accumulated, jnp.sum(portion_f * portion_f, axis=1))
    projected = accumulated * lax.rsqrt(squares / D_ENC + epsilon)[:, None]
    qkv_act = projected.astype(jnp.bfloat16)
    local_head_output = offsets.shape[0]
    fields = qkv_act.reshape(ENCODER_SLOTS, local_head_output, 3, HEAD_WIDTH)
    query_rows = fields[:, :, 0, :]
    keys_local = fields[:, :, 1, :]
    values_local = fields[:, :, 2, :]
    scale_factor = HEAD_WIDTH ** (-0.5)
    row_selector = (jnp.arange(DILATION_STEP, dtype=jnp.int32)[None, :] == offsets[:, None]).astype(
        jnp.float32
    )
    selected_rows = ENCODER_SLOTS // DILATION_STEP

    def select_rows(slide_field):
        reshaped_rows = slide_field.astype(jnp.float32).reshape(
            selected_rows, DILATION_STEP, local_head_output, HEAD_WIDTH
        )
        return jnp.einsum("rdhe,hd->rhe", reshaped_rows, row_selector).astype(jnp.bfloat16)

    query_sel = select_rows(query_rows)
    package = jnp.concatenate([select_rows(keys_local), select_rows(values_local)], axis=2).reshape(
        selected_rows, local_head_output * 2 * HEAD_WIDTH
    )
    portion = gather_seq(package)
    parts_kv = portion.reshape(portion.shape[0], local_head_output, 2, HEAD_WIDTH)
    scores = (
        jnp.einsum(
            "qhe,khe->hqk", query_sel, parts_kv[:, :, 0, :], preferred_element_type=jnp.float32
        )
        * scale_factor
    )
    weights = jnp.exp(scores)
    numer = jnp.einsum(
        "hqk,khe->hqe",
        weights.astype(jnp.bfloat16),
        parts_kv[:, :, 1, :],
        preferred_element_type=jnp.float32,
    )
    remote_den = jnp.sum(weights, axis=-1)
    scores = (
        jnp.einsum("qhe,khe->hqk", query_rows, keys_local, preferred_element_type=jnp.float32)
        * scale_factor
    )
    weights = jnp.exp(scores)
    local_num = jnp.einsum(
        "hqk,khe->hqe",
        weights.astype(jnp.bfloat16),
        values_local,
        preferred_element_type=jnp.float32,
    )
    local_den = jnp.sum(weights, axis=-1)
    spread_num = jnp.einsum("hre,hd->hrde", numer, row_selector).reshape(
        local_head_output, ENCODER_SLOTS, HEAD_WIDTH
    )
    spread_den = jnp.einsum("hr,hd->hrd", remote_den, row_selector).reshape(
        local_head_output, ENCODER_SLOTS
    )
    result = (local_num + spread_num) / (local_den + spread_den)[..., None]
    return (
        jnp.transpose(result, (1, 0, 2))
        .reshape(ENCODER_SLOTS, local_head_output * HEAD_WIDTH)
        .astype(jnp.bfloat16)
    )


def swap(array, axis, distance):
    size = lax.axis_size(axis)
    return lax.ppermute(array, axis, [(i, i ^ distance) for i in range(size)])


def block_at(array, index, size, axis):
    return lax.dynamic_slice_in_dim(array, index * size, size, axis)


def call(body, outs, inputs, spaces=None, scratch=(), copies=0, megabytes=40):
    spaces = spaces or [pltpu.VMEM] * len(inputs)
    scratch = list(scratch)
    if copies:
        scratch.append(pltpu.SemaphoreType.DMA((copies,)))
    return pl.pallas_call(
        body,
        out_shape=[jax.ShapeDtypeStruct(shape, kind) for shape, kind in outs],
        in_specs=[pl.BlockSpec(memory_space=space) for space in spaces],
        out_specs=[pl.BlockSpec(memory_space=pltpu.VMEM)] * len(outs),
        scratch_shapes=scratch,
        compiler_params=pltpu.CompilerParams(vmem_limit_bytes=megabytes * 1024 * 1024),
    )(*inputs)


def at(index, size):
    return pl.ds(pl.multiple_of(index * size, size), size)


def place():
    return tuple(lax.axis_index(name) for name in ("seq", "mp", "groups"))


def column_block(seq, mp):
    step = jnp.where(mp == 2, seq + 1, seq + 3) & 3
    return jnp.where(mp < 2, seq ^ (2 * mp), step)


def column_user(seq, mp):
    step = jnp.where(mp == 2, seq + 3, seq + 1) & 3
    return jnp.where(mp < 2, seq ^ (2 * mp), step)


def copier(sems, group):
    copies, used = [], [0]

    def copy(source, target, other=None):
        started = pltpu.make_async_copy(source, target, sems.at[used[0]])
        if other is None:
            started.start()
        else:
            second = pltpu.make_async_copy(other, target, sems.at[used[0]])
            pl.when(group == 0)(started.start)
            pl.when(group != 0)(second.start)
        copies.append(started)
        used[0] += 1

    return copies, copy


def normalise(rows, part, gain):
    values = rows[...].astype(jnp.float32)
    squares = jnp.sum(values * values, axis=1, keepdims=True)
    inverse = lax.rsqrt(squares * (1.0 / D_ENC) + epsilon)
    return (part.astype(jnp.float32) * inverse * gain[None, :]).astype(jnp.bfloat16)


def cut_first_body(
    count, tiles, w_gate, w_up, gain, first_out, second_out, quarter, held, sems
):
    seq, mp, group = place()
    copies, copy = copier(sems, group)
    half, units = w_gate.shape[0] // 2, w_gate.shape[1] // count
    features = quarter.shape[1]
    copy(tiles, held)
    for i in range(2):
        span = pl.ds(i * half, half), at(seq ^ 2, units)
        columns = pl.ds(features + i * units, units)
        copy(w_gate.at[span], second_out.at[:, columns], w_up.at[span])
        span = pl.ds(i * half, half), at(seq ^ 1, units)
        for k, weight in enumerate((w_gate, w_up)):
            columns = pl.ds(features + (2 * i + k) * units, units)
            copy(weight.at[span], first_out.at[:, columns])
    copies.pop(0).wait()
    columns = at(mp, features)
    own_columns = normalise(held, held[:, columns], gain[columns])
    second_out[:, :features] = own_columns
    first_out[:, :features] = own_columns
    quarter[...] = own_columns
    for started in copies:
        started.wait()


def cut_second_body(
    count, tiles, w_gate, w_up, w_down, gain, third_out, kept, near, far, normed, residual, held, sems
):
    seq, mp, group = place()
    copies, copy = copier(sems, group)
    half, units = w_gate.shape[0] // 2, w_gate.shape[1] // count
    copy(tiles, held)
    part = units // 2
    for j, target in ((2, far), (0, near)):
        rows = at(column_user(seq, mp ^ j) * 2 + group, part)
        copy(w_down.at[rows, :], target.at[pl.ds(0, part), :])
        rows = at(column_user(seq, mp ^ (j + 1)), units)
        copy(w_down.at[rows, :], target.at[pl.ds(part, units), :])
    for i in range(2):
        span = pl.ds(i * half, half), at(seq ^ 3, units)
        copy(w_gate.at[span], third_out.at[:, pl.ds(i * units, units)], w_up.at[span])
    for i, weight in enumerate((w_gate, w_up)):
        copy(weight.at[:, at(seq, units)], kept.at[:, pl.ds(i * units, units)])
    copies.pop(0).wait()
    normed[...] = normalise(held, held[...], gain[...])
    residual[...] = held[:, at(column_block(seq, mp), residual.shape[1])]
    for started in copies:
        started.wait()


def restack_body(second, third, first, stacked, columns):
    features = stacked.shape[2]
    stacked[0] = first[:, :features]
    stacked[1] = second[:, :features]
    stacked[2] = third[...]
    columns[...] = second[:, features:]


def pair_body(near, far, even, odd):
    for i, rows in enumerate((near, far)):
        even[i] = rows[: even.shape[1], :]
        odd[i] = rows[even.shape[1] :, :]


def routes_body(count, counts, offsets, dest, dest_row, routes):
    seq, _, _ = place()
    rows = dest_row.shape[1]
    capacity = ENCODER_SLOTS // count
    later = lax.broadcasted_iota(jnp.int32, (rows, rows), 1)
    earlier = lax.broadcasted_iota(jnp.int32, (rows, rows), 0)
    same = (dest[...] == dest_row[...]) & (earlier < later)
    rank = jnp.sum(jnp.where(same, 1, 0), axis=0, keepdims=True)
    live = lax.broadcasted_iota(jnp.int32, (1, rows), 1) < counts[0]
    codes = jnp.where(live, dest_row[...] * capacity + rank, -1)

    def chosen(wanted):
        return jnp.where(codes == wanted, 1.0, 0.0).astype(jnp.bfloat16)

    slot = lax.broadcasted_iota(jnp.int32, (capacity, rows), 0)
    for d in range(count):
        routes[pl.ds(d * capacity, capacity), :] = chosen((seq ^ d) * capacity + slot)
    per_block = capacity // DILATION_STEP
    spread = count * per_block
    index = lax.broadcasted_iota(jnp.int32, (spread, rows), 0)
    wanted = (index // per_block) * capacity + (index % per_block) * DILATION_STEP
    for h in range(offsets.shape[0]):
        routes[pl.ds(count * capacity + h * spread, spread), :] = chosen(wanted + offsets[h])


def hidden_body(count, normed, own, far, near, near_far, kept, next_in, *refs):
    (second, second_other, third, third_other), (out, weights) = refs[:4], refs[4:]
    seq, mp, group = place()
    depth, units = weights.shape[2:]
    half = depth // 2
    rows = normed.shape[0]
    for k in range(2):
        weights[k, seq] = kept[:, k * units : (k + 1) * units]
        for i in range(2):
            start = own.shape[2] + (2 * i + k) * units
            span = pl.ds(i * half, half)
            weights[k, seq ^ 1, span, :] = next_in[:, start : start + units]
    for d, mine, other in ((2, second, second_other), (3, third, third_other)):
        for i in range(2):
            span, columns = pl.ds(i * half, half), slice(i * units, (i + 1) * units)
            weights[group, seq ^ d, span, :] = mine[:, columns]
            weights[1 - group, seq ^ d, span, :] = other[:, columns]
    for d in range(count):
        if d == 0:
            pieces = [(normed[:, q * depth : (q + 1) * depth], q) for q in range(count)]
        else:
            pieces = [(own[d - 1], mp), (near[d - 1], mp ^ 1)]
            pieces += [(far[d - 1], mp ^ 2), (near_far[d - 1], mp ^ 3)]
        gate_act, up_act = (
            sum(
                jnp.dot(piece, weights[k, index], preferred_element_type=jnp.float32)
                for piece, index in pieces
            )
            for k in range(2)
        )
        gated = gate_act * jax.nn.sigmoid(gate_act) * up_act
        out[pl.ds(d * rows, rows), :] = gated.astype(jnp.bfloat16)


def down_body(residual, own, far, near, near_far, even, even_other, odd, *outs):
    _, _, group = place()
    rows = outs[0].shape[0]
    weights = [None, odd[0], None, odd[1]]
    for j in range(2):
        mine, other = even[j], even_other[j]
        low, high = jnp.where(group == 0, mine, other), jnp.where(group == 0, other, mine)
        weights[2 * j] = jnp.concatenate([low, high], axis=0)
    for i, out in enumerate(outs):
        total = residual[...].astype(jnp.float32) if i == 0 else 0.0
        for j, piece in enumerate((own, near, far, near_far)):
            total += jnp.dot(
                piece[pl.ds(i * rows, rows), :], weights[j], preferred_element_type=jnp.float32
            )
        out[...] = total.astype(out.dtype)


def sum_body(own, *refs):
    parts, out = refs[:-1], refs[-1]
    total = own[...] + sum(part[...].astype(jnp.float32) for part in parts)
    out[...] = total.astype(out.dtype)


def project_body(count, gain, routes, w_qkv_t, own, far, near, near_far, *outs):
    seq, mp, _ = place()
    features = own.shape[1]
    capacity = outs[0].shape[0]
    heads = w_qkv_t.shape[0] // (3 * HEAD_WIDTH)
    squares, total = 0.0, 0.0
    for j, piece in enumerate((own, near, far, near_far)):
        index = column_block(seq, mp ^ j)
        v = piece[...].astype(jnp.float32)
        squares += jnp.sum(v * v, axis=1, keepdims=True)
        scaled = (v * gain[:, at(index, features)]).astype(jnp.bfloat16)
        total += lax.dot_general(
            scaled,
            w_qkv_t[:, at(index, features)],
            (((1,), (1,)), ((), ())),
            preferred_element_type=jnp.float32,
        )
    projected = (total * lax.rsqrt(squares * (1.0 / D_ENC) + epsilon)).astype(jnp.bfloat16)
    routed = jnp.dot(routes[...], projected, preferred_element_type=jnp.float32)
    routed = routed.astype(jnp.bfloat16)
    width = projected.shape[1]
    spread = capacity // 2
    for d, out in enumerate(outs):
        out[:, :width] = routed[d * capacity : (d + 1) * capacity]
    for h in range(heads):
        first = count * capacity + h * spread
        for i in range(2):
            start = (3 * h + 1 + i) * HEAD_WIDTH
            piece = routed[first : first + spread, start : start + HEAD_WIDTH]
            for out in outs:
                span = slice(width + h * HEAD_WIDTH, width + (h + 1) * HEAD_WIDTH)
                out[i * spread : (i + 1) * spread, span] = piece


def attend_body(count, offsets, *refs):
    packages, out, rows = refs[:count], refs[count], refs[count + 1]
    seq, _, _ = place()
    capacity = packages[0].shape[0]
    heads = offsets.shape[0]
    width = heads * 3 * HEAD_WIDTH
    for d, package in zip(ORDER, packages):
        rows[at(seq ^ d, capacity), :] = package[:, :width]
    far = [package[:, width:] for package in packages]
    half = capacity // 2
    far_keys = jnp.concatenate([f[:half] for f in far], axis=0)
    far_values = jnp.concatenate([f[half:] for f in far], axis=0)
    residue = lax.broadcasted_iota(jnp.int32, (1, out.shape[1]), 1) % DILATION_STEP
    scale_factor = HEAD_WIDTH ** (-0.5)

    local = out.shape[1]
    for h in range(heads):
        query, key, value = (
            rows[:, pl.ds((3 * h + i) * HEAD_WIDTH, HEAD_WIDTH)] for i in range(3)
        )
        span = slice(h * HEAD_WIDTH, (h + 1) * HEAD_WIDTH)
        keys = jnp.concatenate([key, far_keys[:, span]], axis=0)
        values = jnp.concatenate([value, far_values[:, span]], axis=0)
        scores = lax.dot_general(
            keys, query, (((1,), (1,)), ((), ())), preferred_element_type=jnp.float32
        )
        weights = jnp.exp(scores * scale_factor)
        dilated = jnp.where(residue == offsets[h], weights[local:], 0.0)
        weights = jnp.concatenate([weights[:local], dilated], axis=0)
        numer = lax.dot_general(
            values,
            weights.astype(jnp.bfloat16),
            (((0,), (0,)), ((), ())),
            preferred_element_type=jnp.float32,
        )
        denom = jnp.sum(weights, axis=0, keepdims=True)
        out[span, :] = (numer / denom).astype(jnp.bfloat16)


def spread_mp(own, beside=None):
    far = swap(own, "mp", 2)
    relayed = far if beside is None else lax.optimization_barrier((far, beside))[0]
    return far, swap(own, "mp", 1), swap(relayed, "mp", 1)


def split_hidden_plan(
    tiles, counts, dest, gain_enc, w_gate, w_up, w_down, gain_slide, w_qkv, offsets
):
    count, mp_size = lax.axis_size("seq"), lax.axis_size("mp")
    seq, mp = lax.axis_index("seq"), lax.axis_index("mp")
    capacity = ENCODER_SLOTS // count
    tile_rows = tiles.shape[0]
    features = D_ENC // mp_size
    depth = w_gate.shape[0]
    units = w_gate.shape[1] // count
    heads = offsets.shape[0]
    bf16 = jnp.bfloat16
    vmem, smem = pltpu.VMEM, pltpu.SMEM

    first_out, second_out, quarter = call(
        functools.partial(cut_first_body, count),
        [
            ((tile_rows, features + 4 * units), bf16),
            ((tile_rows, features + 2 * units), bf16),
            ((tile_rows, features), bf16),
        ],
        (tiles, w_gate, w_up, gain_enc),
        spaces=[pltpu.HBM] * 3 + [vmem],
        copies=7,
        scratch=[pltpu.VMEM((tile_rows, D_ENC), bf16)],
        megabytes=57,
    )
    third_out, kept, down_near, down_far, normed, residual = call(
        functools.partial(cut_second_body, count),
        [
            ((tile_rows, 2 * units), bf16),
            ((depth, 2 * units), bf16),
            ((3 * units // 2, features), bf16),
            ((3 * units // 2, features), bf16),
            ((tile_rows, D_ENC), bf16),
            ((tile_rows, features), bf16),
        ],
        (tiles, w_gate, w_up, w_down, gain_enc),
        spaces=[pltpu.HBM] * 4 + [vmem],
        scratch=[pltpu.VMEM((tile_rows, D_ENC), bf16)],
        copies=9,
        megabytes=57,
    )
    routes = call(
        functools.partial(routes_body, count),
        [((ENCODER_SLOTS + heads * ENCODER_SLOTS // DILATION_STEP, tile_rows), bf16)],
        (counts, offsets, dest, dest.reshape(1, tile_rows)),
        spaces=[smem, smem, vmem, vmem],
    )[0]

    second_in, third_in = swap(second_out, "seq", 2), swap(quarter, "seq", 3)
    arrived = second_in, third_in, swap(first_out, "seq", 1)
    from_far = swap(down_far, "mp", 2)
    arrived, from_far, routes = lax.optimization_barrier((arrived, from_far, routes))
    own, columns = call(
        restack_body,
        [
            ((count - 1, tile_rows, features), bf16),
            ((tile_rows, 2 * units), bf16),
        ],
        arrived,
    )
    third_out, _ = lax.optimization_barrier((third_out, arrived[0]))
    down_near, _ = lax.optimization_barrier((down_near, own))
    down_send = call(
        pair_body,
        [((2, units // 2, features), bf16), ((2, units, features), bf16)],
        (down_near, from_far),
    )
    third, others, far, near, down_send = lax.optimization_barrier(
        (
            swap(third_out, "seq", 3),
            swap(columns, "groups", 1),
            swap(own, "mp", 2),
            swap(own, "mp", 1),
            down_send,
        )
    )
    halves = columns, others, third, swap(third, "groups", 1)
    spread = far, near, swap(far, "mp", 1)
    parts = []
    for j in range(2):
        perm = []
        for s in range(count):
            for m in range(mp_size):
                k = m ^ j
                user = (s ^ 2 * k) if k < 2 else (s + 2 * k - 5) % count
                perm.append((s * mp_size + m, user * mp_size + k))
        parts.append(lax.ppermute(down_send[j], ("seq", "mp"), perm))
    hidden = call(
        functools.partial(hidden_body, count),
        [((count * tile_rows, units), bf16)],
        (normed, own, *spread, kept, arrived[2], *halves),
        scratch=[
            pltpu.VMEM((2, count, depth, units), bf16),
        ],
    )[0]
    even, odd = parts
    even_other = swap(even, "groups", 1)
    sums = call(
        down_body,
        [((tile_rows, features), kind) for kind in (jnp.float32, bf16, bf16, bf16)],
        (residual, hidden, *spread_mp(hidden, (even_other, odd)), even, even_other, odd),
    )
    holder = [0, 2, 1, 3]

    def to_owner(part, d):
        perm = []
        for s in range(count):
            for m in range(mp_size):
                owner = s ^ d
                perm.append((s * mp_size + m, owner * mp_size + holder[(s + holder[m] - owner) % count]))
        return lax.ppermute(part, ("seq", "mp"), perm)

    arrived = [to_owner(sums[d], d) for d in (2, 1, 3)]
    embedded_cols = call(
        sum_body, [((tile_rows, features), bf16)], (sums[0], *arrived)
    )[0]

    packages = call(
        functools.partial(project_body, count),
        [((capacity, 4 * heads * HEAD_WIDTH), bf16)] * count,
        (gain_slide[None, :], routes, w_qkv.T, embedded_cols, *spread_mp(embedded_cols)),
    )
    packages = [swap(packages[d], "seq", d) for d in ORDER[:-1]] + [packages[0]]
    return call(
        functools.partial(attend_body, count),
        [((heads * HEAD_WIDTH, ENCODER_SLOTS), bf16)],
        (offsets, *packages),
        spaces=[smem] + [vmem] * count,
        scratch=[pltpu.VMEM((ENCODER_SLOTS, 3 * heads * HEAD_WIDTH), bf16)],
    )[0].T


def on_device(*arrays):
    sizes = lax.axis_size("groups"), lax.axis_size("seq"), lax.axis_size("mp")
    if sizes == (2, 4, 4):
        return split_hidden_plan(*arrays)
    return gathered_plan(*arrays)


def solution(mesh):
    return jax.shard_map(
        on_device,
        mesh=mesh,
        in_specs=(
            P(("groups", "seq"), None),
            P(("groups", "seq")),
            P(("groups", "seq"), None),
            P(),
            P("seq", "mp"),
            P("seq", "mp"),
            P("mp", "seq"),
            P(),
            P(None, "mp"),
            P("mp"),
        ),
        out_specs=P(("groups", "seq"), "mp"),
        check_vma=False,
    )
```

```python
import functools

import jax
import jax.numpy as jnp
from jax import lax
from jax.experimental import pallas as pl
from jax.experimental.pallas import tpu as pltpu
from jax.sharding import PartitionSpec as P

D_ENC = 1536
HEAD_WIDTH = 64
DILATION_STEP = 8
ENCODER_SLOTS = 256
ORDER = (1, 2, 3, 0)


epsilon = 1e-05


def gather_seq(package):
    count = lax.axis_size("seq")
    if count & (count - 1) == 0 and count <= 4:
        return jnp.concatenate([package] + [swap(package, "seq", d) for d in range(1, count)])
    return lax.all_gather(package, "seq", axis=0, tiled=True)


def gathered_plan(tiles, counts, dest, gain_enc, w_gate, w_up, w_down, gain_slide, w_qkv, offsets):
    seq_count = lax.axis_size("seq")
    capacity = ENCODER_SLOTS // seq_count
    tile_rows = tiles.shape[0]
    target = dest[:, 0]
    live_rows = jnp.arange(tile_rows, dtype=jnp.int32) < counts[0]
    chosen = (
        (target[:, None] == jnp.arange(seq_count, dtype=jnp.int32)[None, :]) & live_rows[:, None]
    ).astype(jnp.int32)
    arrival = jnp.sum((jnp.cumsum(chosen, axis=0) - chosen) * chosen, axis=1)
    slot_index = jnp.where(live_rows, target * capacity + arrival, ENCODER_SLOTS)
    outgoing = (
        jnp.zeros((ENCODER_SLOTS, D_ENC), jnp.bfloat16).at[slot_index].set(tiles, mode="drop")
    )
    arrived = lax.all_to_all(outgoing, "seq", split_axis=0, concat_axis=0, tiled=True)
    arrived_f = arrived.astype(jnp.float32)
    inverse = lax.rsqrt(jnp.mean(arrived_f * arrived_f, axis=-1, keepdims=True) + epsilon)
    normed = (arrived_f * inverse * gain_enc).astype(jnp.bfloat16)

    def add_rows(portion):
        return jnp.dot(normed, portion, preferred_element_type=jnp.float32)

    gate_act = add_rows(lax.all_gather(w_gate, "seq", axis=0, tiled=True))
    up_act = add_rows(lax.all_gather(w_up, "seq", axis=0, tiled=True))
    hidden = (jax.nn.silu(gate_act) * up_act).astype(jnp.bfloat16)
    partial_out = jnp.dot(
        hidden,
        lax.all_gather(w_down, "seq", axis=1, tiled=True),
        preferred_element_type=jnp.float32,
    )
    share = lax.psum_scatter(partial_out, "mp", scatter_dimension=1, tiled=True)
    share_width = share.shape[1]
    own_cols = lax.dynamic_slice_in_dim(
        arrived_f, lax.axis_index("mp") * share_width, share_width, 1
    )
    embedded_cols = (own_cols + share).astype(jnp.bfloat16)
    embedded = lax.all_gather(embedded_cols, "mp", axis=1, tiled=True)
    return slide_layer(embedded, gain_slide, w_qkv, offsets)


def slide_layer(embedded, gain_slide, w_qkv, offsets):
    portion_f = embedded.astype(jnp.float32)
    accumulated = jnp.dot(
        (portion_f * gain_slide).astype(jnp.bfloat16), w_qkv, preferred_element_type=jnp.float32
    )
    accumulated, squares = (accumulated, jnp.sum(portion_f * portion_f, axis=1))
    projected = accumulated * lax.rsqrt(squares / D_ENC + epsilon)[:, None]
    qkv_act = projected.astype(jnp.bfloat16)
    local_head_output = offsets.shape[0]
    fields = qkv_act.reshape(ENCODER_SLOTS, local_head_output, 3, HEAD_WIDTH)
    query_rows = fields[:, :, 0, :]
    keys_local = fields[:, :, 1, :]
    values_local = fields[:, :, 2, :]
    scale_factor = HEAD_WIDTH ** (-0.5)
    row_selector = (jnp.arange(DILATION_STEP, dtype=jnp.int32)[None, :] == offsets[:, None]).astype(
        jnp.float32
    )
    selected_rows = ENCODER_SLOTS // DILATION_STEP

    def select_rows(slide_field):
        reshaped_rows = slide_field.astype(jnp.float32).reshape(
            selected_rows, DILATION_STEP, local_head_output, HEAD_WIDTH
        )
        return jnp.einsum("rdhe,hd->rhe", reshaped_rows, row_selector).astype(jnp.bfloat16)

    query_sel = select_rows(query_rows)
    package = jnp.concatenate([select_rows(keys_local), select_rows(values_local)], axis=2).reshape(
        selected_rows, local_head_output * 2 * HEAD_WIDTH
    )
    portion = gather_seq(package)
    parts_kv = portion.reshape(portion.shape[0], local_head_output, 2, HEAD_WIDTH)
    scores = (
        jnp.einsum(
            "qhe,khe->hqk", query_sel, parts_kv[:, :, 0, :], preferred_element_type=jnp.float32
        )
        * scale_factor
    )
    weights = jnp.exp(scores)
    numer = jnp.einsum(
        "hqk,khe->hqe",
        weights.astype(jnp.bfloat16),
        parts_kv[:, :, 1, :],
        preferred_element_type=jnp.float32,
    )
    remote_den = jnp.sum(weights, axis=-1)
    scores = (
        jnp.einsum("qhe,khe->hqk", query_rows, keys_local, preferred_element_type=jnp.float32)
        * scale_factor
    )
    weights = jnp.exp(scores)
    local_num = jnp.einsum(
        "hqk,khe->hqe",
        weights.astype(jnp.bfloat16),
        values_local,
        preferred_element_type=jnp.float32,
    )
    local_den = jnp.sum(weights, axis=-1)
    spread_num = jnp.einsum("hre,hd->hrde", numer, row_selector).reshape(
        local_head_output, ENCODER_SLOTS, HEAD_WIDTH
    )
    spread_den = jnp.einsum("hr,hd->hrd", remote_den, row_selector).reshape(
        local_head_output, ENCODER_SLOTS
    )
    result = (local_num + spread_num) / (local_den + spread_den)[..., None]
    return (
        jnp.transpose(result, (1, 0, 2))
        .reshape(ENCODER_SLOTS, local_head_output * HEAD_WIDTH)
        .astype(jnp.bfloat16)
    )


def swap(array, axis, distance):
    size = lax.axis_size(axis)
    return lax.ppermute(array, axis, [(i, i ^ distance) for i in range(size)])


def block_at(array, index, size, axis):
    return lax.dynamic_slice_in_dim(array, index * size, size, axis)


def call(body, outs, inputs, spaces=None, scratch=(), copies=0, megabytes=40):
    spaces = spaces or [pltpu.VMEM] * len(inputs)
    scratch = list(scratch)
    if copies:
        scratch.append(pltpu.SemaphoreType.DMA((copies,)))
    return pl.pallas_call(
        body,
        out_shape=[jax.ShapeDtypeStruct(shape, kind) for shape, kind in outs],
        in_specs=[pl.BlockSpec(memory_space=space) for space in spaces],
        out_specs=[pl.BlockSpec(memory_space=pltpu.VMEM)] * len(outs),
        scratch_shapes=scratch,
        compiler_params=pltpu.CompilerParams(vmem_limit_bytes=megabytes * 1024 * 1024),
    )(*inputs)


def at(index, size):
    return pl.ds(pl.multiple_of(index * size, size), size)


def place():
    return tuple(lax.axis_index(name) for name in ("seq", "mp", "groups"))


def column_block(seq, mp):
    step = jnp.where(mp == 2, seq + 1, seq + 3) & 3
    return jnp.where(mp < 2, seq ^ (2 * mp), step)


def column_user(seq, mp):
    step = jnp.where(mp == 2, seq + 3, seq + 1) & 3
    return jnp.where(mp < 2, seq ^ (2 * mp), step)


def copier(sems, group):
    copies, used = [], [0]

    def copy(source, target, other=None):
        started = pltpu.make_async_copy(source, target, sems.at[used[0]])
        if other is None:
            started.start()
        else:
            second = pltpu.make_async_copy(other, target, sems.at[used[0]])
            pl.when(group == 0)(started.start)
            pl.when(group != 0)(second.start)
        copies.append(started)
        used[0] += 1

    return copies, copy


def normalise(rows, part, gain):
    values = rows[...].astype(jnp.float32)
    squares = jnp.sum(values * values, axis=1, keepdims=True)
    inverse = lax.rsqrt(squares * (1.0 / D_ENC) + epsilon)
    return (part.astype(jnp.float32) * inverse * gain[None, :]).astype(jnp.bfloat16)


def cut_first_body(
    count, tiles, w_gate, w_up, gain, first_out, second_out, quarter, held, sems
):
    seq, mp, group = place()
    copies, copy = copier(sems, group)
    half, units = w_gate.shape[0] // 2, w_gate.shape[1] // count
    features = quarter.shape[1]
    copy(tiles, held)
    for i in range(2):
        span = pl.ds(i * half, half), at(seq ^ 2, units)
        columns = pl.ds(features + i * units, units)
        copy(w_gate.at[span], second_out.at[:, columns], w_up.at[span])
        span = pl.ds(i * half, half), at(seq ^ 1, units)
        for k, weight in enumerate((w_gate, w_up)):
            columns = pl.ds(features + (2 * i + k) * units, units)
            copy(weight.at[span], first_out.at[:, columns])
    copies.pop(0).wait()
    columns = at(mp, features)
    own_columns = normalise(held, held[:, columns], gain[columns])
    second_out[:, :features] = own_columns
    first_out[:, :features] = own_columns
    quarter[...] = own_columns
    for started in copies:
        started.wait()


def cut_second_body(
    count, tiles, w_gate, w_up, w_down, gain, third_out, kept, near, far, normed, residual, held, sems
):
    seq, mp, group = place()
    copies, copy = copier(sems, group)
    half, units = w_gate.shape[0] // 2, w_gate.shape[1] // count
    copy(tiles, held)
    part = units // 2
    for j, target in ((2, far), (0, near)):
        rows = at(column_user(seq, mp ^ j) * 2 + group, part)
        copy(w_down.at[rows, :], target.at[pl.ds(0, part), :])
        rows = at(column_user(seq, mp ^ (j + 1)), units)
        copy(w_down.at[rows, :], target.at[pl.ds(part, units), :])
    for i in range(2):
        span = pl.ds(i * half, half), at(seq ^ 3, units)
        copy(w_gate.at[span], third_out.at[:, pl.ds(i * units, units)], w_up.at[span])
    for i, weight in enumerate((w_gate, w_up)):
        copy(weight.at[:, at(seq, units)], kept.at[:, pl.ds(i * units, units)])
    copies.pop(0).wait()
    normed[...] = normalise(held, held[...], gain[...])
    residual[...] = held[:, at(column_block(seq, mp), residual.shape[1])]
    for started in copies:
        started.wait()


def restack_body(second, third, first, stacked, columns):
    features = stacked.shape[2]
    stacked[0] = first[:, :features]
    stacked[1] = second[:, :features]
    stacked[2] = third[...]
    columns[...] = second[:, features:]


def pair_body(near, far, even, odd):
    for i, rows in enumerate((near, far)):
        even[i] = rows[: even.shape[1], :]
        odd[i] = rows[even.shape[1] :, :]


def routes_body(count, counts, offsets, dest, dest_row, routes):
    seq, _, _ = place()
    rows = dest_row.shape[1]
    capacity = ENCODER_SLOTS // count
    later = lax.broadcasted_iota(jnp.int32, (rows, rows), 1)
    earlier = lax.broadcasted_iota(jnp.int32, (rows, rows), 0)
    same = (dest[...] == dest_row[...]) & (earlier < later)
    rank = jnp.sum(jnp.where(same, 1, 0), axis=0, keepdims=True)
    live = lax.broadcasted_iota(jnp.int32, (1, rows), 1) < counts[0]
    codes = jnp.where(live, dest_row[...] * capacity + rank, -1)

    def chosen(wanted):
        return jnp.where(codes == wanted, 1.0, 0.0).astype(jnp.bfloat16)

    slot = lax.broadcasted_iota(jnp.int32, (capacity, rows), 0)
    for d in range(count):
        routes[pl.ds(d * capacity, capacity), :] = chosen((seq ^ d) * capacity + slot)
    per_block = capacity // DILATION_STEP
    spread = count * per_block
    index = lax.broadcasted_iota(jnp.int32, (spread, rows), 0)
    wanted = (index // per_block) * capacity + (index % per_block) * DILATION_STEP
    for h in range(offsets.shape[0]):
        routes[pl.ds(count * capacity + h * spread, spread), :] = chosen(wanted + offsets[h])


def hidden_body(count, normed, own, far, near, near_far, kept, next_in, *refs):
    (second, second_other, third, third_other), (out, weights) = refs[:4], refs[4:]
    seq, mp, group = place()
    depth, units = weights.shape[2:]
    half = depth // 2
    rows = normed.shape[0]
    for k in range(2):
        weights[k, seq] = kept[:, k * units : (k + 1) * units]
        for i in range(2):
            start = own.shape[2] + (2 * i + k) * units
            span = pl.ds(i * half, half)
            weights[k, seq ^ 1, span, :] = next_in[:, start : start + units]
    for d, mine, other in ((2, second, second_other), (3, third, third_other)):
        for i in range(2):
            span, columns = pl.ds(i * half, half), slice(i * units, (i + 1) * units)
            weights[group, seq ^ d, span, :] = mine[:, columns]
            weights[1 - group, seq ^ d, span, :] = other[:, columns]
    for d in range(count):
        if d == 0:
            pieces = [(normed[:, q * depth : (q + 1) * depth], q) for q in range(count)]
        else:
            pieces = [(own[d - 1], mp), (near[d - 1], mp ^ 1)]
            pieces += [(far[d - 1], mp ^ 2), (near_far[d - 1], mp ^ 3)]
        gate_act, up_act = (
            sum(
                jnp.dot(piece, weights[k, index], preferred_element_type=jnp.float32)
                for piece, index in pieces
            )
            for k in range(2)
        )
        gated = gate_act * jax.nn.sigmoid(gate_act) * up_act
        out[pl.ds(d * rows, rows), :] = gated.astype(jnp.bfloat16)


def down_body(residual, own, far, near, near_far, even, even_other, odd, *outs):
    _, _, group = place()
    rows = outs[0].shape[0]
    weights = [None, odd[0], None, odd[1]]
    for j in range(2):
        mine, other = even[j], even_other[j]
        low, high = jnp.where(group == 0, mine, other), jnp.where(group == 0, other, mine)
        weights[2 * j] = jnp.concatenate([low, high], axis=0)
    for i, out in enumerate(outs):
        total = residual[...].astype(jnp.float32) if i == 0 else 0.0
        for j, piece in enumerate((own, near, far, near_far)):
            total += jnp.dot(
                piece[pl.ds(i * rows, rows), :], weights[j], preferred_element_type=jnp.float32
            )
        out[...] = total.astype(out.dtype)


def sum_body(own, *refs):
    parts, out = refs[:-1], refs[-1]
    total = own[...] + sum(part[...].astype(jnp.float32) for part in parts)
    out[...] = total.astype(out.dtype)


def project_body(count, gain, routes, w_qkv_t, own, far, near, near_far, *outs):
    seq, mp, _ = place()
    features = own.shape[1]
    capacity = outs[0].shape[0]
    heads = w_qkv_t.shape[0] // (3 * HEAD_WIDTH)
    squares, total = 0.0, 0.0
    for j, piece in enumerate((own, near, far, near_far)):
        index = column_block(seq, mp ^ j)
        v = piece[...].astype(jnp.float32)
        squares += jnp.sum(v * v, axis=1, keepdims=True)
        scaled = (v * gain[:, at(index, features)]).astype(jnp.bfloat16)
        total += lax.dot_general(
            scaled,
            w_qkv_t[:, at(index, features)],
            (((1,), (1,)), ((), ())),
            preferred_element_type=jnp.float32,
        )
    projected = (total * lax.rsqrt(squares * (1.0 / D_ENC) + epsilon)).astype(jnp.bfloat16)
    routed = jnp.dot(routes[...], projected, preferred_element_type=jnp.float32)
    routed = routed.astype(jnp.bfloat16)
    width = projected.shape[1]
    spread = capacity // 2
    for d, out in enumerate(outs):
        out[:, :width] = routed[d * capacity : (d + 1) * capacity]
    for h in range(heads):
        first = count * capacity + h * spread
        for i in range(2):
            start = (3 * h + 1 + i) * HEAD_WIDTH
            piece = routed[first : first + spread, start : start + HEAD_WIDTH]
            for out in outs:
                span = slice(width + h * HEAD_WIDTH, width + (h + 1) * HEAD_WIDTH)
                out[i * spread : (i + 1) * spread, span] = piece


def attend_body(count, offsets, *refs):
    packages, out, rows = refs[:count], refs[count], refs[count + 1]
    seq, _, _ = place()
    capacity = packages[0].shape[0]
    heads = offsets.shape[0]
    width = heads * 3 * HEAD_WIDTH
    for d, package in zip(ORDER, packages):
        rows[at(seq ^ d, capacity), :] = package[:, :width]
    far = [package[:, width:] for package in packages]
    half = capacity // 2
    far_keys = jnp.concatenate([f[:half] for f in far], axis=0)
    far_values = jnp.concatenate([f[half:] for f in far], axis=0)
    residue = lax.broadcasted_iota(jnp.int32, (1, out.shape[1]), 1) % DILATION_STEP
    scale_factor = HEAD_WIDTH ** (-0.5)

    local = out.shape[1]
    for h in range(heads):
        query, key, value = (
            rows[:, pl.ds((3 * h + i) * HEAD_WIDTH, HEAD_WIDTH)] for i in range(3)
        )
        span = slice(h * HEAD_WIDTH, (h + 1) * HEAD_WIDTH)
        keys = jnp.concatenate([key, far_keys[:, span]], axis=0)
        values = jnp.concatenate([value, far_values[:, span]], axis=0)
        scores = lax.dot_general(
            keys, query, (((1,), (1,)), ((), ())), preferred_element_type=jnp.float32
        )
        weights = jnp.exp(scores * scale_factor)
        dilated = jnp.where(residue == offsets[h], weights[local:], 0.0)
        weights = jnp.concatenate([weights[:local], dilated], axis=0)
        numer = lax.dot_general(
            values,
            weights.astype(jnp.bfloat16),
            (((0,), (0,)), ((), ())),
            preferred_element_type=jnp.float32,
        )
        denom = jnp.sum(weights, axis=0, keepdims=True)
        out[span, :] = (numer / denom).astype(jnp.bfloat16)


def spread_mp(own, beside=None):
    far = swap(own, "mp", 2)
    relayed = far if beside is None else lax.optimization_barrier((far, beside))[0]
    return far, swap(own, "mp", 1), swap(relayed, "mp", 1)


def split_hidden_plan(
    tiles, counts, dest, gain_enc, w_gate, w_up, w_down, gain_slide, w_qkv, offsets
):
    count, mp_size = lax.axis_size("seq"), lax.axis_size("mp")
    seq, mp = lax.axis_index("seq"), lax.axis_index("mp")
    capacity = ENCODER_SLOTS // count
    tile_rows = tiles.shape[0]
    features = D_ENC // mp_size
    depth = w_gate.shape[0]
    units = w_gate.shape[1] // count
    heads = offsets.shape[0]
    bf16 = jnp.bfloat16
    vmem, smem = pltpu.VMEM, pltpu.SMEM

    first_out, second_out, quarter = call(
        functools.partial(cut_first_body, count),
        [
            ((tile_rows, features + 4 * units), bf16),
            ((tile_rows, features + 2 * units), bf16),
            ((tile_rows, features), bf16),
        ],
        (tiles, w_gate, w_up, gain_enc),
        spaces=[pltpu.HBM] * 3 + [vmem],
        copies=7,
        scratch=[pltpu.VMEM((tile_rows, D_ENC), bf16)],
        megabytes=57,
    )
    third_out, kept, down_near, down_far, normed, residual = call(
        functools.partial(cut_second_body, count),
        [
            ((tile_rows, 2 * units), bf16),
            ((depth, 2 * units), bf16),
            ((3 * units // 2, features), bf16),
            ((3 * units // 2, features), bf16),
            ((tile_rows, D_ENC), bf16),
            ((tile_rows, features), bf16),
        ],
        (tiles, w_gate, w_up, w_down, gain_enc),
        spaces=[pltpu.HBM] * 4 + [vmem],
        scratch=[pltpu.VMEM((tile_rows, D_ENC), bf16)],
        copies=9,
        megabytes=57,
    )
    routes = call(
        functools.partial(routes_body, count),
        [((ENCODER_SLOTS + heads * ENCODER_SLOTS // DILATION_STEP, tile_rows), bf16)],
        (counts, offsets, dest, dest.reshape(1, tile_rows)),
        spaces=[smem, smem, vmem, vmem],
    )[0]

    second_in, third_in = swap(second_out, "seq", 2), swap(quarter, "seq", 3)
    arrived = second_in, third_in, swap(first_out, "seq", 1)
    from_far = swap(down_far, "mp", 2)
    arrived, from_far, routes = lax.optimization_barrier((arrived, from_far, routes))
    own, columns = call(
        restack_body,
        [
            ((count - 1, tile_rows, features), bf16),
            ((tile_rows, 2 * units), bf16),
        ],
        arrived,
    )
    third_out, _ = lax.optimization_barrier((third_out, arrived[0]))
    down_near, _ = lax.optimization_barrier((down_near, own))
    down_send = call(
        pair_body,
        [((2, units // 2, features), bf16), ((2, units, features), bf16)],
        (down_near, from_far),
    )
    third, others, far, near, down_send = lax.optimization_barrier(
        (
            swap(third_out, "seq", 3),
            swap(columns, "groups", 1),
            swap(own, "mp", 2),
            swap(own, "mp", 1),
            down_send,
        )
    )
    halves = columns, others, third, swap(third, "groups", 1)
    spread = far, near, swap(far, "mp", 1)
    parts = []
    for j in range(2):
        perm = []
        for s in range(count):
            for m in range(mp_size):
                k = m ^ j
                user = (s ^ 2 * k) if k < 2 else (s + 2 * k - 5) % count
                perm.append((s * mp_size + m, user * mp_size + k))
        parts.append(lax.ppermute(down_send[j], ("seq", "mp"), perm))
    hidden = call(
        functools.partial(hidden_body, count),
        [((count * tile_rows, units), bf16)],
        (normed, own, *spread, kept, arrived[2], *halves),
        scratch=[
            pltpu.VMEM((2, count, depth, units), bf16),
        ],
    )[0]
    even, odd = parts
    even_other = swap(even, "groups", 1)
    sums = call(
        down_body,
        [((tile_rows, features), kind) for kind in (jnp.float32, bf16, bf16, bf16)],
        (residual, hidden, *spread_mp(hidden, (even_other, odd)), even, even_other, odd),
    )
    holder = [0, 2, 1, 3]

    def to_owner(part, d):
        perm = []
        for s in range(count):
            for m in range(mp_size):
                owner = s ^ d
                perm.append((s * mp_size + m, owner * mp_size + holder[(s + holder[m] - owner) % count]))
        return lax.ppermute(part, ("seq", "mp"), perm)

    arrived = [to_owner(sums[d], d) for d in (1, 2, 3)]
    embedded_cols = call(
        sum_body, [((tile_rows, features), bf16)], (sums[0], *arrived)
    )[0]

    packages = call(
        functools.partial(project_body, count),
        [((capacity, 4 * heads * HEAD_WIDTH), bf16)] * count,
        (gain_slide[None, :], routes, w_qkv.T, embedded_cols, *spread_mp(embedded_cols)),
    )
    packages = [swap(packages[d], "seq", d) for d in ORDER[:-1]] + [packages[0]]
    return call(
        functools.partial(attend_body, count),
        [((heads * HEAD_WIDTH, ENCODER_SLOTS), bf16)],
        (offsets, *packages),
        spaces=[smem] + [vmem] * count,
        scratch=[pltpu.VMEM((ENCODER_SLOTS, 3 * heads * HEAD_WIDTH), bf16)],
    )[0].T


def on_device(*arrays):
    sizes = lax.axis_size("groups"), lax.axis_size("seq"), lax.axis_size("mp")
    if sizes == (2, 4, 4):
        return split_hidden_plan(*arrays)
    return gathered_plan(*arrays)


def solution(mesh):
    return jax.shard_map(
        on_device,
        mesh=mesh,
        in_specs=(
            P(("groups", "seq"), None),
            P(("groups", "seq")),
            P(("groups", "seq"), None),
            P(),
            P("seq", "mp"),
            P("seq", "mp"),
            P("mp", "seq"),
            P(),
            P(None, "mp"),
            P("mp"),
        ),
        out_specs=P(("groups", "seq"), "mp"),
        check_vma=False,
    )
```
